32 devices in a mesh: groups: 2 (over x), blk: 16 (over z, y, core).
Axes of the slice: x: 2, y: 2, z: 4, core: 2. Of those that a mesh axis runs over, the one named last changes fastest.
Arguments:
- projections: bfloat16 [2, 512, 8192], P(None, ('groups', 'blk')), parts along dimension 1, may hold values from -12 to 12
- images: bfloat16 [64, 8192], P(('groups', 'blk')), parts along dimension 0, may hold values from -16 to 16, as said below
- ctf_group: int32 [64], P(('groups', 'blk')), parts along dimension 0, may hold values from 0 to 15
- shift_offsets: int32 [64, 9, 2], P(('groups', 'blk')), parts along dimension 0, may hold values from -8 to 8
- shell_limit: int32 [64], P(('groups', 'blk')), parts along dimension 0, may hold values from 16 to 63
- ctf_table: float32 [32, 4096], P('groups'), parts along dimension 0, may hold values from -1 to 1
- noise_weight: float32 [32, 4096], P('groups'), parts along dimension 0, may hold values from 0.25 to 4
Outputs:
- slices: float32 [2, 512, 8192], P(None, ('groups', 'blk')), parts along dimension 1
- best_posterior: float32 [64], P(('groups', 'blk')), parts along dimension 0
- log_total: float32 [64], P(('groups', 'blk')), parts along dimension 0
The draws below stay inside these ranges and needn't reach their ends.
There are 2 independent parts, one for each index of `groups`. The reference program is written for one: setup_inputs(seed, part) draws one part's arguments, and reference() takes and returns one part's arrays. A program takes and returns all parts, laid end to end along the dimension named above; each array names one. Nothing has to cross between parts.
Inputs may be any that keep to these rules, and one draw needn't show every extreme that they name: `images`: image coefficients.
All inputs are finite; a program needn't handle non-finite values.
Results may differ from the reference program's by a relative error of at most 0.006.
Values may be sent and summed in bfloat16 or wider, within the bound.
A program may use at most 128 MiB of HBM per device.

```python
import math
import jax
import jax.numpy as jnp
from jax import lax

F = 4096
KY = 64
IMG = 256
S = 9
BATCHES = 2
G = 16
P_SIZE = 32
ORIENT = 256


def group_values(key):
    return jax.random.randint(jax.random.fold_in(key, 11), (P_SIZE,), 0, G, dtype=jnp.int32)


def offset_values(key):
    return jax.random.randint(jax.random.fold_in(key, 12), (P_SIZE, S, 2), -8, 9, dtype=jnp.int32)


def ctf_values(key):
    drawn = jax.random.uniform(jax.random.fold_in(key, 13), (G, F), jnp.float32, -1.0, 1.0)
    return drawn


def projection_values(key):
    row_total = BATCHES * ORIENT
    drawn = jax.random.normal(jax.random.fold_in(key, 14), (row_total, 2 * F), jnp.float32)
    return jnp.clip(drawn, -6.0, 6.0)


def draw_projections(key, part):
    values = projection_values(key)
    return values.reshape(BATCHES, ORIENT, 2 * F).astype(jnp.bfloat16)


def draw_ctf_group(key, part):
    return group_values(key)


def draw_shift_offsets(key, part):
    return offset_values(key)


def draw_ctf_table(key, part):
    values = ctf_values(key)
    return values.astype(jnp.float32)


def draw_images(key, part):
    drawn = jnp.clip(jax.random.normal(jax.random.fold_in(key, 31), (P_SIZE, 2 * F), jnp.float32), -6.0, 6.0)
    return drawn.astype(jnp.bfloat16)


def set_ends(values, stream_key, low, high):
    spot = [jax.random.randint(jax.random.fold_in(stream_key, axis), (), 0, length) for axis, length in enumerate(values.shape)]
    main_axis = values.shape.index(max(values.shape))
    next_to = spot[:main_axis] + [(spot[main_axis] + 1) % values.shape[main_axis]] + spot[main_axis + 1:]
    return values.at[tuple(spot)].set(low).at[tuple(next_to)].set(high)


def setup_inputs(seed: int = 0, part: int = 0) -> dict:
    splits = jax.random.split(jax.random.key(seed), 8)
    own_keys = jax.random.split(jax.random.fold_in(splits[7], part), 8)
    return {
        "projections": draw_projections(jax.random.fold_in(jax.random.fold_in(splits[7], part), 71), part),
        "images": draw_images(jax.random.fold_in(jax.random.fold_in(splits[7], part), 71), part),
        "ctf_group": draw_ctf_group(jax.random.fold_in(jax.random.fold_in(splits[7], part), 71), part),
        "shift_offsets": draw_shift_offsets(jax.random.fold_in(jax.random.fold_in(splits[7], part), 71), part),
        "shell_limit": set_ends(jax.random.randint(own_keys[4], (P_SIZE,), KY // 4, KY // 2 + F // KY // 2), jax.random.fold_in(own_keys[4], 1), KY // 4, (KY // 2 + F // KY // 2) - 1).astype(jnp.int32),
        "ctf_table": draw_ctf_table(jax.random.fold_in(jax.random.fold_in(splits[7], part), 71), part),
        "noise_weight": jnp.clip(jnp.exp(jax.random.uniform(own_keys[6], (G, F), jnp.float32, math.log(0.25), math.log(4.0))), 0.25, 4.0),
    }


def frequencies(half_width):
    positions = jnp.arange(half_width, dtype=jnp.int32)
    return (positions // KY, positions % KY - KY // 2)

def shift_factors(offsets, half_width):
    row_count = offsets.shape[0]
    shift_count = offsets.shape[1]
    row_freq = jnp.arange(half_width // KY, dtype=jnp.int32)
    col_freq = jnp.arange(KY, dtype=jnp.int32) - KY // 2
    turns_x = row_freq[None, None, :] * offsets[:, :, 0:1] % IMG
    turns_y = col_freq[None, None, :] * offsets[:, :, 1:2] % IMG
    angle_x = turns_x.astype(jnp.float32) * (2.0 * math.pi / IMG)
    angle_y = turns_y.astype(jnp.float32) * (2.0 * math.pi / IMG)
    cosine_x = jnp.cos(angle_x)[:, :, :, None]
    sine_x = jnp.sin(angle_x)[:, :, :, None]
    cosine_y = jnp.cos(angle_y)[:, :, None, :]
    sine_y = jnp.sin(angle_y)[:, :, None, :]
    cosine = cosine_x * cosine_y - sine_x * sine_y
    sine_part = sine_x * cosine_y + cosine_x * sine_y
    return (cosine.reshape(row_count, shift_count, half_width), sine_part.reshape(row_count, shift_count, half_width))

def particle_terms(image_rows, ctf_rows, weight_rows, offsets, limits, freq_x, freq_y):
    half_width = image_rows.shape[1] // 2
    image_real = image_rows[:, :half_width].astype(jnp.float32)
    image_imag = image_rows[:, half_width:].astype(jnp.float32)
    radius_sq = freq_x * freq_x + freq_y * freq_y
    inside = (radius_sq[None, :] < (limits * limits)[:, None]).astype(jnp.float32)
    masked_weight = inside * weight_rows
    ctf_weight = masked_weight * ctf_rows
    norm_term = lax.optimization_barrier(jnp.sum(masked_weight * (image_real * image_real + image_imag * image_imag), axis=1))
    quad_weight = ctf_weight * ctf_rows
    cosine, sine_part = shift_factors(offsets, half_width)
    shift_real = image_real[:, None, :] * cosine + image_imag[:, None, :] * sine_part
    shift_imag = image_imag[:, None, :] * cosine - image_real[:, None, :] * sine_part
    weighted = jnp.concatenate([ctf_weight[:, None, :] * shift_real, ctf_weight[:, None, :] * shift_imag], axis=2).astype(jnp.bfloat16)
    return (weighted, norm_term, quad_weight)

def reference(projections, images, ctf_group, shift_offsets, shell_limit, ctf_table, noise_weight):
    full_width = images.shape[1]
    half_width = full_width // 2
    candidates = BATCHES * ORIENT
    flat_proj = projections.reshape(candidates, full_width)
    proj_real = flat_proj[:, :half_width].astype(jnp.float32)
    proj_imag = flat_proj[:, half_width:].astype(jnp.float32)
    proj_power = proj_real * proj_real + proj_imag * proj_imag
    flat_wide = flat_proj.astype(jnp.float32)
    freq_x, freq_y = frequencies(half_width)
    score_scale = 0.5 / math.sqrt(half_width)
    block_rows = 16
    block_count = P_SIZE // block_rows

    def split_rows(source):
        return source.reshape((block_count, block_rows) + source.shape[1:])

    def block_terms(members):
        image_rows, groups, offsets, limits = members
        return particle_terms(image_rows, ctf_table[groups], noise_weight[groups], offsets, limits, freq_x, freq_y)

    def score_block(members):
        weighted, norm_term, quad_weight = block_terms(members)
        cross_term = lax.dot_general(weighted.astype(jnp.float32), flat_wide, (((2,), (1,)), ((), ())))
        quad_term = lax.dot_general(quad_weight, proj_power, (((1,), (1,)), ((), ())), precision=lax.Precision.HIGHEST)
        return -(norm_term[:, None, None] - 2.0 * cross_term + quad_term[:, None, :]) * score_scale
    members = (split_rows(images), split_rows(ctf_group), split_rows(shift_offsets), split_rows(shell_limit))
    scores = lax.map(score_block, members).reshape(P_SIZE, S, candidates)
    score_top = lax.optimization_barrier(jnp.max(scores, axis=(1, 2)))
    exp_total = lax.optimization_barrier(jnp.sum(jnp.exp(scores - score_top[:, None, None]), axis=(1, 2)))
    log_total = score_top + jnp.log(exp_total)
    best_posterior = jnp.exp(score_top - log_total)

    def add_block(carry, packed):
        member_block, score_values, log_block = packed
        weighted = block_terms(member_block)[0]
        posterior = jnp.exp(score_values - log_block[:, None, None]).astype(jnp.bfloat16)
        contrib = lax.dot_general(posterior.astype(jnp.float32), weighted.astype(jnp.float32), (((0, 1), (0, 1)), ((), ())))
        return (carry + contrib, None)
    zero_slices = jnp.zeros((candidates, full_width), jnp.float32)
    summed, unused_out = lax.scan(add_block, zero_slices, (members, split_rows(scores), split_rows(log_total)))
    slices = (summed * (BATCHES * ORIENT / P_SIZE)).reshape(BATCHES, ORIENT, full_width)
    return (slices, best_posterior, log_total)
```

```python
import functools
import math

import jax
import jax.numpy as jnp
from jax import lax
from jax.experimental import pallas as pl
from jax.experimental.pallas import tpu as pltpu
from jax.sharding import PartitionSpec as P

KY = 64
IMG = 256


def combined_all(value, axis, join):
    pieces = jax.tree.map(lambda part: lax.all_gather(part, axis), value)
    head = jax.tree.map(lambda part: part[0], pieces)
    tail = jax.tree.map(lambda part: part[1:], pieces)
    so_far, _ = lax.scan(lambda so_far, section: (join(so_far, section), None), head, tail)
    return so_far


def frequencies(half_width):
    positions = jnp.arange(half_width, dtype=jnp.int32)
    return (positions // KY, positions % KY - KY // 2)


def shift_factors(offsets, half_width):
    row_count = offsets.shape[0]
    shift_count = offsets.shape[1]
    row_freq = jnp.arange(half_width // KY, dtype=jnp.int32)
    col_freq = jnp.arange(KY, dtype=jnp.int32) - KY // 2
    turns_x = row_freq[None, None, :] * offsets[:, :, 0:1] % IMG
    turns_y = col_freq[None, None, :] * offsets[:, :, 1:2] % IMG
    angle_x = turns_x.astype(jnp.float32) * (2.0 * math.pi / IMG)
    angle_y = turns_y.astype(jnp.float32) * (2.0 * math.pi / IMG)
    cosine_x = jnp.cos(angle_x)[:, :, :, None]
    sine_x = jnp.sin(angle_x)[:, :, :, None]
    cosine_y = jnp.cos(angle_y)[:, :, None, :]
    sine_y = jnp.sin(angle_y)[:, :, None, :]
    cosine = cosine_x * cosine_y - sine_x * sine_y
    sine_part = sine_x * cosine_y + cosine_x * sine_y
    return (
        cosine.reshape(row_count, shift_count, half_width),
        sine_part.reshape(row_count, shift_count, half_width),
    )


def particle_terms(image_rows, ctf_rows, weight_rows, offsets, limits, freq_x, freq_y):
    half_width = image_rows.shape[1] // 2
    image_real = image_rows[:, :half_width].astype(jnp.float32)
    image_imag = image_rows[:, half_width:].astype(jnp.float32)
    radius_sq = freq_x * freq_x + freq_y * freq_y
    inside = (radius_sq[None, :] < (limits * limits)[:, None]).astype(jnp.float32)
    masked_weight = inside * weight_rows
    ctf_weight = masked_weight * ctf_rows
    norm_term = jnp.sum(masked_weight * (image_real * image_real + image_imag * image_imag), axis=1)
    quad_weight = ctf_weight * ctf_rows
    cosine, sine_part = shift_factors(offsets, half_width)
    shift_real = image_real[:, None, :] * cosine + image_imag[:, None, :] * sine_part
    shift_imag = image_imag[:, None, :] * cosine - image_real[:, None, :] * sine_part
    weighted = jnp.concatenate(
        [ctf_weight[:, None, :] * shift_real, ctf_weight[:, None, :] * shift_imag], axis=2
    ).astype(jnp.bfloat16)
    return (weighted, norm_term, quad_weight)


def combine_lse(first, second):
    score_top = jnp.maximum(first[0], second[0])
    exp_total = first[1] * jnp.exp(first[0] - score_top) + second[1] * jnp.exp(
        second[0] - score_top
    )
    return (score_top, exp_total)


def block_shape(row_count):
    return 64 if row_count % 64 == 0 else row_count


def split_rows(members, block_rows):
    return tuple(
        (
            member.reshape((member.shape[0] // block_rows, block_rows) + member.shape[1:])
            for member in members
        )
    )


def local(projections, images, ctf_group, shift_offsets, shell_limit, ctf_table, noise_weight):
    batch_count, orient_dev, full_width = projections.shape
    half_width = full_width // 2
    candidates = batch_count * orient_dev
    flat_proj = projections.reshape(candidates, full_width)
    proj_real = flat_proj[:, :half_width].astype(jnp.float32)
    proj_imag = flat_proj[:, half_width:].astype(jnp.float32)
    proj_power = proj_real * proj_real + proj_imag * proj_imag
    freq_x, freq_y = frequencies(half_width)
    score_scale = 0.5 / math.sqrt(half_width)
    group_count = ctf_table.shape[0]
    particles_dev = images.shape[0]

    def block_terms(members):
        image_rows, groups, offsets, limits = members
        one_hot = (groups[:, None] == jnp.arange(group_count, dtype=jnp.int32)[None, :]).astype(
            jnp.float32
        )
        ctf_rows = jnp.dot(
            one_hot, ctf_table, precision=lax.Precision.HIGHEST, preferred_element_type=jnp.float32
        )
        weight_rows = jnp.dot(
            one_hot,
            noise_weight,
            precision=lax.Precision.HIGHEST,
            preferred_element_type=jnp.float32,
        )
        return particle_terms(image_rows, ctf_rows, weight_rows, offsets, limits, freq_x, freq_y)

    def score_block(members):
        weighted, norm_term, quad_weight = block_terms(members)
        cross_term = lax.dot_general(
            weighted, flat_proj, (((2,), (1,)), ((), ())), preferred_element_type=jnp.float32
        )
        quad_term = lax.dot_general(
            quad_weight,
            proj_power,
            (((1,), (1,)), ((), ())),
            precision=lax.Precision.HIGHEST,
            preferred_element_type=jnp.float32,
        )
        return -(norm_term[:, None, None] - 2.0 * cross_term + quad_term[:, None, :]) * score_scale

    members = (
        lax.all_gather(images, "blk", axis=0, tiled=True),
        lax.all_gather(ctf_group, "blk", axis=0, tiled=True),
        lax.all_gather(shift_offsets, "blk", axis=0, tiled=True),
        lax.all_gather(shell_limit, "blk", axis=0, tiled=True),
    )
    row_count = members[0].shape[0]
    block_rows = block_shape(row_count)
    blocks = lax.map(score_block, split_rows(members, block_rows))
    scores = blocks.reshape((row_count,) + blocks.shape[2:])
    local_top = jnp.max(scores, axis=(1, 2))
    local_total = jnp.sum(jnp.exp(scores - local_top[:, None, None]), axis=(1, 2))
    score_top, exp_total = combined_all((local_top, local_total), "blk", combine_lse)
    log_total = score_top + jnp.log(exp_total)
    pieces = (
        lax.all_gather(images, "blk", axis=0, tiled=True),
        lax.all_gather(ctf_group, "blk", axis=0, tiled=True),
        lax.all_gather(shift_offsets, "blk", axis=0, tiled=True),
        lax.all_gather(shell_limit, "blk", axis=0, tiled=True),
    )
    row_count = pieces[0].shape[0]
    block_rows = block_shape(row_count)

    def add_block(carry, packed):
        member_block, score_block_values, log_block = packed
        weighted = block_terms(member_block)[0]
        posterior = jnp.exp(score_block_values - log_block[:, None, None]).astype(jnp.bfloat16)
        contrib = lax.dot_general(
            posterior, weighted, (((0, 1), (0, 1)), ((), ())), preferred_element_type=jnp.float32
        )
        return (carry + contrib, None)

    zero_slices = jnp.zeros((candidates, full_width), jnp.float32)
    packed_scores = split_rows((scores, log_total), block_rows)
    summed, unused_out = lax.scan(
        add_block, zero_slices, (split_rows(pieces, block_rows), packed_scores[0], packed_scores[1])
    )
    slices = (summed * (candidates / particles_dev)).reshape(batch_count, orient_dev, full_width)
    own_start = lax.axis_index("blk") * particles_dev
    own_top = lax.dynamic_slice_in_dim(score_top, own_start, particles_dev, 0)
    own_log = lax.dynamic_slice_in_dim(log_total, own_start, particles_dev, 0)
    best_posterior = jnp.exp(own_top - own_log)
    return (slices, best_posterior, own_log)


LANES = 128
TILE_KX = LANES // KY
VMEM_LIMIT = 48 * 1024 * 1024


def turn_cos_sin(turns):
    turns = turns - IMG * jnp.floor(turns * (1.0 / IMG) + 0.5)
    half = turns * (math.pi / IMG)
    sq = half * half
    sin_poly = 1.0 / math.factorial(13)
    for power in (11, 9, 7, 5, 3, 1):
        sin_poly = sin_poly * sq + (-1.0) ** (power // 2) / math.factorial(power)
    cos_poly = 1.0 / math.factorial(14) * -1.0
    for power in (12, 10, 8, 6, 4, 2, 0):
        cos_poly = cos_poly * sq + (-1.0) ** (power // 2) / math.factorial(power)
    sin_half = sin_poly * half
    return 1.0 - 2.0 * sin_half * sin_half, 2.0 * sin_half * cos_poly


def three_parts(values):
    first = values.astype(jnp.bfloat16)
    rest = values - first.astype(jnp.float32)
    second = rest.astype(jnp.bfloat16)
    third = (rest - second.astype(jnp.float32)).astype(jnp.bfloat16)
    return first, second, third


def grid_sides(device_count):
    chips = device_count // 2
    outer = 2 ** ((chips.bit_length()) // 2)
    return outer, chips // outer


def kernel(
    sizes,
    proj_ref, img_ref, grp_ref, off_ref, lim_ref, ctf_ref, noise_ref,
    out_ref, best_ref, log_ref,
    pkt, image, power, quad_w, tabs, ec_p, es_p, ec_m, es_m, dc, ds, wbuf, cross, norm, stats,
    send_sem, recv_sem, stat_send, stat_recv,
):
    n, na, nb, rows, shifts, half_width = sizes
    own_rows = rows // n
    full = 2 * half_width
    tiles = half_width // LANES
    groups = ctf_ref.shape[0]
    me = lax.axis_index("blk")
    core = me % 2
    chip = me // 2
    a, b = chip // nb, chip % nb

    def at(pa, pb, pc):
        return (pa * nb + pb) * 2 + pc

    barrier = pltpu.get_barrier_semaphore()
    for step in range(1, n):
        pl.semaphore_signal(barrier, inc=1, device_id={"blk": (me + step) % n})

    sub = lax.broadcasted_iota(jnp.int32, (own_rows, LANES), 0)
    lane = lax.broadcasted_iota(jnp.int32, (own_rows, LANES), 1)
    meta = jnp.zeros((own_rows, LANES), jnp.float32)
    for p in range(own_rows):
        entries = [off_ref[p, s, j] for s in range(shifts) for j in range(2)]
        entries += [grp_ref[p], lim_ref[p]]
        for column, entry in enumerate(entries):
            meta = jnp.where((sub == p) & (lane == column), entry.astype(jnp.float32), meta)
    pkt[me, :, :full] = img_ref[...]
    pkt[me, :, full:] = meta.astype(jnp.bfloat16)

    pl.semaphore_wait(barrier, n - 1)

    sends = []

    def send(slot, target):
        copy = pltpu.make_async_remote_copy(
            src_ref=pkt.at[slot], dst_ref=pkt.at[slot],
            send_sem=send_sem.at[len(sends)], recv_sem=recv_sem.at[slot],
            device_id={"blk": target},
        )
        copy.start()
        sends.append(copy)

    def arrived(slot):
        pltpu.make_async_remote_copy(
            src_ref=pkt.at[slot], dst_ref=pkt.at[slot],
            send_sem=send_sem.at[0], recv_sem=recv_sem.at[slot],
            device_id={"blk": (me + 1) % n},
        ).wait_recv()

    other = me + 1 - 2 * core
    for j in range(1, na):
        send(me, at((a + j) % na, b, core))
    for k in range(1, nb):
        send(me, at(a, (b + k) % nb, core))
    send(me, other)

    for which, ref in enumerate((ctf_ref, noise_ref)):
        for part, value in enumerate(three_parts(ref[...])):
            tabs[part * groups:(part + 1) * groups, which * half_width:(which + 1) * half_width] = value
    proj_rows = proj_ref.shape[1]
    for batch in range(proj_ref.shape[0]):
        real = proj_ref[batch, :, :half_width].astype(jnp.float32)
        imag = proj_ref[batch, :, half_width:].astype(jnp.float32)
        power[batch * proj_rows:(batch + 1) * proj_rows, :] = real * real + imag * imag

    for j in range(1, na):
        slot = at((a + na - j) % na, b, core)
        arrived(slot)
        for k in range(1, nb):
            send(slot, at(a, (b + k) % nb, core))
        send(slot, other)
    for k in range(1, nb):
        for j in range(na):
            slot = at((a + na - j) % na, (b + nb - k) % nb, core)
            arrived(slot)
            send(slot, other)
    for k in range(nb):
        for j in range(na):
            arrived(at((a + na - j) % na, (b + nb - k) % nb, 1 - core))

    for d in range(n):
        image[d * own_rows:(d + 1) * own_rows, :] = pkt[d].astype(jnp.float32)

    lane = lax.broadcasted_iota(jnp.int32, (rows, LANES), 1)
    sub = lax.broadcasted_iota(jnp.int32, (rows, LANES), 0)
    side = lane // KY
    freq_y = lane % KY - KY // 2
    side_f, freq_yf = side.astype(jnp.float32), freq_y.astype(jnp.float32)
    meta = image[:, full:]

    def column(j):
        return jnp.broadcast_to(meta[:, j:j + 1], (rows, LANES))

    middle = TILE_KX * (tiles // 2)
    for s in range(shifts):
        at_rows = slice(s * rows, (s + 1) * rows)
        off_x, off_y = column(2 * s), column(2 * s + 1)
        c0, s0 = turn_cos_sin((middle + side_f) * off_x + freq_yf * off_y)
        cd, sd = turn_cos_sin(TILE_KX * off_x)
        ec_p[at_rows, :], es_p[at_rows, :] = c0, s0
        ec_m[at_rows, :], es_m[at_rows, :] = c0 * cd + s0 * sd, s0 * cd - c0 * sd
        dc[at_rows, :], ds[at_rows, :] = cd, sd
    group_of = column(2 * shifts)[:, :3 * groups].astype(jnp.int32)
    lane_group = lax.broadcasted_iota(jnp.int32, (rows, 3 * groups), 1) % groups
    one_hot = (group_of == lane_group).astype(jnp.float32).astype(jnp.bfloat16)
    limit = column(2 * shifts + 1)
    limit_sq = limit * limit

    cross[...] = jnp.zeros_like(cross)
    norm[...] = jnp.zeros_like(norm)

    def tile_step(tile, ec, es, sign):
        re_cols = pl.ds(pl.multiple_of(tile * LANES, LANES), LANES)
        im_cols = pl.ds(pl.multiple_of(half_width + tile * LANES, LANES), LANES)
        two = pl.ds(pl.multiple_of(tile * 2 * LANES, 2 * LANES), 2 * LANES)
        x_re, x_im = image[:, re_cols], image[:, im_cols]
        c = jnp.dot(one_hot, tabs[:, re_cols], preferred_element_type=jnp.float32)
        w = jnp.dot(one_hot, tabs[:, im_cols], preferred_element_type=jnp.float32)
        freq_x = (TILE_KX * tile + side).astype(jnp.float32)
        w = jnp.where(freq_x * freq_x + freq_yf * freq_yf < limit_sq, w, 0.0)
        wc = w * c
        norm[...] += w * (x_re * x_re + x_im * x_im)
        quad_w[:, re_cols] = wc * c
        u_re, u_im = wc * x_re, wc * x_im
        for s in range(shifts):
            at_rows = slice(s * rows, (s + 1) * rows)
            ck, sk = ec[at_rows, :], es[at_rows, :]
            wbuf[at_rows, pl.ds(pl.multiple_of(tile * 2 * LANES, LANES), LANES)] = (
                u_re * ck + u_im * sk).astype(jnp.bfloat16)
            wbuf[at_rows, pl.ds(pl.multiple_of(tile * 2 * LANES + LANES, LANES), LANES)] = (
                u_im * ck - u_re * sk).astype(jnp.bfloat16)
            cd, sd = dc[at_rows, :], ds[at_rows, :] * sign
            ec[at_rows, :] = ck * cd - sk * sd
            es[at_rows, :] = sk * cd + ck * sd
        p_tile = jnp.concatenate(
            [jnp.concatenate([proj_ref[k, :, re_cols], proj_ref[k, :, im_cols]], axis=1)
             for k in range(proj_ref.shape[0])], axis=0)
        cross[...] += lax.dot_general(
            wbuf[:, two], p_tile, (((1,), (1,)), ((), ())), preferred_element_type=jnp.float32)

    @pl.loop(0, tiles // 2)
    def _(m):
        tile_step(tiles // 2 + m, ec_p, es_p, 1.0)
        tile_step(tiles // 2 - 1 - m, ec_m, es_m, -1.0)

    quad = lax.dot_general(
        quad_w[...], power[...], (((1,), (1,)), ((), ())),
        precision=lax.Precision.HIGHEST, preferred_element_type=jnp.float32)
    base = jnp.sum(norm[...], axis=1, keepdims=True) + quad
    scale = 0.5 / math.sqrt(half_width)
    scores = [-(base - 2.0 * cross[s * rows:(s + 1) * rows, :]) * scale for s in range(shifts)]
    top = functools.reduce(jnp.maximum, scores)
    top = jnp.max(top, axis=1, keepdims=True)
    total = sum(jnp.exp(score - top) for score in scores)
    total = jnp.sum(total, axis=1, keepdims=True)

    mid = LANES // 2
    row = jnp.where(lane == sub, top, 0.0) + jnp.where(lane == sub + mid, total, 0.0)
    stats[me] = jnp.sum(row, axis=0, keepdims=True)
    stat_copies = []
    for step in range(1, n):
        copy = pltpu.make_async_remote_copy(
            src_ref=stats.at[me], dst_ref=stats.at[me],
            send_sem=stat_send.at[step], recv_sem=stat_recv.at[me],
            device_id={"blk": (me + step) % n},
        )
        copy.start()
        stat_copies.append(copy)
    for step in range(1, n):
        slot = (me + n - step) % n
        pltpu.make_async_remote_copy(
            src_ref=stats.at[slot], dst_ref=stats.at[slot],
            send_sem=stat_send.at[step], recv_sem=stat_recv.at[slot],
            device_id={"blk": (me + step) % n},
        ).wait_recv()
    tops = jnp.concatenate([stats[d] for d in range(n)], axis=0)
    totals = pltpu.roll(tops, mid, 1)
    best = jnp.max(tops, axis=0, keepdims=True)
    all_total = jnp.sum(totals * jnp.exp(tops - best), axis=0, keepdims=True)
    log_row = best + jnp.log(all_total)
    log_total = jnp.sum(jnp.where(lane == sub, log_row, 0.0), axis=1, keepdims=True)
    best_row = jnp.exp(best - log_row)
    lane_one = lax.broadcasted_iota(jnp.int32, (1, LANES), 1)
    for p in range(own_rows):
        mine = lane_one == me * own_rows + p
        best_ref[p] = jnp.sum(jnp.where(mine, best_row, 0.0))
        log_ref[p] = jnp.sum(jnp.where(mine, log_row, 0.0))

    posterior = jnp.concatenate([jnp.exp(score - log_total) for score in scores], axis=0)
    posterior = posterior.T.astype(jnp.bfloat16)
    gain = proj_ref.shape[0] * proj_rows / own_rows

    @pl.loop(0, tiles)
    def _(tile):
        two = pl.ds(pl.multiple_of(tile * 2 * LANES, 2 * LANES), 2 * LANES)
        part = jnp.dot(posterior, wbuf[:, two], preferred_element_type=jnp.float32) * gain
        for k in range(proj_ref.shape[0]):
            block = part[k * proj_rows:(k + 1) * proj_rows]
            out_ref[k, :, pl.ds(pl.multiple_of(tile * LANES, LANES), LANES)] = block[:, :LANES]
            out_ref[k, :, pl.ds(pl.multiple_of(half_width + tile * LANES, LANES), LANES)] = block[:, LANES:]

    for copy in sends + stat_copies:
        copy.wait_send()


def fused(n, projections, images, ctf_group, shift_offsets, shell_limit, ctf_table, noise_weight):
    batches, orient, full = projections.shape
    half_width = full // 2
    own_rows, shifts = shift_offsets.shape[:2]
    rows, cand = n * own_rows, batches * orient
    na, nb = grid_sides(n)
    groups = ctf_table.shape[0]
    vmem, smem = pl.BlockSpec(memory_space=pltpu.VMEM), pl.BlockSpec(memory_space=pltpu.SMEM)
    f32, bf16 = jnp.float32, jnp.bfloat16
    table = pltpu.VMEM((shifts * rows, LANES), f32)
    return pl.pallas_call(
        functools.partial(kernel, (n, na, nb, rows, shifts, half_width)),
        out_shape=(
            jax.ShapeDtypeStruct(projections.shape, f32),
            jax.ShapeDtypeStruct((own_rows,), f32),
            jax.ShapeDtypeStruct((own_rows,), f32),
        ),
        in_specs=[vmem, vmem, smem, smem, smem, vmem, vmem],
        out_specs=(vmem, smem, smem),
        scratch_shapes=[
            pltpu.VMEM((n, own_rows, full + LANES), bf16),
            pltpu.VMEM((rows, full + LANES), f32),
            pltpu.VMEM((cand, half_width), f32),
            pltpu.VMEM((rows, half_width), f32),
            pltpu.VMEM((3 * groups, full), bf16),
            table, table, table, table, table, table,
            pltpu.VMEM((shifts * rows, full), bf16),
            pltpu.VMEM((shifts * rows, cand), f32),
            pltpu.VMEM((rows, LANES), f32),
            pltpu.VMEM((n, 1, LANES), f32),
            pltpu.SemaphoreType.DMA((n,)),
            pltpu.SemaphoreType.DMA((n,)),
            pltpu.SemaphoreType.DMA((n,)),
            pltpu.SemaphoreType.DMA((n,)),
        ],
        compiler_params=pltpu.CompilerParams(
            collective_id=0, has_side_effects=True, vmem_limit_bytes=VMEM_LIMIT),
    )(projections, images, ctf_group, shift_offsets, shell_limit, ctf_table, noise_weight)


def per_device(n, *args):
    particles = n * args[1].shape[0]
    if particles > LANES // 2:
        return local(*args)
    return fused(n, *args)


def solution(mesh):
    in_specs = (
        P(None, ("groups", "blk"), None),
        P(("groups", "blk"), None),
        P(("groups", "blk")),
        P(("groups", "blk"), None, None),
        P(("groups", "blk")),
        P("groups", None),
        P("groups", None),
    )
    out_specs = (P(None, ("groups", "blk"), None), P(("groups", "blk")), P(("groups", "blk")))
    return jax.shard_map(
        functools.partial(per_device, mesh.shape["blk"]),
        mesh=mesh, in_specs=in_specs, out_specs=out_specs, check_vma=False,
    )
```

```python
import functools
import math

import jax
import jax.numpy as jnp
from jax import lax
from jax.experimental import pallas as pl
from jax.experimental.pallas import tpu as pltpu
from jax.sharding import PartitionSpec as P

KY = 64
IMG = 256


def combined_all(value, axis, join):
    pieces = jax.tree.map(lambda part: lax.all_gather(part, axis), value)
    head = jax.tree.map(lambda part: part[0], pieces)
    tail = jax.tree.map(lambda part: part[1:], pieces)
    so_far, _ = lax.scan(lambda so_far, section: (join(so_far, section), None), head, tail)
    return so_far


def frequencies(half_width):
    positions = jnp.arange(half_width, dtype=jnp.int32)
    return (positions // KY, positions % KY - KY // 2)


def shift_factors(offsets, half_width):
    row_count = offsets.shape[0]
    shift_count = offsets.shape[1]
    row_freq = jnp.arange(half_width // KY, dtype=jnp.int32)
    col_freq = jnp.arange(KY, dtype=jnp.int32) - KY // 2
    turns_x = row_freq[None, None, :] * offsets[:, :, 0:1] % IMG
    turns_y = col_freq[None, None, :] * offsets[:, :, 1:2] % IMG
    angle_x = turns_x.astype(jnp.float32) * (2.0 * math.pi / IMG)
    angle_y = turns_y.astype(jnp.float32) * (2.0 * math.pi / IMG)
    cosine_x = jnp.cos(angle_x)[:, :, :, None]
    sine_x = jnp.sin(angle_x)[:, :, :, None]
    cosine_y = jnp.cos(angle_y)[:, :, None, :]
    sine_y = jnp.sin(angle_y)[:, :, None, :]
    cosine = cosine_x * cosine_y - sine_x * sine_y
    sine_part = sine_x * cosine_y + cosine_x * sine_y
    return (
        cosine.reshape(row_count, shift_count, half_width),
        sine_part.reshape(row_count, shift_count, half_width),
    )


def particle_terms(image_rows, ctf_rows, weight_rows, offsets, limits, freq_x, freq_y):
    half_width = image_rows.shape[1] // 2
    image_real = image_rows[:, :half_width].astype(jnp.float32)
    image_imag = image_rows[:, half_width:].astype(jnp.float32)
    radius_sq = freq_x * freq_x + freq_y * freq_y
    inside = (radius_sq[None, :] < (limits * limits)[:, None]).astype(jnp.float32)
    masked_weight = inside * weight_rows
    ctf_weight = masked_weight * ctf_rows
    norm_term = jnp.sum(masked_weight * (image_real * image_real + image_imag * image_imag), axis=1)
    quad_weight = ctf_weight * ctf_rows
    cosine, sine_part = shift_factors(offsets, half_width)
    shift_real = image_real[:, None, :] * cosine + image_imag[:, None, :] * sine_part
    shift_imag = image_imag[:, None, :] * cosine - image_real[:, None, :] * sine_part
    weighted = jnp.concatenate(
        [ctf_weight[:, None, :] * shift_real, ctf_weight[:, None, :] * shift_imag], axis=2
    ).astype(jnp.bfloat16)
    return (weighted, norm_term, quad_weight)


def combine_lse(first, second):
    score_top = jnp.maximum(first[0], second[0])
    exp_total = first[1] * jnp.exp(first[0] - score_top) + second[1] * jnp.exp(
        second[0] - score_top
    )
    return (score_top, exp_total)


def block_shape(row_count):
    return 64 if row_count % 64 == 0 else row_count


def split_rows(members, block_rows):
    return tuple(
        (
            member.reshape((member.shape[0] // block_rows, block_rows) + member.shape[1:])
            for member in members
        )
    )


def local(projections, images, ctf_group, shift_offsets, shell_limit, ctf_table, noise_weight):
    batch_count, orient_dev, full_width = projections.shape
    half_width = full_width // 2
    candidates = batch_count * orient_dev
    flat_proj = projections.reshape(candidates, full_width)
    proj_real = flat_proj[:, :half_width].astype(jnp.float32)
    proj_imag = flat_proj[:, half_width:].astype(jnp.float32)
    proj_power = proj_real * proj_real + proj_imag * proj_imag
    freq_x, freq_y = frequencies(half_width)
    score_scale = 0.5 / math.sqrt(half_width)
    group_count = ctf_table.shape[0]
    particles_dev = images.shape[0]

    def block_terms(members):
        image_rows, groups, offsets, limits = members
        one_hot = (groups[:, None] == jnp.arange(group_count, dtype=jnp.int32)[None, :]).astype(
            jnp.float32
        )
        ctf_rows = jnp.dot(
            one_hot, ctf_table, precision=lax.Precision.HIGHEST, preferred_element_type=jnp.float32
        )
        weight_rows = jnp.dot(
            one_hot,
            noise_weight,
            precision=lax.Precision.HIGHEST,
            preferred_element_type=jnp.float32,
        )
        return particle_terms(image_rows, ctf_rows, weight_rows, offsets, limits, freq_x, freq_y)

    def score_block(members):
        weighted, norm_term, quad_weight = block_terms(members)
        cross_term = lax.dot_general(
            weighted, flat_proj, (((2,), (1,)), ((), ())), preferred_element_type=jnp.float32
        )
        quad_term = lax.dot_general(
            quad_weight,
            proj_power,
            (((1,), (1,)), ((), ())),
            precision=lax.Precision.HIGHEST,
            preferred_element_type=jnp.float32,
        )
        return -(norm_term[:, None, None] - 2.0 * cross_term + quad_term[:, None, :]) * score_scale

    members = (
        lax.all_gather(images, "blk", axis=0, tiled=True),
        lax.all_gather(ctf_group, "blk", axis=0, tiled=True),
        lax.all_gather(shift_offsets, "blk", axis=0, tiled=True),
        lax.all_gather(shell_limit, "blk", axis=0, tiled=True),
    )
    row_count = members[0].shape[0]
    block_rows = block_shape(row_count)
    blocks = lax.map(score_block, split_rows(members, block_rows))
    scores = blocks.reshape((row_count,) + blocks.shape[2:])
    local_top = jnp.max(scores, axis=(1, 2))
    local_total = jnp.sum(jnp.exp(scores - local_top[:, None, None]), axis=(1, 2))
    score_top, exp_total = combined_all((local_top, local_total), "blk", combine_lse)
    log_total = score_top + jnp.log(exp_total)
    pieces = (
        lax.all_gather(images, "blk", axis=0, tiled=True),
        lax.all_gather(ctf_group, "blk", axis=0, tiled=True),
        lax.all_gather(shift_offsets, "blk", axis=0, tiled=True),
        lax.all_gather(shell_limit, "blk", axis=0, tiled=True),
    )
    row_count = pieces[0].shape[0]
    block_rows = block_shape(row_count)

    def add_block(carry, packed):
        member_block, score_block_values, log_block = packed
        weighted = block_terms(member_block)[0]
        posterior = jnp.exp(score_block_values - log_block[:, None, None]).astype(jnp.bfloat16)
        contrib = lax.dot_general(
            posterior, weighted, (((0, 1), (0, 1)), ((), ())), preferred_element_type=jnp.float32
        )
        return (carry + contrib, None)

    zero_slices = jnp.zeros((candidates, full_width), jnp.float32)
    packed_scores = split_rows((scores, log_total), block_rows)
    summed, unused_out = lax.scan(
        add_block, zero_slices, (split_rows(pieces, block_rows), packed_scores[0], packed_scores[1])
    )
    slices = (summed * (candidates / particles_dev)).reshape(batch_count, orient_dev, full_width)
    own_start = lax.axis_index("blk") * particles_dev
    own_top = lax.dynamic_slice_in_dim(score_top, own_start, particles_dev, 0)
    own_log = lax.dynamic_slice_in_dim(log_total, own_start, particles_dev, 0)
    best_posterior = jnp.exp(own_top - own_log)
    return (slices, best_posterior, own_log)


LANES = 128
TILE_KX = LANES // KY
VMEM_LIMIT = 60 * 1024 * 1024


def turn_cos_sin(turns):
    turns = turns - IMG * jnp.floor(turns * (1.0 / IMG) + 0.5)
    half = turns * (math.pi / IMG)
    sq = half * half
    sin_poly = 1.0 / math.factorial(13)
    for power in (11, 9, 7, 5, 3, 1):
        sin_poly = sin_poly * sq + (-1.0) ** (power // 2) / math.factorial(power)
    cos_poly = 1.0 / math.factorial(14) * -1.0
    for power in (12, 10, 8, 6, 4, 2, 0):
        cos_poly = cos_poly * sq + (-1.0) ** (power // 2) / math.factorial(power)
    sin_half = sin_poly * half
    return 1.0 - 2.0 * sin_half * sin_half, 2.0 * sin_half * cos_poly


def three_parts(values):
    first = values.astype(jnp.bfloat16)
    rest = values - first.astype(jnp.float32)
    second = rest.astype(jnp.bfloat16)
    third = (rest - second.astype(jnp.float32)).astype(jnp.bfloat16)
    return first, second, third


def grid_sides(device_count):
    chips = device_count // 2
    outer = 2 ** ((chips.bit_length()) // 2)
    return outer, chips // outer


def kernel(
    sizes,
    proj_hbm, img_hbm, grp_hbm, off_hbm, lim_hbm, ctf_hbm, noise_hbm,
    out_hbm, best_ref, log_ref,
    out_ref, proj_ref, grp_ref, off_ref, lim_ref, ctf_ref, noise_ref,
    pkt, image, power, quad_w, tabs, ctf_rows, ec_p, es_p, ec_m, es_m, dc, ds, wbuf, stats,
    load_sem, store_sem, send_sem, recv_sem, stat_send, stat_recv,
):
    n, na, nb, rows, shifts, half_width = sizes
    own_rows = rows // n
    full = 2 * half_width
    tiles = half_width // LANES
    groups = ctf_ref.shape[0]
    me = lax.axis_index("blk")
    core = me % 2
    chip = me // 2
    a, b = chip // nb, chip % nb

    def at(pa, pb, pc):
        return (pa * nb + pb) * 2 + pc

    loads = [
        pltpu.make_async_copy(source, target, load_sem.at[k])
        for k, (source, target) in enumerate((
            (grp_hbm, grp_ref), (off_hbm, off_ref), (lim_hbm, lim_ref),
            (img_hbm, pkt.at[me, :, pl.ds(0, full)]),
            (ctf_hbm, ctf_ref), (noise_hbm, noise_ref), (proj_hbm, proj_ref),
        ))
    ]
    for load in loads:
        load.start()

    barrier = pltpu.get_barrier_semaphore()
    for step in range(1, n):
        pl.semaphore_signal(barrier, inc=1, device_id={"blk": (me + step) % n})

    sub = lax.broadcasted_iota(jnp.int32, (own_rows, LANES), 0)
    lane = lax.broadcasted_iota(jnp.int32, (own_rows, LANES), 1)
    for load in loads[:3]:
        load.wait()
    meta = jnp.zeros((own_rows, LANES), jnp.float32)
    for p in range(own_rows):
        entries = [off_ref[p, j, s] for s in range(shifts) for j in range(2)]
        entries += [grp_ref[p], lim_ref[p]]
        for column, entry in enumerate(entries):
            meta = jnp.where((sub == p) & (lane == column), entry.astype(jnp.float32), meta)
    pkt[me, :, full:] = meta.astype(jnp.bfloat16)
    loads[3].wait()

    pl.semaphore_wait(barrier, n - 1)

    sends = []

    def send(slot, target):
        copy = pltpu.make_async_remote_copy(
            src_ref=pkt.at[slot], dst_ref=pkt.at[slot],
            send_sem=send_sem.at[len(sends)], recv_sem=recv_sem.at[slot],
            device_id={"blk": target},
        )
        copy.start()
        sends.append(copy)

    def arrived(slot):
        pltpu.make_async_remote_copy(
            src_ref=pkt.at[slot], dst_ref=pkt.at[slot],
            send_sem=send_sem.at[0], recv_sem=recv_sem.at[slot],
            device_id={"blk": (me + 1) % n},
        ).wait_recv()

    other = me + 1 - 2 * core
    for j in range(1, na):
        send(me, at((a + j) % na, b, core))
    for k in range(1, nb):
        send(me, at(a, (b + k) % nb, core))
    send(me, other)

    plane = 2 * nb * own_rows

    def widen(pa):
        at_rows = pl.ds(pl.multiple_of(pa * plane, plane), plane)
        image[at_rows, :] = jnp.concatenate(
            [pkt[pa * nb * 2 + d].astype(jnp.float32) for d in range(2 * nb)], axis=0)

    for which, ref in enumerate((ctf_ref, noise_ref)):
        loads[4 + which].wait()
        for part, value in enumerate(three_parts(ref[...])):
            tabs[part * groups:(part + 1) * groups, which * half_width:(which + 1) * half_width] = value
    loads[6].wait()
    proj_rows = proj_ref.shape[1]
    for batch in range(proj_ref.shape[0]):
        real = proj_ref[batch, :, :half_width].astype(jnp.float32)
        imag = proj_ref[batch, :, half_width:].astype(jnp.float32)
        power[batch * proj_rows:(batch + 1) * proj_rows, :] = real * real + imag * imag

    for j in range(1, na):
        slot = at((a + na - j) % na, b, core)
        arrived(slot)
        for k in range(1, nb):
            send(slot, at(a, (b + k) % nb, core))
        send(slot, other)
    for k in range(1, nb):
        for j in range(na):
            slot = at((a + na - j) % na, (b + nb - k) % nb, core)
            arrived(slot)
            send(slot, other)
    for j in range(na):
        pa = (a + na - j) % na
        for k in range(nb):
            arrived(at(pa, (b + nb - k) % nb, 1 - core))
        widen(pa)

    lane = lax.broadcasted_iota(jnp.int32, (rows, LANES), 1)
    sub = lax.broadcasted_iota(jnp.int32, (rows, LANES), 0)
    side = lane // KY
    freq_y = lane % KY - KY // 2
    side_f, freq_yf = side.astype(jnp.float32), freq_y.astype(jnp.float32)
    meta = image[:, full:]

    def column(j):
        return jnp.broadcast_to(meta[:, j:j + 1], (rows, LANES))

    middle = TILE_KX * (tiles // 2)
    for s in range(shifts):
        at_rows = slice(s * rows, (s + 1) * rows)
        off_x, off_y = column(2 * s), column(2 * s + 1)
        c0, s0 = turn_cos_sin((middle + side_f) * off_x + freq_yf * off_y)
        cd, sd = turn_cos_sin(TILE_KX * off_x)
        ec_p[at_rows, :], es_p[at_rows, :] = c0, s0
        ec_m[at_rows, :], es_m[at_rows, :] = c0 * cd + s0 * sd, s0 * cd - c0 * sd
        dc[at_rows, :], ds[at_rows, :] = cd, sd
    group_of = column(2 * shifts)[:, :3 * groups].astype(jnp.int32)
    lane_group = lax.broadcasted_iota(jnp.int32, (rows, 3 * groups), 1) % groups
    one_hot = (group_of == lane_group).astype(jnp.float32).astype(jnp.bfloat16)
    limit = column(2 * shifts + 1)
    limit_sq = limit * limit

    ctf_rows[...] = jnp.dot(one_hot, tabs[...], preferred_element_type=jnp.float32)
    chunk = 4 * LANES
    lane_chunk = lax.broadcasted_iota(jnp.int32, (rows, chunk), 1)
    chunk_x = lane_chunk // KY
    chunk_y = (lane_chunk % KY - KY // 2).astype(jnp.float32)
    limit_chunk = jnp.concatenate([limit_sq] * (chunk // LANES), axis=1)

    def weight_step(step, norm):
        re_cols = pl.ds(pl.multiple_of(step * chunk, chunk), chunk)
        im_cols = pl.ds(pl.multiple_of(half_width + step * chunk, chunk), chunk)
        x_re, x_im = image[:, re_cols], image[:, im_cols]
        c, w = ctf_rows[:, re_cols], ctf_rows[:, im_cols]
        freq_x = (chunk // KY * step + chunk_x).astype(jnp.float32)
        w = jnp.where(freq_x * freq_x + chunk_y * chunk_y < limit_chunk, w, 0.0)
        wc = w * c
        quad_w[:, re_cols] = wc * c
        image[:, re_cols], image[:, im_cols] = wc * x_re, wc * x_im
        return norm + w * (x_re * x_re + x_im * x_im)

    norm = lax.fori_loop(0, half_width // chunk, weight_step, jnp.zeros((rows, chunk), jnp.float32))
    norm = jnp.sum(norm, axis=1, keepdims=True)

    depth = 4
    for ec, es, sign in ((ec_p, es_p, 1), (ec_m, es_m, -1)):
        first = tiles // 2 if sign > 0 else tiles // 2 - 1

        @pl.loop(0, tiles // 2 // depth)
        def _(m):
            for r in range(0, rows, 16):
                cols, factors = [], []
                for q in range(depth):
                    tile = first + sign * (m * depth + q)
                    re_cols = pl.ds(pl.multiple_of(tile * LANES, LANES), LANES)
                    im_cols = pl.ds(pl.multiple_of(half_width + tile * LANES, LANES), LANES)
                    cols.append((re_cols, im_cols))
                    factors.append((image[r:r + 16, re_cols], image[r:r + 16, im_cols]))
                for s in range(shifts):
                    at_rows = slice(s * rows + r, s * rows + r + 16)
                    ck, sk, cd, sd = ec[at_rows, :], es[at_rows, :], dc[at_rows, :], ds[at_rows, :]
                    for (re_cols, im_cols), (u_re, u_im) in zip(cols, factors):
                        wbuf[at_rows, re_cols] = (u_re * ck + u_im * sk).astype(jnp.bfloat16)
                        wbuf[at_rows, im_cols] = (u_im * ck - u_re * sk).astype(jnp.bfloat16)
                        if sign > 0:
                            ck, sk = ck * cd - sk * sd, sk * cd + ck * sd
                        else:
                            ck, sk = ck * cd + sk * sd, sk * cd - ck * sd
                    ec[at_rows, :], es[at_rows, :] = ck, sk

    p_rows = jnp.concatenate([proj_ref[k] for k in range(proj_ref.shape[0])], axis=0)
    cross = lax.dot_general(
        wbuf[...], p_rows, (((1,), (1,)), ((), ())), preferred_element_type=jnp.float32)
    quad = lax.dot_general(
        quad_w[...], power[...], (((1,), (1,)), ((), ())),
        precision=lax.Precision.HIGHEST, preferred_element_type=jnp.float32)
    base = norm + quad
    scale = 0.5 / math.sqrt(half_width)
    scores = [-(base - 2.0 * cross[s * rows:(s + 1) * rows, :]) * scale for s in range(shifts)]
    top = functools.reduce(jnp.maximum, scores)
    top = jnp.max(top, axis=1, keepdims=True)
    total = sum(jnp.exp(score - top) for score in scores)
    total = jnp.sum(total, axis=1, keepdims=True)

    mid = LANES // 2
    row = jnp.where(lane == sub, top, 0.0) + jnp.where(lane == sub + mid, total, 0.0)
    stats[me] = jnp.sum(row, axis=0, keepdims=True)
    stat_copies = []
    for step in range(1, n):
        copy = pltpu.make_async_remote_copy(
            src_ref=stats.at[me], dst_ref=stats.at[me],
            send_sem=stat_send.at[step], recv_sem=stat_recv.at[me],
            device_id={"blk": (me + step) % n},
        )
        copy.start()
        stat_copies.append(copy)
    for step in range(1, n):
        slot = (me + n - step) % n
        pltpu.make_async_remote_copy(
            src_ref=stats.at[slot], dst_ref=stats.at[slot],
            send_sem=stat_send.at[step], recv_sem=stat_recv.at[slot],
            device_id={"blk": (me + step) % n},
        ).wait_recv()
    tops = jnp.concatenate([stats[d] for d in range(n)], axis=0)
    totals = pltpu.roll(tops, mid, 1)
    best = jnp.max(tops, axis=0, keepdims=True)
    all_total = jnp.sum(totals * jnp.exp(tops - best), axis=0, keepdims=True)
    log_row = best + jnp.log(all_total)
    log_total = jnp.sum(jnp.where(lane == sub, log_row, 0.0), axis=1, keepdims=True)
    best_row = jnp.exp(best - log_row)
    lane_one = lax.broadcasted_iota(jnp.int32, (1, LANES), 1)
    for p in range(own_rows):
        mine = lane_one == me * own_rows + p
        best_ref[p] = jnp.sum(jnp.where(mine, best_row, 0.0))
        log_ref[p] = jnp.sum(jnp.where(mine, log_row, 0.0))

    posterior = jnp.concatenate([jnp.exp(score - log_total) for score in scores], axis=0)
    posterior = posterior.T.astype(jnp.bfloat16)
    gain = proj_ref.shape[0] * proj_rows / own_rows

    wide = full // store_sem.shape[0]

    def store(step):
        cols = pl.ds(pl.multiple_of(step * wide, wide), wide)
        return pltpu.make_async_copy(
            out_ref.at[:, :, cols], out_hbm.at[:, :, cols], store_sem.at[step])

    @pl.loop(0, full // wide)
    def _(step):
        cols = pl.ds(pl.multiple_of(step * wide, wide), wide)
        part = jnp.dot(posterior, wbuf[:, cols], preferred_element_type=jnp.float32) * gain
        for k in range(proj_ref.shape[0]):
            out_ref[k, :, cols] = part[k * proj_rows:(k + 1) * proj_rows]
        store(step).start()

    @pl.loop(0, full // wide)
    def _(step):
        store(step).wait()

    for copy in sends + stat_copies:
        copy.wait_send()


def fused(n, projections, images, ctf_group, shift_offsets, shell_limit, ctf_table, noise_weight):
    batches, orient, full = projections.shape
    half_width = full // 2
    own_rows, shifts = shift_offsets.shape[:2]
    rows, cand = n * own_rows, batches * orient
    na, nb = grid_sides(n)
    groups = ctf_table.shape[0]
    smem = pl.BlockSpec(memory_space=pltpu.SMEM)
    f32, bf16 = jnp.float32, jnp.bfloat16
    table = pltpu.VMEM((shifts * rows, LANES), f32)
    return pl.pallas_call(
        functools.partial(kernel, (n, na, nb, rows, shifts, half_width)),
        out_shape=(
            jax.ShapeDtypeStruct(projections.shape, f32),
            jax.ShapeDtypeStruct((own_rows,), f32),
            jax.ShapeDtypeStruct((own_rows,), f32),
        ),
        in_specs=[pl.BlockSpec(memory_space=pltpu.HBM)] * 7,
        out_specs=(pl.BlockSpec(memory_space=pltpu.HBM), smem, smem),
        scratch_shapes=[
            pltpu.VMEM(projections.shape, f32),
            pltpu.VMEM(projections.shape, bf16),
            pltpu.SMEM(ctf_group.shape, jnp.int32),
            pltpu.SMEM((own_rows, 2, shifts), jnp.int32),
            pltpu.SMEM(shell_limit.shape, jnp.int32),
            pltpu.VMEM(ctf_table.shape, f32),
            pltpu.VMEM(noise_weight.shape, f32),
            pltpu.VMEM((n, own_rows, full + LANES), bf16),
            pltpu.VMEM((rows, full + LANES), f32),
            pltpu.VMEM((cand, half_width), f32),
            pltpu.VMEM((rows, half_width), f32),
            pltpu.VMEM((3 * groups, full), bf16),
            pltpu.VMEM((rows, full), f32),
            table, table, table, table, table, table,
            pltpu.VMEM((shifts * rows, full), bf16),
            pltpu.VMEM((n, 1, LANES), f32),
            pltpu.SemaphoreType.DMA((7,)),
            pltpu.SemaphoreType.DMA((8,)),
            pltpu.SemaphoreType.DMA((n,)),
            pltpu.SemaphoreType.DMA((n,)),
            pltpu.SemaphoreType.DMA((n,)),
            pltpu.SemaphoreType.DMA((n,)),
        ],
        compiler_params=pltpu.CompilerParams(
            collective_id=0, has_side_effects=True, vmem_limit_bytes=VMEM_LIMIT),
    )(projections, images, ctf_group, shift_offsets.transpose(0, 2, 1), shell_limit, ctf_table, noise_weight)


def per_device(n, *args):
    particles = n * args[1].shape[0]
    if particles > LANES // 2:
        return local(*args)
    return fused(n, *args)


def solution(mesh):
    in_specs = (
        P(None, ("groups", "blk"), None),
        P(("groups", "blk"), None),
        P(("groups", "blk")),
        P(("groups", "blk"), None, None),
        P(("groups", "blk")),
        P("groups", None),
        P("groups", None),
    )
    out_specs = (P(None, ("groups", "blk"), None), P(("groups", "blk")), P(("groups", "blk")))
    return jax.shard_map(
        functools.partial(per_device, mesh.shape["blk"]),
        mesh=mesh, in_specs=in_specs, out_specs=out_specs, check_vma=False,
    )
```

```python
import functools
import math

import jax
import jax.numpy as jnp
from jax import lax
from jax.experimental import pallas as pl
from jax.experimental.pallas import tpu as pltpu
from jax.sharding import PartitionSpec as P

KY = 64
IMG = 256


def combined_all(value, axis, join):
    pieces = jax.tree.map(lambda part: lax.all_gather(part, axis), value)
    head = jax.tree.map(lambda part: part[0], pieces)
    tail = jax.tree.map(lambda part: part[1:], pieces)
    so_far, _ = lax.scan(lambda so_far, section: (join(so_far, section), None), head, tail)
    return so_far


def frequencies(half_width):
    positions = jnp.arange(half_width, dtype=jnp.int32)
    return (positions // KY, positions % KY - KY // 2)


def shift_factors(offsets, half_width):
    row_count = offsets.shape[0]
    shift_count = offsets.shape[1]
    row_freq = jnp.arange(half_width // KY, dtype=jnp.int32)
    col_freq = jnp.arange(KY, dtype=jnp.int32) - KY // 2
    turns_x = row_freq[None, None, :] * offsets[:, :, 0:1] % IMG
    turns_y = col_freq[None, None, :] * offsets[:, :, 1:2] % IMG
    angle_x = turns_x.astype(jnp.float32) * (2.0 * math.pi / IMG)
    angle_y = turns_y.astype(jnp.float32) * (2.0 * math.pi / IMG)
    cosine_x = jnp.cos(angle_x)[:, :, :, None]
    sine_x = jnp.sin(angle_x)[:, :, :, None]
    cosine_y = jnp.cos(angle_y)[:, :, None, :]
    sine_y = jnp.sin(angle_y)[:, :, None, :]
    cosine = cosine_x * cosine_y - sine_x * sine_y
    sine_part = sine_x * cosine_y + cosine_x * sine_y
    return (
        cosine.reshape(row_count, shift_count, half_width),
        sine_part.reshape(row_count, shift_count, half_width),
    )


def particle_terms(image_rows, ctf_rows, weight_rows, offsets, limits, freq_x, freq_y):
    half_width = image_rows.shape[1] // 2
    image_real = image_rows[:, :half_width].astype(jnp.float32)
    image_imag = image_rows[:, half_width:].astype(jnp.float32)
    radius_sq = freq_x * freq_x + freq_y * freq_y
    inside = (radius_sq[None, :] < (limits * limits)[:, None]).astype(jnp.float32)
    masked_weight = inside * weight_rows
    ctf_weight = masked_weight * ctf_rows
    norm_term = jnp.sum(masked_weight * (image_real * image_real + image_imag * image_imag), axis=1)
    quad_weight = ctf_weight * ctf_rows
    cosine, sine_part = shift_factors(offsets, half_width)
    shift_real = image_real[:, None, :] * cosine + image_imag[:, None, :] * sine_part
    shift_imag = image_imag[:, None, :] * cosine - image_real[:, None, :] * sine_part
    weighted = jnp.concatenate(
        [ctf_weight[:, None, :] * shift_real, ctf_weight[:, None, :] * shift_imag], axis=2
    ).astype(jnp.bfloat16)
    return (weighted, norm_term, quad_weight)


def combine_lse(first, second):
    score_top = jnp.maximum(first[0], second[0])
    exp_total = first[1] * jnp.exp(first[0] - score_top) + second[1] * jnp.exp(
        second[0] - score_top
    )
    return (score_top, exp_total)


def block_shape(row_count):
    return 64 if row_count % 64 == 0 else row_count


def split_rows(members, block_rows):
    return tuple(
        (
            member.reshape((member.shape[0] // block_rows, block_rows) + member.shape[1:])
            for member in members
        )
    )


def local(projections, images, ctf_group, shift_offsets, shell_limit, ctf_table, noise_weight):
    batch_count, orient_dev, full_width = projections.shape
    half_width = full_width // 2
    candidates = batch_count * orient_dev
    flat_proj = projections.reshape(candidates, full_width)
    proj_real = flat_proj[:, :half_width].astype(jnp.float32)
    proj_imag = flat_proj[:, half_width:].astype(jnp.float32)
    proj_power = proj_real * proj_real + proj_imag * proj_imag
    freq_x, freq_y = frequencies(half_width)
    score_scale = 0.5 / math.sqrt(half_width)
    group_count = ctf_table.shape[0]
    particles_dev = images.shape[0]

    def block_terms(members):
        image_rows, groups, offsets, limits = members
        one_hot = (groups[:, None] == jnp.arange(group_count, dtype=jnp.int32)[None, :]).astype(
            jnp.float32
        )
        ctf_rows = jnp.dot(
            one_hot, ctf_table, precision=lax.Precision.HIGHEST, preferred_element_type=jnp.float32
        )
        weight_rows = jnp.dot(
            one_hot,
            noise_weight,
            precision=lax.Precision.HIGHEST,
            preferred_element_type=jnp.float32,
        )
        return particle_terms(image_rows, ctf_rows, weight_rows, offsets, limits, freq_x, freq_y)

    def score_block(members):
        weighted, norm_term, quad_weight = block_terms(members)
        cross_term = lax.dot_general(
            weighted, flat_proj, (((2,), (1,)), ((), ())), preferred_element_type=jnp.float32
        )
        quad_term = lax.dot_general(
            quad_weight,
            proj_power,
            (((1,), (1,)), ((), ())),
            precision=lax.Precision.HIGHEST,
            preferred_element_type=jnp.float32,
        )
        return -(norm_term[:, None, None] - 2.0 * cross_term + quad_term[:, None, :]) * score_scale

    members = (
        lax.all_gather(images, "blk", axis=0, tiled=True),
        lax.all_gather(ctf_group, "blk", axis=0, tiled=True),
        lax.all_gather(shift_offsets, "blk", axis=0, tiled=True),
        lax.all_gather(shell_limit, "blk", axis=0, tiled=True),
    )
    row_count = members[0].shape[0]
    block_rows = block_shape(row_count)
    blocks = lax.map(score_block, split_rows(members, block_rows))
    scores = blocks.reshape((row_count,) + blocks.shape[2:])
    local_top = jnp.max(scores, axis=(1, 2))
    local_total = jnp.sum(jnp.exp(scores - local_top[:, None, None]), axis=(1, 2))
    score_top, exp_total = combined_all((local_top, local_total), "blk", combine_lse)
    log_total = score_top + jnp.log(exp_total)
    pieces = (
        lax.all_gather(images, "blk", axis=0, tiled=True),
        lax.all_gather(ctf_group, "blk", axis=0, tiled=True),
        lax.all_gather(shift_offsets, "blk", axis=0, tiled=True),
        lax.all_gather(shell_limit, "blk", axis=0, tiled=True),
    )
    row_count = pieces[0].shape[0]
    block_rows = block_shape(row_count)

    def add_block(carry, packed):
        member_block, score_block_values, log_block = packed
        weighted = block_terms(member_block)[0]
        posterior = jnp.exp(score_block_values - log_block[:, None, None]).astype(jnp.bfloat16)
        contrib = lax.dot_general(
            posterior, weighted, (((0, 1), (0, 1)), ((), ())), preferred_element_type=jnp.float32
        )
        return (carry + contrib, None)

    zero_slices = jnp.zeros((candidates, full_width), jnp.float32)
    packed_scores = split_rows((scores, log_total), block_rows)
    summed, unused_out = lax.scan(
        add_block, zero_slices, (split_rows(pieces, block_rows), packed_scores[0], packed_scores[1])
    )
    slices = (summed * (candidates / particles_dev)).reshape(batch_count, orient_dev, full_width)
    own_start = lax.axis_index("blk") * particles_dev
    own_top = lax.dynamic_slice_in_dim(score_top, own_start, particles_dev, 0)
    own_log = lax.dynamic_slice_in_dim(log_total, own_start, particles_dev, 0)
    best_posterior = jnp.exp(own_top - own_log)
    return (slices, best_posterior, own_log)


LANES = 128
TILE_KX = LANES // KY
VMEM_LIMIT = 60 * 1024 * 1024


def turn_cos_sin(turns):
    turns = turns - IMG * jnp.floor(turns * (1.0 / IMG) + 0.5)
    half = turns * (math.pi / IMG)
    sq = half * half
    sin_poly = 1.0 / math.factorial(13)
    for power in (11, 9, 7, 5, 3, 1):
        sin_poly = sin_poly * sq + (-1.0) ** (power // 2) / math.factorial(power)
    cos_poly = 1.0 / math.factorial(14) * -1.0
    for power in (12, 10, 8, 6, 4, 2, 0):
        cos_poly = cos_poly * sq + (-1.0) ** (power // 2) / math.factorial(power)
    sin_half = sin_poly * half
    return 1.0 - 2.0 * sin_half * sin_half, 2.0 * sin_half * cos_poly


def three_parts(values):
    first = values.astype(jnp.bfloat16)
    rest = values - first.astype(jnp.float32)
    second = rest.astype(jnp.bfloat16)
    third = (rest - second.astype(jnp.float32)).astype(jnp.bfloat16)
    return first, second, third


def grid_sides(device_count):
    chips = device_count // 2
    outer = 2 ** ((chips.bit_length()) // 2)
    return outer, chips // outer


def score_kernel(
    sizes,
    proj_hbm, img_hbm, grp_hbm, off_hbm, lim_hbm, ctf_hbm, noise_hbm,
    post_ref, wide_hbm, best_ref, log_ref,
    proj_ref, grp_ref, off_ref, lim_ref, ctf_ref, noise_ref,
    pkt, notes, image, power, quad_w, quad, tabs, look, ec_p, es_p, ec_m, es_m, dc, ds, wbuf, score, stats,
    load_sem, wide_sem, send_sem, recv_sem, note_send, note_recv, stat_send, stat_recv,
):
    n, na, nb, rows, shifts, half_width = sizes
    own_rows = rows // n
    full = 2 * half_width
    tiles = half_width // LANES
    groups = ctf_ref.shape[0]
    plane = 2 * nb * own_rows
    pairs, pair_rows = na // 2, 2 * plane
    block = shifts * pair_rows
    me = lax.axis_index("blk")
    core = me % 2
    chip = me // 2
    a, b = chip // nb, chip % nb
    other = me + 1 - 2 * core

    def at(pa, pb, pc):
        return (pa * nb + pb) * 2 + pc

    def plane_at(step, half, sign):
        pair = (a // 2 + pairs + sign * step) % pairs
        return 2 * pair + (a % 2 if half == 0 else 1 - a % 2)

    loads = [
        pltpu.make_async_copy(source, target, load_sem.at[k])
        for k, (source, target) in enumerate((
            (grp_hbm, grp_ref), (off_hbm, off_ref), (lim_hbm, lim_ref),
            (img_hbm, pkt.at[me]),
            (ctf_hbm, ctf_ref), (noise_hbm, noise_ref), (proj_hbm, proj_ref),
        ))
    ]
    for load in loads:
        load.start()

    barrier = pltpu.get_barrier_semaphore()
    for step in range(1, n):
        pl.semaphore_signal(barrier, inc=1, device_id={"blk": (me + step) % n})

    sub = lax.broadcasted_iota(jnp.int32, (own_rows, LANES), 0)
    lane = lax.broadcasted_iota(jnp.int32, (own_rows, LANES), 1)
    for load in loads[:3]:
        load.wait()
    note = jnp.zeros((own_rows, LANES), jnp.float32)
    for p in range(own_rows):
        entries = [off_ref[p, j, s] for s in range(shifts) for j in range(2)]
        entries += [grp_ref[p], lim_ref[p]]
        for column, entry in enumerate(entries):
            note = jnp.where((sub == p) & (lane == column), entry.astype(jnp.float32), note)
    notes[me] = note
    loads[3].wait()

    pl.semaphore_wait(barrier, n - 1)

    sends = []

    def send(slot, target):
        copy = pltpu.make_async_remote_copy(
            src_ref=pkt.at[slot], dst_ref=pkt.at[slot],
            send_sem=send_sem.at[len(sends)], recv_sem=recv_sem.at[slot],
            device_id={"blk": target},
        )
        copy.start()
        sends.append(copy)

    def arrived(slot):
        pltpu.make_async_remote_copy(
            src_ref=pkt.at[slot], dst_ref=pkt.at[slot],
            send_sem=send_sem.at[0], recv_sem=recv_sem.at[slot],
            device_id={"blk": (me + 1) % n},
        ).wait_recv()

    def swap(buffer, send_sems, recv_sems):
        copies = []
        for step in range(1, n):
            copy = pltpu.make_async_remote_copy(
                src_ref=buffer.at[me], dst_ref=buffer.at[me],
                send_sem=send_sems.at[step], recv_sem=recv_sems.at[me],
                device_id={"blk": (me + step) % n},
            )
            copy.start()
            copies.append(copy)
        return copies

    def swapped(buffer, send_sems, recv_sems):
        for step in range(1, n):
            slot = (me + n - step) % n
            pltpu.make_async_remote_copy(
                src_ref=buffer.at[slot], dst_ref=buffer.at[slot],
                send_sem=send_sems.at[step], recv_sem=recv_sems.at[slot],
                device_id={"blk": (me + step) % n},
            ).wait_recv()

    far = [(step, half) for step in range(pairs) for half in range(2)][1:]
    for step, half in far:
        send(me, at(plane_at(step, half, 1), b, core))
    for k in range(1, nb):
        send(me, at(a, (b + k) % nb, core))
    send(me, other)
    note_copies = swap(notes, note_send, note_recv)

    for which, ref in enumerate((ctf_ref, noise_ref)):
        loads[4 + which].wait()
        for part, value in enumerate(three_parts(ref[...])):
            tabs[part * groups:(part + 1) * groups, which * half_width:(which + 1) * half_width] = value
    loads[6].wait()
    proj_rows = proj_ref.shape[1]
    for batch in range(proj_ref.shape[0]):
        real = proj_ref[batch, :, :half_width].astype(jnp.float32)
        imag = proj_ref[batch, :, half_width:].astype(jnp.float32)
        power[batch * proj_rows:(batch + 1) * proj_rows, :] = real * real + imag * imag

    def pass_plane(step, half):
        slot = at(plane_at(step, half, -1), b, core)
        arrived(slot)
        for k in range(1, nb):
            send(slot, at(a, (b + k) % nb, core))
        send(slot, other)

    def pass_side(step, half):
        for k in range(1, nb):
            slot = at(plane_at(step, half, -1), (b + nb - k) % nb, core)
            arrived(slot)
            send(slot, other)

    pass_plane(0, 1)
    pass_side(0, 0)

    swapped(notes, note_send, note_recv)
    meta = jnp.concatenate([notes[d] for d in range(n)], axis=0)
    lane = lax.broadcasted_iota(jnp.int32, (rows, LANES), 1)
    sub = lax.broadcasted_iota(jnp.int32, (rows, LANES), 0)
    side_f = (lane // KY).astype(jnp.float32)
    freq_yf = (lane % KY - KY // 2).astype(jnp.float32)

    def column(j):
        return jnp.broadcast_to(meta[:, j:j + 1], (rows, LANES))

    middle = TILE_KX * (tiles // 2)
    for s in range(shifts):
        off_x, off_y = column(2 * s), column(2 * s + 1)
        c0, s0 = turn_cos_sin((middle + side_f) * off_x + freq_yf * off_y)
        cd, sd = turn_cos_sin(TILE_KX * off_x)
        cm, sm = c0 * cd + s0 * sd, s0 * cd - c0 * sd
        for pair in range(pairs):
            at_rows = slice(pair * block + s * pair_rows, pair * block + (s + 1) * pair_rows)
            own = slice(pair * pair_rows, (pair + 1) * pair_rows)
            for ref, value in ((ec_p, c0), (es_p, s0), (ec_m, cm), (es_m, sm), (dc, cd), (ds, sd)):
                ref[at_rows, :] = value[own]

    for step, half in far[1:]:
        pass_plane(step, half)
    pass_side(0, 1)

    group_of = column(2 * shifts)[:, :3 * groups].astype(jnp.int32)
    lane_group = lax.broadcasted_iota(jnp.int32, (rows, 3 * groups), 1) % groups
    one_hot = (group_of == lane_group).astype(jnp.float32).astype(jnp.bfloat16)
    look[...] = jnp.dot(one_hot, tabs[...], preferred_element_type=jnp.float32)
    limit = column(2 * shifts + 1)
    limit_sq = limit * limit
    chunk = 4 * LANES
    lane_chunk = lax.broadcasted_iota(jnp.int32, (rows, chunk), 1)
    chunk_x = lane_chunk // KY
    chunk_y = (lane_chunk % KY - KY // 2).astype(jnp.float32)
    limit_chunk = jnp.concatenate([limit_sq] * (chunk // LANES), axis=1)

    @pl.loop(0, half_width // chunk)
    def _(step):
        c_cols = pl.ds(pl.multiple_of(step * chunk, chunk), chunk)
        w_cols = pl.ds(pl.multiple_of(half_width + step * chunk, chunk), chunk)
        c, w = look[:, c_cols], look[:, w_cols]
        freq_x = (chunk // KY * step + chunk_x).astype(jnp.float32)
        w = jnp.where(freq_x * freq_x + chunk_y * chunk_y < limit_chunk, w, 0.0)
        wc = w * c
        quad_w[:, c_cols] = wc * c
        look[:, c_cols], look[:, w_cols] = wc, w

    for step, half in far[1:]:
        pass_side(step, half)
    quad[...] = lax.dot_general(
        quad_w[...], power[...], (((1,), (1,)), ((), ())),
        precision=lax.Precision.HIGHEST, preferred_element_type=jnp.float32)

    scale = 0.5 / math.sqrt(half_width)
    mid = LANES // 2
    depth = 4
    p_rows = jnp.concatenate([proj_ref[k] for k in range(proj_ref.shape[0])], axis=0)
    stat_row = jnp.zeros((1, LANES), jnp.float32)
    wide_copies = []
    for pp in range(pairs):
        pair = (a // 2 + pairs - pp) % pairs
        for half in range(2):
            pa = plane_at(pp, half, -1)
            for k in range(nb):
                arrived(at(pa, (b + nb - k) % nb, 1 - core))
        norms = []
        for half in range(2):
            pa = 2 * pair + half
            at_rows = pl.ds(pl.multiple_of(pa * plane, plane), plane)
            x = jnp.concatenate(
                [pkt[pa * nb * 2 + d].astype(jnp.float32) for d in range(2 * nb)], axis=0)
            x_re, x_im = x[:, :half_width], x[:, half_width:]
            wc, w = look[at_rows, :half_width], look[at_rows, half_width:]
            image[at_rows, :half_width] = wc * x_re
            image[at_rows, half_width:] = wc * x_im
            norms.append(jnp.sum(w * (x_re * x_re + x_im * x_im), axis=1, keepdims=True))
        norm = jnp.concatenate(norms, axis=0)
        in_rows = pl.ds(pl.multiple_of(pair * pair_rows, pair_rows), pair_rows)
        block_rows = pl.ds(pl.multiple_of(pair * block, block), block)

        for ec, es, sign in ((ec_p, es_p, 1), (ec_m, es_m, -1)):
            first = tiles // 2 if sign > 0 else tiles // 2 - 1

            @pl.loop(0, tiles // 2 // depth)
            def _(m):
                cols, factors = [], []
                for q in range(depth):
                    tile = first + sign * (m * depth + q)
                    re_cols = pl.ds(pl.multiple_of(tile * LANES, LANES), LANES)
                    im_cols = pl.ds(pl.multiple_of(half_width + tile * LANES, LANES), LANES)
                    cols.append((re_cols, im_cols))
                    factors.append((image[in_rows, re_cols], image[in_rows, im_cols]))
                for s in range(shifts):
                    at_rows = pl.ds(pl.multiple_of(pair * block + s * pair_rows, pair_rows), pair_rows)
                    ck, sk, cd, sd = ec[at_rows, :], es[at_rows, :], dc[at_rows, :], ds[at_rows, :]
                    for (re_cols, im_cols), (u_re, u_im) in zip(cols, factors):
                        wbuf[at_rows, re_cols] = (u_re * ck + u_im * sk).astype(jnp.bfloat16)
                        wbuf[at_rows, im_cols] = (u_im * ck - u_re * sk).astype(jnp.bfloat16)
                        if sign > 0:
                            ck, sk = ck * cd - sk * sd, sk * cd + ck * sd
                        else:
                            ck, sk = ck * cd + sk * sd, sk * cd - ck * sd
                    ec[at_rows, :], es[at_rows, :] = ck, sk

        copy = pltpu.make_async_copy(wbuf.at[block_rows], wide_hbm.at[block_rows], wide_sem.at[pp])
        copy.start()
        wide_copies.append(copy)
        cross = lax.dot_general(
            wbuf[block_rows, :], p_rows, (((1,), (1,)), ((), ())), preferred_element_type=jnp.float32)
        base = norm + quad[in_rows, :]
        scores = [-(base - 2.0 * cross[s * pair_rows:(s + 1) * pair_rows]) * scale for s in range(shifts)]
        score[block_rows, :] = jnp.concatenate(scores, axis=0)
        top = functools.reduce(jnp.maximum, scores)
        top = jnp.max(top, axis=1, keepdims=True)
        total = sum(jnp.exp(part - top) for part in scores)
        total = jnp.sum(total, axis=1, keepdims=True)
        spot = (lane - sub)[:pair_rows] - pair * pair_rows
        row = jnp.where(spot == 0, top, 0.0) + jnp.where(spot == mid, total, 0.0)
        stat_row = stat_row + jnp.sum(row, axis=0, keepdims=True)

    stats[me] = stat_row
    stat_copies = swap(stats, stat_send, stat_recv)
    swapped(stats, stat_send, stat_recv)
    tops = jnp.concatenate([stats[d] for d in range(n)], axis=0)
    totals = pltpu.roll(tops, mid, 1)
    best = jnp.max(tops, axis=0, keepdims=True)
    all_total = jnp.sum(totals * jnp.exp(tops - best), axis=0, keepdims=True)
    log_row = best + jnp.log(all_total)
    log_total = jnp.sum(jnp.where(lane == sub, log_row, 0.0), axis=1, keepdims=True)
    posterior = []
    for pair in range(pairs):
        own = jnp.concatenate([log_total[pair * pair_rows:(pair + 1) * pair_rows]] * shifts, axis=0)
        posterior.append(jnp.exp(score[pair * block:(pair + 1) * block, :] - own))
    post_ref[...] = jnp.concatenate(posterior, axis=0).T.astype(jnp.bfloat16)
    best_row = jnp.exp(best - log_row)
    lane_one = lax.broadcasted_iota(jnp.int32, (1, LANES), 1)
    for p in range(own_rows):
        mine = lane_one == me * own_rows + p
        best_ref[p] = jnp.sum(jnp.where(mine, best_row, 0.0))
        log_ref[p] = jnp.sum(jnp.where(mine, log_row, 0.0))

    for copy in sends + note_copies + stat_copies:
        copy.wait_send()
    for copy in wide_copies:
        copy.wait()


def slice_kernel(gain, post_ref, wide_ref, best_ref, log_ref, out_ref, best_out, log_out):
    part = jnp.dot(post_ref[...], wide_ref[...], preferred_element_type=jnp.float32) * gain
    out_ref[...] = part.reshape(out_ref.shape)
    for p in range(best_ref.shape[0]):
        best_out[p] = best_ref[p]
        log_out[p] = log_ref[p]


def fused(n, projections, images, ctf_group, shift_offsets, shell_limit, ctf_table, noise_weight):
    batches, orient, full = projections.shape
    half_width = full // 2
    own_rows, shifts = shift_offsets.shape[:2]
    rows, cand = n * own_rows, batches * orient
    na, nb = grid_sides(n)
    groups = ctf_table.shape[0]
    hbm, smem = pl.BlockSpec(memory_space=pltpu.HBM), pl.BlockSpec(memory_space=pltpu.SMEM)
    vmem = pl.BlockSpec(memory_space=pltpu.VMEM)
    f32, bf16 = jnp.float32, jnp.bfloat16
    table = pltpu.VMEM((shifts * rows, LANES), f32)
    pair_count = jax.ShapeDtypeStruct((own_rows,), f32)
    posterior, wide, best, log_total = pl.pallas_call(
        functools.partial(score_kernel, (n, na, nb, rows, shifts, half_width)),
        out_shape=(
            jax.ShapeDtypeStruct((cand, shifts * rows), bf16),
            jax.ShapeDtypeStruct((shifts * rows, full), bf16),
            pair_count,
            pair_count,
        ),
        in_specs=[hbm] * 7,
        out_specs=(vmem, hbm, smem, smem),
        scratch_shapes=[
            pltpu.VMEM(projections.shape, bf16),
            pltpu.SMEM(ctf_group.shape, jnp.int32),
            pltpu.SMEM((own_rows, 2, shifts), jnp.int32),
            pltpu.SMEM(shell_limit.shape, jnp.int32),
            pltpu.VMEM(ctf_table.shape, f32),
            pltpu.VMEM(noise_weight.shape, f32),
            pltpu.VMEM((n, own_rows, full), bf16),
            pltpu.VMEM((n, own_rows, LANES), f32),
            pltpu.VMEM((rows, full), f32),
            pltpu.VMEM((cand, half_width), f32),
            pltpu.VMEM((rows, half_width), f32),
            pltpu.VMEM((rows, cand), f32),
            pltpu.VMEM((3 * groups, full), bf16),
            pltpu.VMEM((rows, full), f32),
            table, table, table, table, table, table,
            pltpu.VMEM((shifts * rows, full), bf16),
            pltpu.VMEM((shifts * rows, cand), f32),
            pltpu.VMEM((n, 1, LANES), f32),
            pltpu.SemaphoreType.DMA((7,)),
            pltpu.SemaphoreType.DMA((na // 2,)),
        ] + [pltpu.SemaphoreType.DMA((n,))] * 6,
        compiler_params=pltpu.CompilerParams(
            collective_id=0, has_side_effects=True, vmem_limit_bytes=VMEM_LIMIT),
    )(projections, images, ctf_group, shift_offsets.transpose(0, 2, 1), shell_limit, ctf_table, noise_weight)
    columns = 1024
    return pl.pallas_call(
        functools.partial(slice_kernel, cand / own_rows),
        grid=(full // columns,),
        out_shape=(jax.ShapeDtypeStruct(projections.shape, f32), pair_count, pair_count),
        in_specs=[
            pl.BlockSpec((cand, shifts * rows), lambda k: (0, 0)),
            pl.BlockSpec((shifts * rows, columns), lambda k: (0, k)),
            smem, smem,
        ],
        out_specs=(pl.BlockSpec((batches, orient, columns), lambda k: (0, 0, k)), smem, smem),
        compiler_params=pltpu.CompilerParams(vmem_limit_bytes=VMEM_LIMIT),
    )(posterior, wide, best, log_total)


def per_device(n, *args):
    particles = n * args[1].shape[0]
    if particles > LANES // 2:
        return local(*args)
    return fused(n, *args)


def solution(mesh):
    in_specs = (
        P(None, ("groups", "blk"), None),
        P(("groups", "blk"), None),
        P(("groups", "blk")),
        P(("groups", "blk"), None, None),
        P(("groups", "blk")),
        P("groups", None),
        P("groups", None),
    )
    out_specs = (P(None, ("groups", "blk"), None), P(("groups", "blk")), P(("groups", "blk")))
    return jax.shard_map(
        functools.partial(per_device, mesh.shape["blk"]),
        mesh=mesh, in_specs=in_specs, out_specs=out_specs, check_vma=False,
    )
```

```python
import functools
import math

import jax
import jax.numpy as jnp
from jax import lax
from jax.experimental import pallas as pl
from jax.experimental.pallas import tpu as pltpu
from jax.sharding import PartitionSpec as P

KY = 64
IMG = 256


def combined_all(value, axis, join):
    pieces = jax.tree.map(lambda part: lax.all_gather(part, axis), value)
    head = jax.tree.map(lambda part: part[0], pieces)
    tail = jax.tree.map(lambda part: part[1:], pieces)
    so_far, _ = lax.scan(lambda so_far, section: (join(so_far, section), None), head, tail)
    return so_far


def frequencies(half_width):
    positions = jnp.arange(half_width, dtype=jnp.int32)
    return (positions // KY, positions % KY - KY // 2)


def shift_factors(offsets, half_width):
    row_count = offsets.shape[0]
    shift_count = offsets.shape[1]
    row_freq = jnp.arange(half_width // KY, dtype=jnp.int32)
    col_freq = jnp.arange(KY, dtype=jnp.int32) - KY // 2
    turns_x = row_freq[None, None, :] * offsets[:, :, 0:1] % IMG
    turns_y = col_freq[None, None, :] * offsets[:, :, 1:2] % IMG
    angle_x = turns_x.astype(jnp.float32) * (2.0 * math.pi / IMG)
    angle_y = turns_y.astype(jnp.float32) * (2.0 * math.pi / IMG)
    cosine_x = jnp.cos(angle_x)[:, :, :, None]
    sine_x = jnp.sin(angle_x)[:, :, :, None]
    cosine_y = jnp.cos(angle_y)[:, :, None, :]
    sine_y = jnp.sin(angle_y)[:, :, None, :]
    cosine = cosine_x * cosine_y - sine_x * sine_y
    sine_part = sine_x * cosine_y + cosine_x * sine_y
    return (
        cosine.reshape(row_count, shift_count, half_width),
        sine_part.reshape(row_count, shift_count, half_width),
    )


def particle_terms(image_rows, ctf_rows, weight_rows, offsets, limits, freq_x, freq_y):
    half_width = image_rows.shape[1] // 2
    image_real = image_rows[:, :half_width].astype(jnp.float32)
    image_imag = image_rows[:, half_width:].astype(jnp.float32)
    radius_sq = freq_x * freq_x + freq_y * freq_y
    inside = (radius_sq[None, :] < (limits * limits)[:, None]).astype(jnp.float32)
    masked_weight = inside * weight_rows
    ctf_weight = masked_weight * ctf_rows
    norm_term = jnp.sum(masked_weight * (image_real * image_real + image_imag * image_imag), axis=1)
    quad_weight = ctf_weight * ctf_rows
    cosine, sine_part = shift_factors(offsets, half_width)
    shift_real = image_real[:, None, :] * cosine + image_imag[:, None, :] * sine_part
    shift_imag = image_imag[:, None, :] * cosine - image_real[:, None, :] * sine_part
    weighted = jnp.concatenate(
        [ctf_weight[:, None, :] * shift_real, ctf_weight[:, None, :] * shift_imag], axis=2
    ).astype(jnp.bfloat16)
    return (weighted, norm_term, quad_weight)


def combine_lse(first, second):
    score_top = jnp.maximum(first[0], second[0])
    exp_total = first[1] * jnp.exp(first[0] - score_top) + second[1] * jnp.exp(
        second[0] - score_top
    )
    return (score_top, exp_total)


def block_shape(row_count):
    return 64 if row_count % 64 == 0 else row_count


def split_rows(members, block_rows):
    return tuple(
        (
            member.reshape((member.shape[0] // block_rows, block_rows) + member.shape[1:])
            for member in members
        )
    )


def local(projections, images, ctf_group, shift_offsets, shell_limit, ctf_table, noise_weight):
    batch_count, orient_dev, full_width = projections.shape
    half_width = full_width // 2
    candidates = batch_count * orient_dev
    flat_proj = projections.reshape(candidates, full_width)
    proj_real = flat_proj[:, :half_width].astype(jnp.float32)
    proj_imag = flat_proj[:, half_width:].astype(jnp.float32)
    proj_power = proj_real * proj_real + proj_imag * proj_imag
    freq_x, freq_y = frequencies(half_width)
    score_scale = 0.5 / math.sqrt(half_width)
    group_count = ctf_table.shape[0]
    particles_dev = images.shape[0]

    def block_terms(members):
        image_rows, groups, offsets, limits = members
        one_hot = (groups[:, None] == jnp.arange(group_count, dtype=jnp.int32)[None, :]).astype(
            jnp.float32
        )
        ctf_rows = jnp.dot(
            one_hot, ctf_table, precision=lax.Precision.HIGHEST, preferred_element_type=jnp.float32
        )
        weight_rows = jnp.dot(
            one_hot,
            noise_weight,
            precision=lax.Precision.HIGHEST,
            preferred_element_type=jnp.float32,
        )
        return particle_terms(image_rows, ctf_rows, weight_rows, offsets, limits, freq_x, freq_y)

    def score_block(members):
        weighted, norm_term, quad_weight = block_terms(members)
        cross_term = lax.dot_general(
            weighted, flat_proj, (((2,), (1,)), ((), ())), preferred_element_type=jnp.float32
        )
        quad_term = lax.dot_general(
            quad_weight,
            proj_power,
            (((1,), (1,)), ((), ())),
            precision=lax.Precision.HIGHEST,
            preferred_element_type=jnp.float32,
        )
        return -(norm_term[:, None, None] - 2.0 * cross_term + quad_term[:, None, :]) * score_scale

    members = (
        lax.all_gather(images, "blk", axis=0, tiled=True),
        lax.all_gather(ctf_group, "blk", axis=0, tiled=True),
        lax.all_gather(shift_offsets, "blk", axis=0, tiled=True),
        lax.all_gather(shell_limit, "blk", axis=0, tiled=True),
    )
    row_count = members[0].shape[0]
    block_rows = block_shape(row_count)
    blocks = lax.map(score_block, split_rows(members, block_rows))
    scores = blocks.reshape((row_count,) + blocks.shape[2:])
    local_top = jnp.max(scores, axis=(1, 2))
    local_total = jnp.sum(jnp.exp(scores - local_top[:, None, None]), axis=(1, 2))
    score_top, exp_total = combined_all((local_top, local_total), "blk", combine_lse)
    log_total = score_top + jnp.log(exp_total)
    pieces = (
        lax.all_gather(images, "blk", axis=0, tiled=True),
        lax.all_gather(ctf_group, "blk", axis=0, tiled=True),
        lax.all_gather(shift_offsets, "blk", axis=0, tiled=True),
        lax.all_gather(shell_limit, "blk", axis=0, tiled=True),
    )
    row_count = pieces[0].shape[0]
    block_rows = block_shape(row_count)

    def add_block(carry, packed):
        member_block, score_block_values, log_block = packed
        weighted = block_terms(member_block)[0]
        posterior = jnp.exp(score_block_values - log_block[:, None, None]).astype(jnp.bfloat16)
        contrib = lax.dot_general(
            posterior, weighted, (((0, 1), (0, 1)), ((), ())), preferred_element_type=jnp.float32
        )
        return (carry + contrib, None)

    zero_slices = jnp.zeros((candidates, full_width), jnp.float32)
    packed_scores = split_rows((scores, log_total), block_rows)
    summed, unused_out = lax.scan(
        add_block, zero_slices, (split_rows(pieces, block_rows), packed_scores[0], packed_scores[1])
    )
    slices = (summed * (candidates / particles_dev)).reshape(batch_count, orient_dev, full_width)
    own_start = lax.axis_index("blk") * particles_dev
    own_top = lax.dynamic_slice_in_dim(score_top, own_start, particles_dev, 0)
    own_log = lax.dynamic_slice_in_dim(log_total, own_start, particles_dev, 0)
    best_posterior = jnp.exp(own_top - own_log)
    return (slices, best_posterior, own_log)


LANES = 128
TILE_KX = LANES // KY
VMEM_LIMIT = 60 * 1024 * 1024


def turn_cos_sin(turns):
    turns = turns - IMG * jnp.floor(turns * (1.0 / IMG) + 0.5)
    half = turns * (math.pi / IMG)
    sq = half * half
    sin_poly = 1.0 / math.factorial(13)
    for power in (11, 9, 7, 5, 3, 1):
        sin_poly = sin_poly * sq + (-1.0) ** (power // 2) / math.factorial(power)
    cos_poly = 1.0 / math.factorial(14) * -1.0
    for power in (12, 10, 8, 6, 4, 2, 0):
        cos_poly = cos_poly * sq + (-1.0) ** (power // 2) / math.factorial(power)
    sin_half = sin_poly * half
    return 1.0 - 2.0 * sin_half * sin_half, 2.0 * sin_half * cos_poly


def three_parts(values):
    first = values.astype(jnp.bfloat16)
    rest = values - first.astype(jnp.float32)
    second = rest.astype(jnp.bfloat16)
    third = (rest - second.astype(jnp.float32)).astype(jnp.bfloat16)
    return first, second, third


def grid_sides(device_count):
    chips = device_count // 2
    outer = 2 ** ((chips.bit_length()) // 2)
    return outer, chips // outer


def kernel(
    sizes,
    proj_hbm, img_hbm, grp_hbm, off_hbm, lim_hbm, ctf_hbm, noise_hbm,
    post_ref, wide_hbm, own_ref,
    proj_ref, grp_ref, off_ref, lim_ref, ctf_ref, noise_ref,
    pkt, image, power, quad_w, tabs, ctf_rows, ec_p, es_p, ec_m, es_m, dc, ds, wbuf, stats,
    load_sem, wide_sem, send_sem, recv_sem, stat_send, stat_recv,
):
    n, na, nb, rows, shifts, half_width = sizes
    own_rows = rows // n
    full = 2 * half_width
    tiles = half_width // LANES
    groups = ctf_ref.shape[0]
    me = lax.axis_index("blk")
    core = me % 2
    chip = me // 2
    a, b = chip // nb, chip % nb

    def at(pa, pb, pc):
        return (pa * nb + pb) * 2 + pc

    loads = [
        pltpu.make_async_copy(source, target, load_sem.at[k])
        for k, (source, target) in enumerate((
            (grp_hbm, grp_ref), (off_hbm, off_ref), (lim_hbm, lim_ref),
            (img_hbm, pkt.at[me, :, pl.ds(0, full)]),
            (ctf_hbm, ctf_ref), (noise_hbm, noise_ref), (proj_hbm, proj_ref),
        ))
    ]
    for load in loads:
        load.start()

    barrier = pltpu.get_barrier_semaphore()
    for step in range(1, n):
        pl.semaphore_signal(barrier, inc=1, device_id={"blk": (me + step) % n})

    sub = lax.broadcasted_iota(jnp.int32, (own_rows, LANES), 0)
    lane = lax.broadcasted_iota(jnp.int32, (own_rows, LANES), 1)
    for load in loads[:3]:
        load.wait()
    meta = jnp.zeros((own_rows, LANES), jnp.float32)
    for p in range(own_rows):
        entries = [off_ref[p, j, s] for s in range(shifts) for j in range(2)]
        entries += [grp_ref[p], lim_ref[p]]
        for column, entry in enumerate(entries):
            meta = jnp.where((sub == p) & (lane == column), entry.astype(jnp.float32), meta)
    pkt[me, :, full:] = meta.astype(jnp.bfloat16)
    loads[3].wait()

    pl.semaphore_wait(barrier, n - 1)

    sends = []

    def send(slot, target):
        copy = pltpu.make_async_remote_copy(
            src_ref=pkt.at[slot], dst_ref=pkt.at[slot],
            send_sem=send_sem.at[len(sends)], recv_sem=recv_sem.at[slot],
            device_id={"blk": target},
        )
        copy.start()
        sends.append(copy)

    def arrived(slot):
        pltpu.make_async_remote_copy(
            src_ref=pkt.at[slot], dst_ref=pkt.at[slot],
            send_sem=send_sem.at[0], recv_sem=recv_sem.at[slot],
            device_id={"blk": (me + 1) % n},
        ).wait_recv()

    other = me + 1 - 2 * core
    for j in range(1, na):
        send(me, at((a + j) % na, b, core))
    for k in range(1, nb):
        send(me, at(a, (b + k) % nb, core))
    send(me, other)

    plane = 2 * nb * own_rows

    def widen(pa):
        at_rows = pl.ds(pl.multiple_of(pa * plane, plane), plane)
        image[at_rows, :] = jnp.concatenate(
            [pkt[pa * nb * 2 + d].astype(jnp.float32) for d in range(2 * nb)], axis=0)

    for which, ref in enumerate((ctf_ref, noise_ref)):
        loads[4 + which].wait()
        for part, value in enumerate(three_parts(ref[...])):
            tabs[part * groups:(part + 1) * groups, which * half_width:(which + 1) * half_width] = value
    loads[6].wait()
    proj_rows = proj_ref.shape[1]
    for batch in range(proj_ref.shape[0]):
        real = proj_ref[batch, :, :half_width].astype(jnp.float32)
        imag = proj_ref[batch, :, half_width:].astype(jnp.float32)
        power[batch * proj_rows:(batch + 1) * proj_rows, :] = real * real + imag * imag

    for j in range(1, na):
        slot = at((a + na - j) % na, b, core)
        arrived(slot)
        for k in range(1, nb):
            send(slot, at(a, (b + k) % nb, core))
        send(slot, other)
    for k in range(1, nb):
        for j in range(na):
            slot = at((a + na - j) % na, (b + nb - k) % nb, core)
            arrived(slot)
            send(slot, other)
    for j in range(na):
        pa = (a + na - j) % na
        for k in range(nb):
            arrived(at(pa, (b + nb - k) % nb, 1 - core))
        widen(pa)

    lane = lax.broadcasted_iota(jnp.int32, (rows, LANES), 1)
    sub = lax.broadcasted_iota(jnp.int32, (rows, LANES), 0)
    side = lane // KY
    freq_y = lane % KY - KY // 2
    side_f, freq_yf = side.astype(jnp.float32), freq_y.astype(jnp.float32)
    meta = image[:, full:]

    def column(j):
        return jnp.broadcast_to(meta[:, j:j + 1], (rows, LANES))

    middle = TILE_KX * (tiles // 2)
    for s in range(shifts):
        at_rows = slice(s * rows, (s + 1) * rows)
        off_x, off_y = column(2 * s), column(2 * s + 1)
        c0, s0 = turn_cos_sin((middle + side_f) * off_x + freq_yf * off_y)
        cd, sd = turn_cos_sin(TILE_KX * off_x)
        ec_p[at_rows, :], es_p[at_rows, :] = c0, s0
        ec_m[at_rows, :], es_m[at_rows, :] = c0 * cd + s0 * sd, s0 * cd - c0 * sd
        dc[at_rows, :], ds[at_rows, :] = cd, sd
    group_of = column(2 * shifts)[:, :3 * groups].astype(jnp.int32)
    lane_group = lax.broadcasted_iota(jnp.int32, (rows, 3 * groups), 1) % groups
    one_hot = (group_of == lane_group).astype(jnp.float32).astype(jnp.bfloat16)
    limit = column(2 * shifts + 1)
    limit_sq = limit * limit

    ctf_rows[...] = jnp.dot(one_hot, tabs[...], preferred_element_type=jnp.float32)
    chunk = 4 * LANES
    lane_chunk = lax.broadcasted_iota(jnp.int32, (rows, chunk), 1)
    chunk_x = lane_chunk // KY
    chunk_y = (lane_chunk % KY - KY // 2).astype(jnp.float32)
    limit_chunk = jnp.concatenate([limit_sq] * (chunk // LANES), axis=1)

    def weight_step(step, norm):
        re_cols = pl.ds(pl.multiple_of(step * chunk, chunk), chunk)
        im_cols = pl.ds(pl.multiple_of(half_width + step * chunk, chunk), chunk)
        x_re, x_im = image[:, re_cols], image[:, im_cols]
        c, w = ctf_rows[:, re_cols], ctf_rows[:, im_cols]
        freq_x = (chunk // KY * step + chunk_x).astype(jnp.float32)
        w = jnp.where(freq_x * freq_x + chunk_y * chunk_y < limit_chunk, w, 0.0)
        wc = w * c
        quad_w[:, re_cols] = wc * c
        image[:, re_cols], image[:, im_cols] = wc * x_re, wc * x_im
        return norm + w * (x_re * x_re + x_im * x_im)

    norm = lax.fori_loop(0, half_width // chunk, weight_step, jnp.zeros((rows, chunk), jnp.float32))
    norm = jnp.sum(norm, axis=1, keepdims=True)

    depth = 4
    for ec, es, sign in ((ec_p, es_p, 1), (ec_m, es_m, -1)):
        first = tiles // 2 if sign > 0 else tiles // 2 - 1

        @pl.loop(0, tiles // 2 // depth)
        def _(m):
            for r in range(0, rows, 16):
                cols, factors = [], []
                for q in range(depth):
                    tile = first + sign * (m * depth + q)
                    re_cols = pl.ds(pl.multiple_of(tile * LANES, LANES), LANES)
                    im_cols = pl.ds(pl.multiple_of(half_width + tile * LANES, LANES), LANES)
                    cols.append((re_cols, im_cols))
                    factors.append((image[r:r + 16, re_cols], image[r:r + 16, im_cols]))
                for s in range(shifts):
                    at_rows = slice(s * rows + r, s * rows + r + 16)
                    ck, sk, cd, sd = ec[at_rows, :], es[at_rows, :], dc[at_rows, :], ds[at_rows, :]
                    for (re_cols, im_cols), (u_re, u_im) in zip(cols, factors):
                        wbuf[at_rows, re_cols] = (u_re * ck + u_im * sk).astype(jnp.bfloat16)
                        wbuf[at_rows, im_cols] = (u_im * ck - u_re * sk).astype(jnp.bfloat16)
                        if sign > 0:
                            ck, sk = ck * cd - sk * sd, sk * cd + ck * sd
                        else:
                            ck, sk = ck * cd + sk * sd, sk * cd - ck * sd
                    ec[at_rows, :], es[at_rows, :] = ck, sk

    wide_copy = pltpu.make_async_copy(wbuf, wide_hbm, wide_sem)
    wide_copy.start()
    p_rows = jnp.concatenate([proj_ref[k] for k in range(proj_ref.shape[0])], axis=0)
    cross = lax.dot_general(
        wbuf[...], p_rows, (((1,), (1,)), ((), ())), preferred_element_type=jnp.float32)
    quad = lax.dot_general(
        quad_w[...], power[...], (((1,), (1,)), ((), ())),
        precision=lax.Precision.HIGHEST, preferred_element_type=jnp.float32)
    base = norm + quad
    scale = 0.5 / math.sqrt(half_width)
    scores = [-(base - 2.0 * cross[s * rows:(s + 1) * rows, :]) * scale for s in range(shifts)]
    top = functools.reduce(jnp.maximum, scores)
    top = jnp.max(top, axis=1, keepdims=True)
    total = sum(jnp.exp(score - top) for score in scores)
    total = jnp.sum(total, axis=1, keepdims=True)

    mid = LANES // 2
    row = jnp.where(lane == sub, top, 0.0) + jnp.where(lane == sub + mid, total, 0.0)
    stats[me] = jnp.sum(row, axis=0, keepdims=True)
    stat_copies = []
    for step in range(1, n):
        copy = pltpu.make_async_remote_copy(
            src_ref=stats.at[me], dst_ref=stats.at[me],
            send_sem=stat_send.at[step], recv_sem=stat_recv.at[me],
            device_id={"blk": (me + step) % n},
        )
        copy.start()
        stat_copies.append(copy)
    for step in range(1, n):
        slot = (me + n - step) % n
        pltpu.make_async_remote_copy(
            src_ref=stats.at[slot], dst_ref=stats.at[slot],
            send_sem=stat_send.at[step], recv_sem=stat_recv.at[slot],
            device_id={"blk": (me + step) % n},
        ).wait_recv()
    tops = jnp.concatenate([stats[d] for d in range(n)], axis=0)
    totals = pltpu.roll(tops, mid, 1)
    best = jnp.max(tops, axis=0, keepdims=True)
    all_total = jnp.sum(totals * jnp.exp(tops - best), axis=0, keepdims=True)
    log_row = best + jnp.log(all_total)
    log_total = jnp.sum(jnp.where(lane == sub, log_row, 0.0), axis=1, keepdims=True)
    best_row = jnp.exp(best - log_row)
    lane_one = lax.broadcasted_iota(jnp.int32, (1, LANES), 1)
    for k, values in enumerate((best_row, log_row)):
        picked = jnp.zeros((1, LANES), jnp.float32)
        for p in range(own_rows):
            mine = jnp.where(lane_one == me * own_rows + p, values, 0.0)
            picked = jnp.where(lane_one == p, jnp.sum(mine, axis=1, keepdims=True), picked)
        own_ref[k:k + 1, :] = picked

    posterior = jnp.concatenate([jnp.exp(score - log_total) for score in scores], axis=0)
    post_ref[...] = posterior.T.astype(jnp.bfloat16)
    wide_copy.wait()
    for copy in sends + stat_copies:
        copy.wait_send()


def fused(n, projections, images, ctf_group, shift_offsets, shell_limit, ctf_table, noise_weight):
    batches, orient, full = projections.shape
    half_width = full // 2
    own_rows, shifts = shift_offsets.shape[:2]
    rows, cand = n * own_rows, batches * orient
    na, nb = grid_sides(n)
    groups = ctf_table.shape[0]
    vmem = pl.BlockSpec(memory_space=pltpu.VMEM)
    f32, bf16 = jnp.float32, jnp.bfloat16
    table = pltpu.VMEM((shifts * rows, LANES), f32)
    posterior, wide, own = pl.pallas_call(
        functools.partial(kernel, (n, na, nb, rows, shifts, half_width)),
        out_shape=(
            jax.ShapeDtypeStruct((cand, shifts * rows), bf16),
            jax.ShapeDtypeStruct((shifts * rows, full), bf16),
            jax.ShapeDtypeStruct((2, LANES), f32),
        ),
        in_specs=[pl.BlockSpec(memory_space=pltpu.HBM)] * 7,
        out_specs=(vmem, pl.BlockSpec(memory_space=pltpu.HBM), vmem),
        scratch_shapes=[
            pltpu.VMEM(projections.shape, bf16),
            pltpu.SMEM(ctf_group.shape, jnp.int32),
            pltpu.SMEM((own_rows, 2, shifts), jnp.int32),
            pltpu.SMEM(shell_limit.shape, jnp.int32),
            pltpu.VMEM(ctf_table.shape, f32),
            pltpu.VMEM(noise_weight.shape, f32),
            pltpu.VMEM((n, own_rows, full + LANES), bf16),
            pltpu.VMEM((rows, full + LANES), f32),
            pltpu.VMEM((cand, half_width), f32),
            pltpu.VMEM((rows, half_width), f32),
            pltpu.VMEM((3 * groups, full), bf16),
            pltpu.VMEM((rows, full), f32),
            table, table, table, table, table, table,
            pltpu.VMEM((shifts * rows, full), bf16),
            pltpu.VMEM((n, 1, LANES), f32),
            pltpu.SemaphoreType.DMA((7,)),
            pltpu.SemaphoreType.DMA,
            pltpu.SemaphoreType.DMA((n,)),
            pltpu.SemaphoreType.DMA((n,)),
            pltpu.SemaphoreType.DMA((n,)),
            pltpu.SemaphoreType.DMA((n,)),
        ],
        compiler_params=pltpu.CompilerParams(
            collective_id=0, has_side_effects=True, vmem_limit_bytes=VMEM_LIMIT),
    )(projections, images, ctf_group, shift_offsets.transpose(0, 2, 1), shell_limit, ctf_table, noise_weight)
    summed = jnp.dot(posterior, wide, preferred_element_type=f32) * (cand / own_rows)
    return summed.reshape(projections.shape), own[0, :own_rows], own[1, :own_rows]


def per_device(n, *args):
    particles = n * args[1].shape[0]
    if particles > LANES // 2:
        return local(*args)
    return fused(n, *args)


def solution(mesh):
    in_specs = (
        P(None, ("groups", "blk"), None),
        P(("groups", "blk"), None),
        P(("groups", "blk")),
        P(("groups", "blk"), None, None),
        P(("groups", "blk")),
        P("groups", None),
        P("groups", None),
    )
    out_specs = (P(None, ("groups", "blk"), None), P(("groups", "blk")), P(("groups", "blk")))
    return jax.shard_map(
        functools.partial(per_device, mesh.shape["blk"]),
        mesh=mesh, in_specs=in_specs, out_specs=out_specs, check_vma=False,
    )
```

```python
import functools
import math

import jax
import jax.numpy as jnp
from jax import lax
from jax.experimental import pallas as pl
from jax.experimental.pallas import tpu as pltpu
from jax.sharding import PartitionSpec as P

KY = 64
IMG = 256


def combined_all(value, axis, join):
    pieces = jax.tree.map(lambda part: lax.all_gather(part, axis), value)
    head = jax.tree.map(lambda part: part[0], pieces)
    tail = jax.tree.map(lambda part: part[1:], pieces)
    so_far, _ = lax.scan(lambda so_far, section: (join(so_far, section), None), head, tail)
    return so_far


def frequencies(half_width):
    positions = jnp.arange(half_width, dtype=jnp.int32)
    return (positions // KY, positions % KY - KY // 2)


def shift_factors(offsets, half_width):
    row_count = offsets.shape[0]
    shift_count = offsets.shape[1]
    row_freq = jnp.arange(half_width // KY, dtype=jnp.int32)
    col_freq = jnp.arange(KY, dtype=jnp.int32) - KY // 2
    turns_x = row_freq[None, None, :] * offsets[:, :, 0:1] % IMG
    turns_y = col_freq[None, None, :] * offsets[:, :, 1:2] % IMG
    angle_x = turns_x.astype(jnp.float32) * (2.0 * math.pi / IMG)
    angle_y = turns_y.astype(jnp.float32) * (2.0 * math.pi / IMG)
    cosine_x = jnp.cos(angle_x)[:, :, :, None]
    sine_x = jnp.sin(angle_x)[:, :, :, None]
    cosine_y = jnp.cos(angle_y)[:, :, None, :]
    sine_y = jnp.sin(angle_y)[:, :, None, :]
    cosine = cosine_x * cosine_y - sine_x * sine_y
    sine_part = sine_x * cosine_y + cosine_x * sine_y
    return (
        cosine.reshape(row_count, shift_count, half_width),
        sine_part.reshape(row_count, shift_count, half_width),
    )


def particle_terms(image_rows, ctf_rows, weight_rows, offsets, limits, freq_x, freq_y):
    half_width = image_rows.shape[1] // 2
    image_real = image_rows[:, :half_width].astype(jnp.float32)
    image_imag = image_rows[:, half_width:].astype(jnp.float32)
    radius_sq = freq_x * freq_x + freq_y * freq_y
    inside = (radius_sq[None, :] < (limits * limits)[:, None]).astype(jnp.float32)
    masked_weight = inside * weight_rows
    ctf_weight = masked_weight * ctf_rows
    norm_term = jnp.sum(masked_weight * (image_real * image_real + image_imag * image_imag), axis=1)
    quad_weight = ctf_weight * ctf_rows
    cosine, sine_part = shift_factors(offsets, half_width)
    shift_real = image_real[:, None, :] * cosine + image_imag[:, None, :] * sine_part
    shift_imag = image_imag[:, None, :] * cosine - image_real[:, None, :] * sine_part
    weighted = jnp.concatenate(
        [ctf_weight[:, None, :] * shift_real, ctf_weight[:, None, :] * shift_imag], axis=2
    ).astype(jnp.bfloat16)
    return (weighted, norm_term, quad_weight)


def combine_lse(first, second):
    score_top = jnp.maximum(first[0], second[0])
    exp_total = first[1] * jnp.exp(first[0] - score_top) + second[1] * jnp.exp(
        second[0] - score_top
    )
    return (score_top, exp_total)


def block_shape(row_count):
    return 64 if row_count % 64 == 0 else row_count


def split_rows(members, block_rows):
    return tuple(
        (
            member.reshape((member.shape[0] // block_rows, block_rows) + member.shape[1:])
            for member in members
        )
    )


def local(projections, images, ctf_group, shift_offsets, shell_limit, ctf_table, noise_weight):
    batch_count, orient_dev, full_width = projections.shape
    half_width = full_width // 2
    candidates = batch_count * orient_dev
    flat_proj = projections.reshape(candidates, full_width)
    proj_real = flat_proj[:, :half_width].astype(jnp.float32)
    proj_imag = flat_proj[:, half_width:].astype(jnp.float32)
    proj_power = proj_real * proj_real + proj_imag * proj_imag
    freq_x, freq_y = frequencies(half_width)
    score_scale = 0.5 / math.sqrt(half_width)
    group_count = ctf_table.shape[0]
    particles_dev = images.shape[0]

    def block_terms(members):
        image_rows, groups, offsets, limits = members
        one_hot = (groups[:, None] == jnp.arange(group_count, dtype=jnp.int32)[None, :]).astype(
            jnp.float32
        )
        ctf_rows = jnp.dot(
            one_hot, ctf_table, precision=lax.Precision.HIGHEST, preferred_element_type=jnp.float32
        )
        weight_rows = jnp.dot(
            one_hot,
            noise_weight,
            precision=lax.Precision.HIGHEST,
            preferred_element_type=jnp.float32,
        )
        return particle_terms(image_rows, ctf_rows, weight_rows, offsets, limits, freq_x, freq_y)

    def score_block(members):
        weighted, norm_term, quad_weight = block_terms(members)
        cross_term = lax.dot_general(
            weighted, flat_proj, (((2,), (1,)), ((), ())), preferred_element_type=jnp.float32
        )
        quad_term = lax.dot_general(
            quad_weight,
            proj_power,
            (((1,), (1,)), ((), ())),
            precision=lax.Precision.HIGHEST,
            preferred_element_type=jnp.float32,
        )
        return -(norm_term[:, None, None] - 2.0 * cross_term + quad_term[:, None, :]) * score_scale

    members = (
        lax.all_gather(images, "blk", axis=0, tiled=True),
        lax.all_gather(ctf_group, "blk", axis=0, tiled=True),
        lax.all_gather(shift_offsets, "blk", axis=0, tiled=True),
        lax.all_gather(shell_limit, "blk", axis=0, tiled=True),
    )
    row_count = members[0].shape[0]
    block_rows = block_shape(row_count)
    blocks = lax.map(score_block, split_rows(members, block_rows))
    scores = blocks.reshape((row_count,) + blocks.shape[2:])
    local_top = jnp.max(scores, axis=(1, 2))
    local_total = jnp.sum(jnp.exp(scores - local_top[:, None, None]), axis=(1, 2))
    score_top, exp_total = combined_all((local_top, local_total), "blk", combine_lse)
    log_total = score_top + jnp.log(exp_total)
    pieces = (
        lax.all_gather(images, "blk", axis=0, tiled=True),
        lax.all_gather(ctf_group, "blk", axis=0, tiled=True),
        lax.all_gather(shift_offsets, "blk", axis=0, tiled=True),
        lax.all_gather(shell_limit, "blk", axis=0, tiled=True),
    )
    row_count = pieces[0].shape[0]
    block_rows = block_shape(row_count)

    def add_block(carry, packed):
        member_block, score_block_values, log_block = packed
        weighted = block_terms(member_block)[0]
        posterior = jnp.exp(score_block_values - log_block[:, None, None]).astype(jnp.bfloat16)
        contrib = lax.dot_general(
            posterior, weighted, (((0, 1), (0, 1)), ((), ())), preferred_element_type=jnp.float32
        )
        return (carry + contrib, None)

    zero_slices = jnp.zeros((candidates, full_width), jnp.float32)
    packed_scores = split_rows((scores, log_total), block_rows)
    summed, unused_out = lax.scan(
        add_block, zero_slices, (split_rows(pieces, block_rows), packed_scores[0], packed_scores[1])
    )
    slices = (summed * (candidates / particles_dev)).reshape(batch_count, orient_dev, full_width)
    own_start = lax.axis_index("blk") * particles_dev
    own_top = lax.dynamic_slice_in_dim(score_top, own_start, particles_dev, 0)
    own_log = lax.dynamic_slice_in_dim(log_total, own_start, particles_dev, 0)
    best_posterior = jnp.exp(own_top - own_log)
    return (slices, best_posterior, own_log)


LANES = 128
TILE_KX = LANES // KY
VMEM_LIMIT = 54 * 1024 * 1024


def turn_cos_sin(turns):
    turns = turns - IMG * jnp.floor(turns * (1.0 / IMG) + 0.5)
    half = turns * (math.pi / IMG)
    sq = half * half
    sin_poly = 1.0 / math.factorial(13)
    for power in (11, 9, 7, 5, 3, 1):
        sin_poly = sin_poly * sq + (-1.0) ** (power // 2) / math.factorial(power)
    cos_poly = 1.0 / math.factorial(14) * -1.0
    for power in (12, 10, 8, 6, 4, 2, 0):
        cos_poly = cos_poly * sq + (-1.0) ** (power // 2) / math.factorial(power)
    sin_half = sin_poly * half
    return 1.0 - 2.0 * sin_half * sin_half, 2.0 * sin_half * cos_poly


def three_parts(values):
    first = values.astype(jnp.bfloat16)
    rest = values - first.astype(jnp.float32)
    second = rest.astype(jnp.bfloat16)
    third = (rest - second.astype(jnp.float32)).astype(jnp.bfloat16)
    return first, second, third


def grid_sides(device_count):
    chips = device_count // 2
    outer = 2 ** ((chips.bit_length()) // 2)
    return outer, chips // outer


def kernel(
    sizes,
    proj_hbm, img_hbm, grp_hbm, off_hbm, lim_hbm, ctf_hbm, noise_hbm,
    out_ref, own_ref,
    proj_ref, grp_ref, off_ref, lim_ref, ctf_ref, noise_ref,
    pkt, image, power, quad_w, tabs, ctf_rows, ec_p, es_p, ec_m, es_m, dc, ds, wbuf, stats,
    load_sem, send_sem, recv_sem, stat_send, stat_recv,
):
    n, na, nb, rows, shifts, half_width = sizes
    own_rows = rows // n
    full = 2 * half_width
    tiles = half_width // LANES
    groups = ctf_ref.shape[0]
    me = lax.axis_index("blk")
    core = me % 2
    chip = me // 2
    a, b = chip // nb, chip % nb

    def at(pa, pb, pc):
        return (pa * nb + pb) * 2 + pc

    loads = [
        pltpu.make_async_copy(source, target, load_sem.at[k])
        for k, (source, target) in enumerate((
            (grp_hbm, grp_ref), (off_hbm, off_ref), (lim_hbm, lim_ref),
            (img_hbm, pkt.at[me, :, pl.ds(0, full)]),
            (ctf_hbm, ctf_ref), (noise_hbm, noise_ref), (proj_hbm, proj_ref),
        ))
    ]
    for load in loads:
        load.start()

    barrier = pltpu.get_barrier_semaphore()
    for step in range(1, n):
        pl.semaphore_signal(barrier, inc=1, device_id={"blk": (me + step) % n})

    sub = lax.broadcasted_iota(jnp.int32, (own_rows, LANES), 0)
    lane = lax.broadcasted_iota(jnp.int32, (own_rows, LANES), 1)
    for load in loads[:3]:
        load.wait()
    meta = jnp.zeros((own_rows, LANES), jnp.float32)
    for p in range(own_rows):
        entries = [off_ref[p, j, s] for s in range(shifts) for j in range(2)]
        entries += [grp_ref[p], lim_ref[p]]
        for column, entry in enumerate(entries):
            meta = jnp.where((sub == p) & (lane == column), entry.astype(jnp.float32), meta)
    pkt[me, :, full:] = meta.astype(jnp.bfloat16)
    loads[3].wait()

    pl.semaphore_wait(barrier, n - 1)

    sends = []

    def send(slot, target):
        copy = pltpu.make_async_remote_copy(
            src_ref=pkt.at[slot], dst_ref=pkt.at[slot],
            send_sem=send_sem.at[len(sends)], recv_sem=recv_sem.at[slot],
            device_id={"blk": target},
        )
        copy.start()
        sends.append(copy)

    def arrived(slot):
        pltpu.make_async_remote_copy(
            src_ref=pkt.at[slot], dst_ref=pkt.at[slot],
            send_sem=send_sem.at[0], recv_sem=recv_sem.at[slot],
            device_id={"blk": (me + 1) % n},
        ).wait_recv()

    other = me + 1 - 2 * core
    for j in range(1, na):
        send(me, at((a + j) % na, b, core))
    for k in range(1, nb):
        send(me, at(a, (b + k) % nb, core))
    send(me, other)

    plane = 2 * nb * own_rows

    def widen(pa):
        at_rows = pl.ds(pl.multiple_of(pa * plane, plane), plane)
        image[at_rows, :] = jnp.concatenate(
            [pkt[pa * nb * 2 + d].astype(jnp.float32) for d in range(2 * nb)], axis=0)

    for which, ref in enumerate((ctf_ref, noise_ref)):
        loads[4 + which].wait()
        for part, value in enumerate(three_parts(ref[...])):
            tabs[part * groups:(part + 1) * groups, which * half_width:(which + 1) * half_width] = value
    loads[6].wait()
    proj_rows = proj_ref.shape[1]
    for batch in range(proj_ref.shape[0]):
        real = proj_ref[batch, :, :half_width].astype(jnp.float32)
        imag = proj_ref[batch, :, half_width:].astype(jnp.float32)
        for part, value in enumerate(three_parts(real * real + imag * imag)):
            power[part, batch * proj_rows:(batch + 1) * proj_rows, :] = value

    for j in range(1, na):
        slot = at((a + na - j) % na, b, core)
        arrived(slot)
        for k in range(1, nb):
            send(slot, at(a, (b + k) % nb, core))
        send(slot, other)
    for k in range(1, nb):
        for j in range(na):
            slot = at((a + na - j) % na, (b + nb - k) % nb, core)
            arrived(slot)
            send(slot, other)
    for j in range(na):
        pa = (a + na - j) % na
        for k in range(nb):
            arrived(at(pa, (b + nb - k) % nb, 1 - core))
        widen(pa)

    lane = lax.broadcasted_iota(jnp.int32, (rows, LANES), 1)
    sub = lax.broadcasted_iota(jnp.int32, (rows, LANES), 0)
    side = lane // KY
    freq_y = lane % KY - KY // 2
    side_f, freq_yf = side.astype(jnp.float32), freq_y.astype(jnp.float32)
    meta = image[:, full:]

    def column(j):
        return jnp.broadcast_to(meta[:, j:j + 1], (rows, LANES))

    middle = TILE_KX * (tiles // 2)
    for s in range(shifts):
        at_rows = slice(s * rows, (s + 1) * rows)
        off_x, off_y = column(2 * s), column(2 * s + 1)
        c0, s0 = turn_cos_sin((middle + side_f) * off_x + freq_yf * off_y)
        cd, sd = turn_cos_sin(TILE_KX * off_x)
        ec_p[at_rows, :], es_p[at_rows, :] = c0, s0
        ec_m[at_rows, :], es_m[at_rows, :] = c0 * cd + s0 * sd, s0 * cd - c0 * sd
        dc[at_rows, :], ds[at_rows, :] = cd, sd
    group_of = column(2 * shifts)[:, :3 * groups].astype(jnp.int32)
    lane_group = lax.broadcasted_iota(jnp.int32, (rows, 3 * groups), 1) % groups
    one_hot = (group_of == lane_group).astype(jnp.float32).astype(jnp.bfloat16)
    limit = column(2 * shifts + 1)
    limit_sq = limit * limit

    ctf_rows[...] = jnp.dot(one_hot, tabs[...], preferred_element_type=jnp.float32)
    chunk = 4 * LANES
    lane_chunk = lax.broadcasted_iota(jnp.int32, (rows, chunk), 1)
    chunk_x = lane_chunk // KY
    chunk_y = (lane_chunk % KY - KY // 2).astype(jnp.float32)
    limit_chunk = jnp.concatenate([limit_sq] * (chunk // LANES), axis=1)

    def weight_step(step, norm):
        re_cols = pl.ds(pl.multiple_of(step * chunk, chunk), chunk)
        im_cols = pl.ds(pl.multiple_of(half_width + step * chunk, chunk), chunk)
        x_re, x_im = image[:, re_cols], image[:, im_cols]
        c, w = ctf_rows[:, re_cols], ctf_rows[:, im_cols]
        freq_x = (chunk // KY * step + chunk_x).astype(jnp.float32)
        w = jnp.where(freq_x * freq_x + chunk_y * chunk_y < limit_chunk, w, 0.0)
        wc = w * c
        for part, value in enumerate(three_parts(wc * c)):
            quad_w[part * rows:(part + 1) * rows, re_cols] = value
        image[:, re_cols], image[:, im_cols] = wc * x_re, wc * x_im
        return norm + w * (x_re * x_re + x_im * x_im)

    norm = lax.fori_loop(0, half_width // chunk, weight_step, jnp.zeros((rows, chunk), jnp.float32))
    norm = jnp.sum(norm, axis=1, keepdims=True)

    depth = 4
    for ec, es, sign in ((ec_p, es_p, 1), (ec_m, es_m, -1)):
        first = tiles // 2 if sign > 0 else tiles // 2 - 1

        @pl.loop(0, tiles // 2 // depth)
        def _(m):
            for r in range(0, rows, 16):
                cols, factors = [], []
                for q in range(depth):
                    tile = first + sign * (m * depth + q)
                    re_cols = pl.ds(pl.multiple_of(tile * LANES, LANES), LANES)
                    im_cols = pl.ds(pl.multiple_of(half_width + tile * LANES, LANES), LANES)
                    cols.append((re_cols, im_cols))
                    factors.append((image[r:r + 16, re_cols], image[r:r + 16, im_cols]))
                for s in range(shifts):
                    at_rows = slice(s * rows + r, s * rows + r + 16)
                    ck, sk, cd, sd = ec[at_rows, :], es[at_rows, :], dc[at_rows, :], ds[at_rows, :]
                    for (re_cols, im_cols), (u_re, u_im) in zip(cols, factors):
                        wbuf[at_rows, re_cols] = (u_re * ck + u_im * sk).astype(jnp.bfloat16)
                        wbuf[at_rows, im_cols] = (u_im * ck - u_re * sk).astype(jnp.bfloat16)
                        if sign > 0:
                            ck, sk = ck * cd - sk * sd, sk * cd + ck * sd
                        else:
                            ck, sk = ck * cd + sk * sd, sk * cd - ck * sd
                    ec[at_rows, :], es[at_rows, :] = ck, sk

    p_rows = jnp.concatenate([proj_ref[k] for k in range(proj_ref.shape[0])], axis=0)
    cross = lax.dot_general(
        wbuf[...], p_rows, (((1,), (1,)), ((), ())), preferred_element_type=jnp.float32)
    quad = jnp.zeros((rows, power.shape[1]), jnp.float32)
    for part in range(3):
        product = lax.dot_general(
            quad_w[:(3 - part) * rows, :], power[part], (((1,), (1,)), ((), ())),
            preferred_element_type=jnp.float32)
        quad = quad + sum(product[k * rows:(k + 1) * rows] for k in reversed(range(3 - part)))
    base = norm + quad
    scale = 0.5 / math.sqrt(half_width)
    scores = [-(base - 2.0 * cross[s * rows:(s + 1) * rows, :]) * scale for s in range(shifts)]
    top = functools.reduce(jnp.maximum, scores)
    top = jnp.max(top, axis=1, keepdims=True)
    total = sum(jnp.exp(score - top) for score in scores)
    total = jnp.sum(total, axis=1, keepdims=True)

    mid = LANES // 2
    row = jnp.where(lane == sub, top, 0.0) + jnp.where(lane == sub + mid, total, 0.0)
    stats[me] = jnp.sum(row, axis=0, keepdims=True)
    stat_copies = []
    for step in range(1, n):
        copy = pltpu.make_async_remote_copy(
            src_ref=stats.at[me], dst_ref=stats.at[me],
            send_sem=stat_send.at[step], recv_sem=stat_recv.at[me],
            device_id={"blk": (me + step) % n},
        )
        copy.start()
        stat_copies.append(copy)
    for step in range(1, n):
        slot = (me + n - step) % n
        pltpu.make_async_remote_copy(
            src_ref=stats.at[slot], dst_ref=stats.at[slot],
            send_sem=stat_send.at[step], recv_sem=stat_recv.at[slot],
            device_id={"blk": (me + step) % n},
        ).wait_recv()
    tops = jnp.concatenate([stats[d] for d in range(n)], axis=0)
    totals = pltpu.roll(tops, mid, 1)
    best = jnp.max(tops, axis=0, keepdims=True)
    all_total = jnp.sum(totals * jnp.exp(tops - best), axis=0, keepdims=True)
    log_row = best + jnp.log(all_total)
    log_total = jnp.sum(jnp.where(lane == sub, log_row, 0.0), axis=1, keepdims=True)
    best_row = jnp.exp(best - log_row)
    lane_one = lax.broadcasted_iota(jnp.int32, (1, LANES), 1)
    for k, values in enumerate((best_row, log_row)):
        picked = jnp.zeros((1, LANES), jnp.float32)
        for p in range(own_rows):
            mine = jnp.where(lane_one == me * own_rows + p, values, 0.0)
            picked = jnp.where(lane_one == p, jnp.sum(mine, axis=1, keepdims=True), picked)
        own_ref[k:k + 1, :] = picked

    posterior = jnp.concatenate([jnp.exp(score - log_total) for score in scores], axis=0)
    posterior = posterior.T.astype(jnp.bfloat16)
    gain = proj_ref.shape[0] * proj_rows / own_rows

    wide = 1024

    @pl.loop(0, full // wide)
    def _(step):
        cols = pl.ds(pl.multiple_of(step * wide, wide), wide)
        part = jnp.dot(posterior, wbuf[:, cols], preferred_element_type=jnp.float32) * gain
        for k in range(proj_ref.shape[0]):
            out_ref[k, :, cols] = part[k * proj_rows:(k + 1) * proj_rows]

    for copy in sends + stat_copies:
        copy.wait_send()


def fused(n, projections, images, ctf_group, shift_offsets, shell_limit, ctf_table, noise_weight):
    batches, orient, full = projections.shape
    half_width = full // 2
    own_rows, shifts = shift_offsets.shape[:2]
    rows, cand = n * own_rows, batches * orient
    na, nb = grid_sides(n)
    groups = ctf_table.shape[0]
    vmem = pl.BlockSpec(memory_space=pltpu.VMEM)
    f32, bf16 = jnp.float32, jnp.bfloat16
    table = pltpu.VMEM((shifts * rows, LANES), f32)
    slices, own = pl.pallas_call(
        functools.partial(kernel, (n, na, nb, rows, shifts, half_width)),
        out_shape=(
            pltpu.VMEM(projections.shape, f32),
            pltpu.VMEM((2, LANES), f32),
        ),
        in_specs=[pl.BlockSpec(memory_space=pltpu.HBM)] * 7,
        out_specs=(vmem, vmem),
        scratch_shapes=[
            pltpu.VMEM(projections.shape, bf16),
            pltpu.SMEM(ctf_group.shape, jnp.int32),
            pltpu.SMEM((own_rows, 2, shifts), jnp.int32),
            pltpu.SMEM(shell_limit.shape, jnp.int32),
            pltpu.VMEM(ctf_table.shape, f32),
            pltpu.VMEM(noise_weight.shape, f32),
            pltpu.VMEM((n, own_rows, full + LANES), bf16),
            pltpu.VMEM((rows, full + LANES), f32),
            pltpu.VMEM((3, cand, half_width), bf16),
            pltpu.VMEM((3 * rows, half_width), bf16),
            pltpu.VMEM((3 * groups, full), bf16),
            pltpu.VMEM((rows, full), f32),
            table, table, table, table, table, table,
            pltpu.VMEM((shifts * rows, full), bf16),
            pltpu.VMEM((n, 1, LANES), f32),
            pltpu.SemaphoreType.DMA((7,)),
            pltpu.SemaphoreType.DMA((n,)),
            pltpu.SemaphoreType.DMA((n,)),
            pltpu.SemaphoreType.DMA((n,)),
            pltpu.SemaphoreType.DMA((n,)),
        ],
        compiler_params=pltpu.CompilerParams(
            collective_id=0, has_side_effects=True, vmem_limit_bytes=VMEM_LIMIT),
    )(projections, images, ctf_group, shift_offsets.transpose(0, 2, 1), shell_limit, ctf_table, noise_weight)
    return slices, own[0, :own_rows], own[1, :own_rows]


def per_device(n, *args):
    particles = n * args[1].shape[0]
    if particles > LANES // 2:
        return local(*args)
    return fused(n, *args)


def solution(mesh):
    in_specs = (
        P(None, ("groups", "blk"), None),
        P(("groups", "blk"), None),
        P(("groups", "blk")),
        P(("groups", "blk"), None, None),
        P(("groups", "blk")),
        P("groups", None),
        P("groups", None),
    )
    out_specs = (P(None, ("groups", "blk"), None), P(("groups", "blk")), P(("groups", "blk")))
    return jax.shard_map(
        functools.partial(per_device, mesh.shape["blk"]),
        mesh=mesh, in_specs=in_specs, out_specs=out_specs, check_vma=False,
    )
```

```python
import functools
import math

import jax
import jax.numpy as jnp
from jax import lax
from jax.experimental import pallas as pl
from jax.experimental.pallas import tpu as pltpu
from jax.sharding import PartitionSpec as P

KY = 64
IMG = 256


def combined_all(value, axis, join):
    pieces = jax.tree.map(lambda part: lax.all_gather(part, axis), value)
    head = jax.tree.map(lambda part: part[0], pieces)
    tail = jax.tree.map(lambda part: part[1:], pieces)
    so_far, _ = lax.scan(lambda so_far, section: (join(so_far, section), None), head, tail)
    return so_far


def frequencies(half_width):
    positions = jnp.arange(half_width, dtype=jnp.int32)
    return (positions // KY, positions % KY - KY // 2)


def shift_factors(offsets, half_width):
    row_count = offsets.shape[0]
    shift_count = offsets.shape[1]
    row_freq = jnp.arange(half_width // KY, dtype=jnp.int32)
    col_freq = jnp.arange(KY, dtype=jnp.int32) - KY // 2
    turns_x = row_freq[None, None, :] * offsets[:, :, 0:1] % IMG
    turns_y = col_freq[None, None, :] * offsets[:, :, 1:2] % IMG
    angle_x = turns_x.astype(jnp.float32) * (2.0 * math.pi / IMG)
    angle_y = turns_y.astype(jnp.float32) * (2.0 * math.pi / IMG)
    cosine_x = jnp.cos(angle_x)[:, :, :, None]
    sine_x = jnp.sin(angle_x)[:, :, :, None]
    cosine_y = jnp.cos(angle_y)[:, :, None, :]
    sine_y = jnp.sin(angle_y)[:, :, None, :]
    cosine = cosine_x * cosine_y - sine_x * sine_y
    sine_part = sine_x * cosine_y + cosine_x * sine_y
    return (
        cosine.reshape(row_count, shift_count, half_width),
        sine_part.reshape(row_count, shift_count, half_width),
    )


def particle_terms(image_rows, ctf_rows, weight_rows, offsets, limits, freq_x, freq_y):
    half_width = image_rows.shape[1] // 2
    image_real = image_rows[:, :half_width].astype(jnp.float32)
    image_imag = image_rows[:, half_width:].astype(jnp.float32)
    radius_sq = freq_x * freq_x + freq_y * freq_y
    inside = (radius_sq[None, :] < (limits * limits)[:, None]).astype(jnp.float32)
    masked_weight = inside * weight_rows
    ctf_weight = masked_weight * ctf_rows
    norm_term = jnp.sum(masked_weight * (image_real * image_real + image_imag * image_imag), axis=1)
    quad_weight = ctf_weight * ctf_rows
    cosine, sine_part = shift_factors(offsets, half_width)
    shift_real = image_real[:, None, :] * cosine + image_imag[:, None, :] * sine_part
    shift_imag = image_imag[:, None, :] * cosine - image_real[:, None, :] * sine_part
    weighted = jnp.concatenate(
        [ctf_weight[:, None, :] * shift_real, ctf_weight[:, None, :] * shift_imag], axis=2
    ).astype(jnp.bfloat16)
    return (weighted, norm_term, quad_weight)


def combine_lse(first, second):
    score_top = jnp.maximum(first[0], second[0])
    exp_total = first[1] * jnp.exp(first[0] - score_top) + second[1] * jnp.exp(
        second[0] - score_top
    )
    return (score_top, exp_total)


def block_shape(row_count):
    return 64 if row_count % 64 == 0 else row_count


def split_rows(members, block_rows):
    return tuple(
        (
            member.reshape((member.shape[0] // block_rows, block_rows) + member.shape[1:])
            for member in members
        )
    )


def local(projections, images, ctf_group, shift_offsets, shell_limit, ctf_table, noise_weight):
    batch_count, orient_dev, full_width = projections.shape
    half_width = full_width // 2
    candidates = batch_count * orient_dev
    flat_proj = projections.reshape(candidates, full_width)
    proj_real = flat_proj[:, :half_width].astype(jnp.float32)
    proj_imag = flat_proj[:, half_width:].astype(jnp.float32)
    proj_power = proj_real * proj_real + proj_imag * proj_imag
    freq_x, freq_y = frequencies(half_width)
    score_scale = 0.5 / math.sqrt(half_width)
    group_count = ctf_table.shape[0]
    particles_dev = images.shape[0]

    def block_terms(members):
        image_rows, groups, offsets, limits = members
        one_hot = (groups[:, None] == jnp.arange(group_count, dtype=jnp.int32)[None, :]).astype(
            jnp.float32
        )
        ctf_rows = jnp.dot(
            one_hot, ctf_table, precision=lax.Precision.HIGHEST, preferred_element_type=jnp.float32
        )
        weight_rows = jnp.dot(
            one_hot,
            noise_weight,
            precision=lax.Precision.HIGHEST,
            preferred_element_type=jnp.float32,
        )
        return particle_terms(image_rows, ctf_rows, weight_rows, offsets, limits, freq_x, freq_y)

    def score_block(members):
        weighted, norm_term, quad_weight = block_terms(members)
        cross_term = lax.dot_general(
            weighted, flat_proj, (((2,), (1,)), ((), ())), preferred_element_type=jnp.float32
        )
        quad_term = lax.dot_general(
            quad_weight,
            proj_power,
            (((1,), (1,)), ((), ())),
            precision=lax.Precision.HIGHEST,
            preferred_element_type=jnp.float32,
        )
        return -(norm_term[:, None, None] - 2.0 * cross_term + quad_term[:, None, :]) * score_scale

    members = (
        lax.all_gather(images, "blk", axis=0, tiled=True),
        lax.all_gather(ctf_group, "blk", axis=0, tiled=True),
        lax.all_gather(shift_offsets, "blk", axis=0, tiled=True),
        lax.all_gather(shell_limit, "blk", axis=0, tiled=True),
    )
    row_count = members[0].shape[0]
    block_rows = block_shape(row_count)
    blocks = lax.map(score_block, split_rows(members, block_rows))
    scores = blocks.reshape((row_count,) + blocks.shape[2:])
    local_top = jnp.max(scores, axis=(1, 2))
    local_total = jnp.sum(jnp.exp(scores - local_top[:, None, None]), axis=(1, 2))
    score_top, exp_total = combined_all((local_top, local_total), "blk", combine_lse)
    log_total = score_top + jnp.log(exp_total)
    pieces = (
        lax.all_gather(images, "blk", axis=0, tiled=True),
        lax.all_gather(ctf_group, "blk", axis=0, tiled=True),
        lax.all_gather(shift_offsets, "blk", axis=0, tiled=True),
        lax.all_gather(shell_limit, "blk", axis=0, tiled=True),
    )
    row_count = pieces[0].shape[0]
    block_rows = block_shape(row_count)

    def add_block(carry, packed):
        member_block, score_block_values, log_block = packed
        weighted = block_terms(member_block)[0]
        posterior = jnp.exp(score_block_values - log_block[:, None, None]).astype(jnp.bfloat16)
        contrib = lax.dot_general(
            posterior, weighted, (((0, 1), (0, 1)), ((), ())), preferred_element_type=jnp.float32
        )
        return (carry + contrib, None)

    zero_slices = jnp.zeros((candidates, full_width), jnp.float32)
    packed_scores = split_rows((scores, log_total), block_rows)
    summed, unused_out = lax.scan(
        add_block, zero_slices, (split_rows(pieces, block_rows), packed_scores[0], packed_scores[1])
    )
    slices = (summed * (candidates / particles_dev)).reshape(batch_count, orient_dev, full_width)
    own_start = lax.axis_index("blk") * particles_dev
    own_top = lax.dynamic_slice_in_dim(score_top, own_start, particles_dev, 0)
    own_log = lax.dynamic_slice_in_dim(log_total, own_start, particles_dev, 0)
    best_posterior = jnp.exp(own_top - own_log)
    return (slices, best_posterior, own_log)


LANES = 128
TILE_KX = LANES // KY
BLOCK = 16
VMEM_LIMIT = 54 * 1024 * 1024


def turn_cos_sin(turns):
    turns = turns - IMG * jnp.floor(turns * (1.0 / IMG) + 0.5)
    half = turns * (math.pi / IMG)
    sq = half * half
    sin_poly = 1.0 / math.factorial(13)
    for power in (11, 9, 7, 5, 3, 1):
        sin_poly = sin_poly * sq + (-1.0) ** (power // 2) / math.factorial(power)
    cos_poly = 1.0 / math.factorial(14) * -1.0
    for power in (12, 10, 8, 6, 4, 2, 0):
        cos_poly = cos_poly * sq + (-1.0) ** (power // 2) / math.factorial(power)
    sin_half = sin_poly * half
    return 1.0 - 2.0 * sin_half * sin_half, 2.0 * sin_half * cos_poly


def three_parts(values):
    first = values.astype(jnp.bfloat16)
    rest = values - first.astype(jnp.float32)
    second = rest.astype(jnp.bfloat16)
    third = (rest - second.astype(jnp.float32)).astype(jnp.bfloat16)
    return first, second, third


def grid_sides(device_count):
    chips = device_count // 2
    outer = 2 ** ((chips.bit_length()) // 2)
    return outer, chips // outer


def kernel(
    sizes,
    proj_hbm, img_hbm, grp_hbm, off_hbm, lim_hbm, ctf_hbm, noise_hbm,
    out_ref, own_ref,
    proj_ref, grp_ref, off_ref, lim_ref, ctf_ref, noise_ref,
    pkt, image, power, quad_w, tabs, ctf_rows, ec_p, es_p, ec_m, es_m, dc, ds, wbuf, stage, cross, stats,
    load_sem, send_sem, recv_sem, stat_send, stat_recv,
):
    n, na, nb, rows, shifts, half_width = sizes
    own_rows = rows // n
    full = 2 * half_width
    tiles = half_width // LANES
    groups = ctf_ref.shape[0]
    me = lax.axis_index("blk")
    core = me % 2
    chip = me // 2
    a, b = chip // nb, chip % nb

    def at(pa, pb, pc):
        return (pa * nb + pb) * 2 + pc

    loads = [
        pltpu.make_async_copy(source, target, load_sem.at[k])
        for k, (source, target) in enumerate((
            (grp_hbm, grp_ref), (off_hbm, off_ref), (lim_hbm, lim_ref),
            (img_hbm, pkt.at[me, :, pl.ds(0, full)]),
            (ctf_hbm, ctf_ref), (noise_hbm, noise_ref), (proj_hbm, proj_ref),
        ))
    ]
    for load in loads:
        load.start()

    barrier = pltpu.get_barrier_semaphore()
    for step in range(1, n):
        pl.semaphore_signal(barrier, inc=1, device_id={"blk": (me + step) % n})

    sub = lax.broadcasted_iota(jnp.int32, (own_rows, LANES), 0)
    lane = lax.broadcasted_iota(jnp.int32, (own_rows, LANES), 1)
    for load in loads[:3]:
        load.wait()
    meta = jnp.zeros((own_rows, LANES), jnp.float32)
    for p in range(own_rows):
        entries = [off_ref[p, j, s] for s in range(shifts) for j in range(2)]
        entries += [grp_ref[p], lim_ref[p]]
        for column, entry in enumerate(entries):
            meta = jnp.where((sub == p) & (lane == column), entry.astype(jnp.float32), meta)
    pkt[me, :, full:] = meta.astype(jnp.bfloat16)
    loads[3].wait()

    pl.semaphore_wait(barrier, n - 1)

    sends = []

    def send(slot, target):
        copy = pltpu.make_async_remote_copy(
            src_ref=pkt.at[slot], dst_ref=pkt.at[slot],
            send_sem=send_sem.at[len(sends)], recv_sem=recv_sem.at[slot],
            device_id={"blk": target},
        )
        copy.start()
        sends.append(copy)

    def arrived(slot):
        pltpu.make_async_remote_copy(
            src_ref=pkt.at[slot], dst_ref=pkt.at[slot],
            send_sem=send_sem.at[0], recv_sem=recv_sem.at[slot],
            device_id={"blk": (me + 1) % n},
        ).wait_recv()

    other = me + 1 - 2 * core
    for j in range(1, na):
        send(me, at((a + j) % na, b, core))
    for k in range(1, nb):
        send(me, at(a, (b + k) % nb, core))
    send(me, other)

    plane = 2 * nb * own_rows

    def widen(pa):
        at_rows = pl.ds(pl.multiple_of(pa * plane, plane), plane)
        image[at_rows, :] = jnp.concatenate(
            [pkt[pa * nb * 2 + d].astype(jnp.float32) for d in range(2 * nb)], axis=0)

    for which, ref in enumerate((ctf_ref, noise_ref)):
        loads[4 + which].wait()
        for part, value in enumerate(three_parts(ref[...])):
            tabs[part * groups:(part + 1) * groups, which * half_width:(which + 1) * half_width] = value
    loads[6].wait()
    proj_rows = proj_ref.shape[1]
    for batch in range(proj_ref.shape[0]):
        real = proj_ref[batch, :, :half_width].astype(jnp.float32)
        imag = proj_ref[batch, :, half_width:].astype(jnp.float32)
        for part, value in enumerate(three_parts(real * real + imag * imag)):
            power[part, batch * proj_rows:(batch + 1) * proj_rows, :] = value

    for j in range(1, na):
        slot = at((a + na - j) % na, b, core)
        arrived(slot)
        for k in range(1, nb):
            send(slot, at(a, (b + k) % nb, core))
        send(slot, other)
    for k in range(1, nb):
        for j in range(na):
            slot = at((a + na - j) % na, (b + nb - k) % nb, core)
            arrived(slot)
            send(slot, other)
    for j in range(na):
        pa = (a + na - j) % na
        for k in range(nb):
            arrived(at(pa, (b + nb - k) % nb, 1 - core))
        widen(pa)

    lane = lax.broadcasted_iota(jnp.int32, (rows, LANES), 1)
    sub = lax.broadcasted_iota(jnp.int32, (rows, LANES), 0)
    side = lane // KY
    freq_y = lane % KY - KY // 2
    side_f, freq_yf = side.astype(jnp.float32), freq_y.astype(jnp.float32)
    meta = image[:, full:]

    def column(j):
        return jnp.broadcast_to(meta[:, j:j + 1], (rows, LANES))

    middle = TILE_KX * (tiles // 2)
    for s in range(shifts):
        at_rows = slice(s * rows, (s + 1) * rows)
        off_x, off_y = column(2 * s), column(2 * s + 1)
        c0, s0 = turn_cos_sin((middle + side_f) * off_x + freq_yf * off_y)
        cd, sd = turn_cos_sin(TILE_KX * off_x)
        ec_p[at_rows, :], es_p[at_rows, :] = c0, s0
        ec_m[at_rows, :], es_m[at_rows, :] = c0 * cd + s0 * sd, s0 * cd - c0 * sd
        dc[at_rows, :], ds[at_rows, :] = cd, sd
    group_of = column(2 * shifts)[:, :3 * groups].astype(jnp.int32)
    lane_group = lax.broadcasted_iota(jnp.int32, (rows, 3 * groups), 1) % groups
    one_hot = (group_of == lane_group).astype(jnp.float32).astype(jnp.bfloat16)
    limit = column(2 * shifts + 1)
    limit_sq = limit * limit

    ctf_rows[...] = jnp.dot(one_hot, tabs[...], preferred_element_type=jnp.float32)
    chunk = 4 * LANES
    lane_chunk = lax.broadcasted_iota(jnp.int32, (rows, chunk), 1)
    chunk_x = lane_chunk // KY
    chunk_y = (lane_chunk % KY - KY // 2).astype(jnp.float32)
    limit_chunk = jnp.concatenate([limit_sq] * (chunk // LANES), axis=1)

    def weight_step(step, norm):
        re_cols = pl.ds(pl.multiple_of(step * chunk, chunk), chunk)
        im_cols = pl.ds(pl.multiple_of(half_width + step * chunk, chunk), chunk)
        x_re, x_im = image[:, re_cols], image[:, im_cols]
        c, w = ctf_rows[:, re_cols], ctf_rows[:, im_cols]
        freq_x = (chunk // KY * step + chunk_x).astype(jnp.float32)
        w = jnp.where(freq_x * freq_x + chunk_y * chunk_y < limit_chunk, w, 0.0)
        wc = w * c
        for part, value in enumerate(three_parts(wc * c)):
            quad_w[part * rows:(part + 1) * rows, re_cols] = value
        image[:, re_cols], image[:, im_cols] = wc * x_re, wc * x_im
        return norm + w * (x_re * x_re + x_im * x_im)

    norm = lax.fori_loop(0, half_width // chunk, weight_step, jnp.zeros((rows, chunk), jnp.float32))
    norm = jnp.sum(norm, axis=1, keepdims=True)

    depth = 4
    span = depth * LANES
    blocks = rows // BLOCK
    cross[...] = jnp.zeros_like(cross)

    def meet(block, base):
        total = cross[block]
        for k, start in enumerate((0, half_width)):
            cols = pl.ds(pl.multiple_of(start + base * LANES, span), span)
            p_cols = jnp.concatenate([proj_ref[batch, :, cols] for batch in range(proj_ref.shape[0])], axis=0)
            total = total + lax.dot_general(
                stage[block, :, k * span:(k + 1) * span], p_cols, (((1,), (1,)), ((), ())),
                preferred_element_type=jnp.float32)
        cross[block] = total

    for ec, es, sign in ((ec_p, es_p, 1), (ec_m, es_m, -1)):
        first = tiles // 2 if sign > 0 else tiles // 2 - depth
        steps = tiles // 2 // depth
        stage[blocks - 1] = jnp.zeros(stage.shape[1:], jnp.bfloat16)

        @pl.loop(0, steps)
        def _(m):
            base = first + sign * depth * m
            base_before = first + sign * depth * jnp.maximum(m - 1, 0)
            for block in range(blocks):
                if block == 0:
                    meet(blocks - 1, base_before)
                else:
                    meet(block - 1, base)
                r = block * BLOCK
                order = range(depth) if sign > 0 else range(depth - 1, -1, -1)
                cols, factors = [], []
                for q in order:
                    tile = base + q
                    re_cols = pl.ds(pl.multiple_of(tile * LANES, LANES), LANES)
                    im_cols = pl.ds(pl.multiple_of(half_width + tile * LANES, LANES), LANES)
                    cols.append((q, re_cols, im_cols))
                    factors.append((image[r:r + BLOCK, re_cols], image[r:r + BLOCK, im_cols]))
                for s in range(shifts):
                    at_rows = slice(s * rows + r, s * rows + r + BLOCK)
                    in_stage = slice(s * BLOCK, (s + 1) * BLOCK)
                    ck, sk, cd, sd = ec[at_rows, :], es[at_rows, :], dc[at_rows, :], ds[at_rows, :]
                    for (q, re_cols, im_cols), (u_re, u_im) in zip(cols, factors):
                        y_re = (u_re * ck + u_im * sk).astype(jnp.bfloat16)
                        y_im = (u_im * ck - u_re * sk).astype(jnp.bfloat16)
                        wbuf[at_rows, re_cols], wbuf[at_rows, im_cols] = y_re, y_im
                        stage[block, in_stage, q * LANES:(q + 1) * LANES] = y_re
                        stage[block, in_stage, span + q * LANES:span + (q + 1) * LANES] = y_im
                        if sign > 0:
                            ck, sk = ck * cd - sk * sd, sk * cd + ck * sd
                        else:
                            ck, sk = ck * cd + sk * sd, sk * cd - ck * sd
                    ec[at_rows, :], es[at_rows, :] = ck, sk

        meet(blocks - 1, first + sign * depth * (steps - 1))

    quad = jnp.zeros((rows, power.shape[1]), jnp.float32)
    for part in range(3):
        product = lax.dot_general(
            quad_w[:(3 - part) * rows, :], power[part], (((1,), (1,)), ((), ())),
            preferred_element_type=jnp.float32)
        quad = quad + sum(product[k * rows:(k + 1) * rows] for k in reversed(range(3 - part)))
    base = norm + quad
    scale = 0.5 / math.sqrt(half_width)
    crosses = [
        jnp.concatenate([cross[block, s * BLOCK:(s + 1) * BLOCK, :] for block in range(blocks)], axis=0)
        for s in range(shifts)
    ]
    scores = [-(base - 2.0 * part) * scale for part in crosses]
    top = functools.reduce(jnp.maximum, scores)
    top = jnp.max(top, axis=1, keepdims=True)
    total = sum(jnp.exp(score - top) for score in scores)
    total = jnp.sum(total, axis=1, keepdims=True)

    mid = LANES // 2
    row = jnp.where(lane == sub, top, 0.0) + jnp.where(lane == sub + mid, total, 0.0)
    stats[me] = jnp.sum(row, axis=0, keepdims=True)
    stat_copies = []
    for step in range(1, n):
        copy = pltpu.make_async_remote_copy(
            src_ref=stats.at[me], dst_ref=stats.at[me],
            send_sem=stat_send.at[step], recv_sem=stat_recv.at[me],
            device_id={"blk": (me + step) % n},
        )
        copy.start()
        stat_copies.append(copy)
    for step in range(1, n):
        slot = (me + n - step) % n
        pltpu.make_async_remote_copy(
            src_ref=stats.at[slot], dst_ref=stats.at[slot],
            send_sem=stat_send.at[step], recv_sem=stat_recv.at[slot],
            device_id={"blk": (me + step) % n},
        ).wait_recv()
    tops = jnp.concatenate([stats[d] for d in range(n)], axis=0)
    totals = pltpu.roll(tops, mid, 1)
    best = jnp.max(tops, axis=0, keepdims=True)
    all_total = jnp.sum(totals * jnp.exp(tops - best), axis=0, keepdims=True)
    log_row = best + jnp.log(all_total)
    log_total = jnp.sum(jnp.where(lane == sub, log_row, 0.0), axis=1, keepdims=True)
    best_row = jnp.exp(best - log_row)
    lane_one = lax.broadcasted_iota(jnp.int32, (1, LANES), 1)
    for k, values in enumerate((best_row, log_row)):
        picked = jnp.zeros((1, LANES), jnp.float32)
        for p in range(own_rows):
            mine = jnp.where(lane_one == me * own_rows + p, values, 0.0)
            picked = jnp.where(lane_one == p, jnp.sum(mine, axis=1, keepdims=True), picked)
        own_ref[k:k + 1, :] = picked

    posterior = jnp.concatenate([jnp.exp(score - log_total) for score in scores], axis=0)
    posterior = posterior.T.astype(jnp.bfloat16)
    gain = proj_ref.shape[0] * proj_rows / own_rows

    wide = 1024

    @pl.loop(0, full // wide)
    def _(step):
        cols = pl.ds(pl.multiple_of(step * wide, wide), wide)
        part = jnp.dot(posterior, wbuf[:, cols], preferred_element_type=jnp.float32) * gain
        for k in range(proj_ref.shape[0]):
            out_ref[k, :, cols] = part[k * proj_rows:(k + 1) * proj_rows]

    for copy in sends + stat_copies:
        copy.wait_send()


def fused(n, projections, images, ctf_group, shift_offsets, shell_limit, ctf_table, noise_weight):
    batches, orient, full = projections.shape
    half_width = full // 2
    own_rows, shifts = shift_offsets.shape[:2]
    rows, cand = n * own_rows, batches * orient
    na, nb = grid_sides(n)
    groups = ctf_table.shape[0]
    vmem = pl.BlockSpec(memory_space=pltpu.VMEM)
    f32, bf16 = jnp.float32, jnp.bfloat16
    table = pltpu.VMEM((shifts * rows, LANES), f32)
    slices, own = pl.pallas_call(
        functools.partial(kernel, (n, na, nb, rows, shifts, half_width)),
        out_shape=(
            pltpu.VMEM(projections.shape, f32),
            pltpu.VMEM((2, LANES), f32),
        ),
        in_specs=[pl.BlockSpec(memory_space=pltpu.HBM)] * 7,
        out_specs=(vmem, vmem),
        scratch_shapes=[
            pltpu.VMEM(projections.shape, bf16),
            pltpu.SMEM(ctf_group.shape, jnp.int32),
            pltpu.SMEM((own_rows, 2, shifts), jnp.int32),
            pltpu.SMEM(shell_limit.shape, jnp.int32),
            pltpu.VMEM(ctf_table.shape, f32),
            pltpu.VMEM(noise_weight.shape, f32),
            pltpu.VMEM((n, own_rows, full + LANES), bf16),
            pltpu.VMEM((rows, full + LANES), f32),
            pltpu.VMEM((3, cand, half_width), bf16),
            pltpu.VMEM((3 * rows, half_width), bf16),
            pltpu.VMEM((3 * groups, full), bf16),
            pltpu.VMEM((rows, full), f32),
            table, table, table, table, table, table,
            pltpu.VMEM((shifts * rows, full), bf16),
            pltpu.VMEM((rows // BLOCK, shifts * BLOCK, 8 * LANES), bf16),
            pltpu.VMEM((rows // BLOCK, shifts * BLOCK, cand), f32),
            pltpu.VMEM((n, 1, LANES), f32),
            pltpu.SemaphoreType.DMA((7,)),
            pltpu.SemaphoreType.DMA((n,)),
            pltpu.SemaphoreType.DMA((n,)),
            pltpu.SemaphoreType.DMA((n,)),
            pltpu.SemaphoreType.DMA((n,)),
        ],
        compiler_params=pltpu.CompilerParams(
            collective_id=0, has_side_effects=True, vmem_limit_bytes=VMEM_LIMIT),
    )(projections, images, ctf_group, shift_offsets.transpose(0, 2, 1), shell_limit, ctf_table, noise_weight)
    return slices, own[0, :own_rows], own[1, :own_rows]


def per_device(n, *args):
    particles = n * args[1].shape[0]
    if particles > LANES // 2 or particles % BLOCK:
        return local(*args)
    return fused(n, *args)


def solution(mesh):
    in_specs = (
        P(None, ("groups", "blk"), None),
        P(("groups", "blk"), None),
        P(("groups", "blk")),
        P(("groups", "blk"), None, None),
        P(("groups", "blk")),
        P("groups", None),
        P("groups", None),
    )
    out_specs = (P(None, ("groups", "blk"), None), P(("groups", "blk")), P(("groups", "blk")))
    return jax.shard_map(
        functools.partial(per_device, mesh.shape["blk"]),
        mesh=mesh, in_specs=in_specs, out_specs=out_specs, check_vma=False,
    )
```

```python
import functools
import math

import jax
import jax.numpy as jnp
from jax import lax
from jax.experimental import pallas as pl
from jax.experimental.pallas import tpu as pltpu
from jax.sharding import PartitionSpec as P

KY = 64
IMG = 256


def combined_all(value, axis, join):
    pieces = jax.tree.map(lambda part: lax.all_gather(part, axis), value)
    head = jax.tree.map(lambda part: part[0], pieces)
    tail = jax.tree.map(lambda part: part[1:], pieces)
    so_far, _ = lax.scan(lambda so_far, section: (join(so_far, section), None), head, tail)
    return so_far


def frequencies(half_width):
    positions = jnp.arange(half_width, dtype=jnp.int32)
    return (positions // KY, positions % KY - KY // 2)


def shift_factors(offsets, half_width):
    row_count = offsets.shape[0]
    shift_count = offsets.shape[1]
    row_freq = jnp.arange(half_width // KY, dtype=jnp.int32)
    col_freq = jnp.arange(KY, dtype=jnp.int32) - KY // 2
    turns_x = row_freq[None, None, :] * offsets[:, :, 0:1] % IMG
    turns_y = col_freq[None, None, :] * offsets[:, :, 1:2] % IMG
    angle_x = turns_x.astype(jnp.float32) * (2.0 * math.pi / IMG)
    angle_y = turns_y.astype(jnp.float32) * (2.0 * math.pi / IMG)
    cosine_x = jnp.cos(angle_x)[:, :, :, None]
    sine_x = jnp.sin(angle_x)[:, :, :, None]
    cosine_y = jnp.cos(angle_y)[:, :, None, :]
    sine_y = jnp.sin(angle_y)[:, :, None, :]
    cosine = cosine_x * cosine_y - sine_x * sine_y
    sine_part = sine_x * cosine_y + cosine_x * sine_y
    return (
        cosine.reshape(row_count, shift_count, half_width),
        sine_part.reshape(row_count, shift_count, half_width),
    )


def particle_terms(image_rows, ctf_rows, weight_rows, offsets, limits, freq_x, freq_y):
    half_width = image_rows.shape[1] // 2
    image_real = image_rows[:, :half_width].astype(jnp.float32)
    image_imag = image_rows[:, half_width:].astype(jnp.float32)
    radius_sq = freq_x * freq_x + freq_y * freq_y
    inside = (radius_sq[None, :] < (limits * limits)[:, None]).astype(jnp.float32)
    masked_weight = inside * weight_rows
    ctf_weight = masked_weight * ctf_rows
    norm_term = jnp.sum(masked_weight * (image_real * image_real + image_imag * image_imag), axis=1)
    quad_weight = ctf_weight * ctf_rows
    cosine, sine_part = shift_factors(offsets, half_width)
    shift_real = image_real[:, None, :] * cosine + image_imag[:, None, :] * sine_part
    shift_imag = image_imag[:, None, :] * cosine - image_real[:, None, :] * sine_part
    weighted = jnp.concatenate(
        [ctf_weight[:, None, :] * shift_real, ctf_weight[:, None, :] * shift_imag], axis=2
    ).astype(jnp.bfloat16)
    return (weighted, norm_term, quad_weight)


def combine_lse(first, second):
    score_top = jnp.maximum(first[0], second[0])
    exp_total = first[1] * jnp.exp(first[0] - score_top) + second[1] * jnp.exp(
        second[0] - score_top
    )
    return (score_top, exp_total)


def block_shape(row_count):
    return 64 if row_count % 64 == 0 else row_count


def split_rows(members, block_rows):
    return tuple(
        (
            member.reshape((member.shape[0] // block_rows, block_rows) + member.shape[1:])
            for member in members
        )
    )


def local(projections, images, ctf_group, shift_offsets, shell_limit, ctf_table, noise_weight):
    batch_count, orient_dev, full_width = projections.shape
    half_width = full_width // 2
    candidates = batch_count * orient_dev
    flat_proj = projections.reshape(candidates, full_width)
    proj_real = flat_proj[:, :half_width].astype(jnp.float32)
    proj_imag = flat_proj[:, half_width:].astype(jnp.float32)
    proj_power = proj_real * proj_real + proj_imag * proj_imag
    freq_x, freq_y = frequencies(half_width)
    score_scale = 0.5 / math.sqrt(half_width)
    group_count = ctf_table.shape[0]
    particles_dev = images.shape[0]

    def block_terms(members):
        image_rows, groups, offsets, limits = members
        one_hot = (groups[:, None] == jnp.arange(group_count, dtype=jnp.int32)[None, :]).astype(
            jnp.float32
        )
        ctf_rows = jnp.dot(
            one_hot, ctf_table, precision=lax.Precision.HIGHEST, preferred_element_type=jnp.float32
        )
        weight_rows = jnp.dot(
            one_hot,
            noise_weight,
            precision=lax.Precision.HIGHEST,
            preferred_element_type=jnp.float32,
        )
        return particle_terms(image_rows, ctf_rows, weight_rows, offsets, limits, freq_x, freq_y)

    def score_block(members):
        weighted, norm_term, quad_weight = block_terms(members)
        cross_term = lax.dot_general(
            weighted, flat_proj, (((2,), (1,)), ((), ())), preferred_element_type=jnp.float32
        )
        quad_term = lax.dot_general(
            quad_weight,
            proj_power,
            (((1,), (1,)), ((), ())),
            precision=lax.Precision.HIGHEST,
            preferred_element_type=jnp.float32,
        )
        return -(norm_term[:, None, None] - 2.0 * cross_term + quad_term[:, None, :]) * score_scale

    members = (
        lax.all_gather(images, "blk", axis=0, tiled=True),
        lax.all_gather(ctf_group, "blk", axis=0, tiled=True),
        lax.all_gather(shift_offsets, "blk", axis=0, tiled=True),
        lax.all_gather(shell_limit, "blk", axis=0, tiled=True),
    )
    row_count = members[0].shape[0]
    block_rows = block_shape(row_count)
    blocks = lax.map(score_block, split_rows(members, block_rows))
    scores = blocks.reshape((row_count,) + blocks.shape[2:])
    local_top = jnp.max(scores, axis=(1, 2))
    local_total = jnp.sum(jnp.exp(scores - local_top[:, None, None]), axis=(1, 2))
    score_top, exp_total = combined_all((local_top, local_total), "blk", combine_lse)
    log_total = score_top + jnp.log(exp_total)
    pieces = (
        lax.all_gather(images, "blk", axis=0, tiled=True),
        lax.all_gather(ctf_group, "blk", axis=0, tiled=True),
        lax.all_gather(shift_offsets, "blk", axis=0, tiled=True),
        lax.all_gather(shell_limit, "blk", axis=0, tiled=True),
    )
    row_count = pieces[0].shape[0]
    block_rows = block_shape(row_count)

    def add_block(carry, packed):
        member_block, score_block_values, log_block = packed
        weighted = block_terms(member_block)[0]
        posterior = jnp.exp(score_block_values - log_block[:, None, None]).astype(jnp.bfloat16)
        contrib = lax.dot_general(
            posterior, weighted, (((0, 1), (0, 1)), ((), ())), preferred_element_type=jnp.float32
        )
        return (carry + contrib, None)

    zero_slices = jnp.zeros((candidates, full_width), jnp.float32)
    packed_scores = split_rows((scores, log_total), block_rows)
    summed, unused_out = lax.scan(
        add_block, zero_slices, (split_rows(pieces, block_rows), packed_scores[0], packed_scores[1])
    )
    slices = (summed * (candidates / particles_dev)).reshape(batch_count, orient_dev, full_width)
    own_start = lax.axis_index("blk") * particles_dev
    own_top = lax.dynamic_slice_in_dim(score_top, own_start, particles_dev, 0)
    own_log = lax.dynamic_slice_in_dim(log_total, own_start, particles_dev, 0)
    best_posterior = jnp.exp(own_top - own_log)
    return (slices, best_posterior, own_log)


LANES = 128
TILE_KX = LANES // KY
VMEM_LIMIT = 54 * 1024 * 1024


def turn_cos_sin(turns):
    turns = turns - IMG * jnp.floor(turns * (1.0 / IMG) + 0.5)
    half = turns * (math.pi / IMG)
    sq = half * half
    sin_poly = 1.0 / math.factorial(13)
    for power in (11, 9, 7, 5, 3, 1):
        sin_poly = sin_poly * sq + (-1.0) ** (power // 2) / math.factorial(power)
    cos_poly = 1.0 / math.factorial(14) * -1.0
    for power in (12, 10, 8, 6, 4, 2, 0):
        cos_poly = cos_poly * sq + (-1.0) ** (power // 2) / math.factorial(power)
    sin_half = sin_poly * half
    return 1.0 - 2.0 * sin_half * sin_half, 2.0 * sin_half * cos_poly


def three_parts(values):
    first = values.astype(jnp.bfloat16)
    rest = values - first.astype(jnp.float32)
    second = rest.astype(jnp.bfloat16)
    third = (rest - second.astype(jnp.float32)).astype(jnp.bfloat16)
    return first, second, third


def grid_sides(device_count):
    chips = device_count // 2
    outer = 2 ** ((chips.bit_length()) // 2)
    return outer, chips // outer


def kernel(
    sizes,
    proj_hbm, img_hbm, grp_hbm, off_hbm, lim_hbm, ctf_hbm, noise_hbm,
    out_ref, own_ref,
    proj_ref, grp_ref, off_ref, lim_ref, ctf_ref, noise_ref,
    pkt, image, power, quad_w, tabs, ctf_rows, ec_p, es_p, ec_m, es_m, dc, ds, wbuf, stats,
    load_sem, send_sem, recv_sem, stat_send, stat_recv,
):
    n, na, nb, rows, shifts, half_width = sizes
    own_rows = rows // n
    full = 2 * half_width
    tiles = half_width // LANES
    groups = ctf_ref.shape[0]
    me = lax.axis_index("blk")
    core = me % 2
    chip = me // 2
    a, b = chip // nb, chip % nb

    def at(pa, pb, pc):
        return (pa * nb + pb) * 2 + pc

    loads = [
        pltpu.make_async_copy(source, target, load_sem.at[k])
        for k, (source, target) in enumerate((
            (grp_hbm, grp_ref), (off_hbm, off_ref), (lim_hbm, lim_ref),
            (img_hbm, pkt.at[me, :, pl.ds(0, full)]),
            (ctf_hbm, ctf_ref), (noise_hbm, noise_ref), (proj_hbm, proj_ref),
        ))
    ]
    for load in loads:
        load.start()

    barrier = pltpu.get_barrier_semaphore()
    for step in range(1, n):
        pl.semaphore_signal(barrier, inc=1, device_id={"blk": (me + step) % n})

    sub = lax.broadcasted_iota(jnp.int32, (own_rows, LANES), 0)
    lane = lax.broadcasted_iota(jnp.int32, (own_rows, LANES), 1)
    for load in loads[:3]:
        load.wait()
    meta = jnp.zeros((own_rows, LANES), jnp.float32)
    for p in range(own_rows):
        entries = [off_ref[p, j, s] for s in range(shifts) for j in range(2)]
        entries += [grp_ref[p], lim_ref[p]]
        for column, entry in enumerate(entries):
            meta = jnp.where((sub == p) & (lane == column), entry.astype(jnp.float32), meta)
    pkt[me, :, full:] = meta.astype(jnp.bfloat16)
    loads[3].wait()

    pl.semaphore_wait(barrier, n - 1)

    sends = []

    def send(slot, target):
        copy = pltpu.make_async_remote_copy(
            src_ref=pkt.at[slot], dst_ref=pkt.at[slot],
            send_sem=send_sem.at[len(sends)], recv_sem=recv_sem.at[slot],
            device_id={"blk": target},
        )
        copy.start()
        sends.append(copy)

    def arrived(slot):
        pltpu.make_async_remote_copy(
            src_ref=pkt.at[slot], dst_ref=pkt.at[slot],
            send_sem=send_sem.at[0], recv_sem=recv_sem.at[slot],
            device_id={"blk": (me + 1) % n},
        ).wait_recv()

    other = me + 1 - 2 * core
    for j in range(1, na):
        send(me, at((a + j) % na, b, core))
    for k in range(1, nb):
        send(me, at(a, (b + k) % nb, core))
    send(me, other)

    plane = 2 * nb * own_rows

    def widen(pa):
        at_rows = pl.ds(pl.multiple_of(pa * plane, plane), plane)
        image[at_rows, :] = jnp.concatenate(
            [pkt[pa * nb * 2 + d].astype(jnp.float32) for d in range(2 * nb)], axis=0)

    for which, ref in enumerate((ctf_ref, noise_ref)):
        loads[4 + which].wait()
        for part, value in enumerate(three_parts(ref[...])):
            tabs[part * groups:(part + 1) * groups, which * half_width:(which + 1) * half_width] = value
    loads[6].wait()
    proj_rows = proj_ref.shape[1]
    for batch in range(proj_ref.shape[0]):
        real = proj_ref[batch, :, :half_width].astype(jnp.float32)
        imag = proj_ref[batch, :, half_width:].astype(jnp.float32)
        for part, value in enumerate(three_parts(real * real + imag * imag)):
            power[part, batch * proj_rows:(batch + 1) * proj_rows, :] = value

    for j in range(1, na):
        slot = at((a + na - j) % na, b, core)
        arrived(slot)
        for k in range(1, nb):
            send(slot, at(a, (b + k) % nb, core))
        send(slot, other)
    for k in range(1, nb):
        for j in range(na):
            slot = at((a + na - j) % na, (b + nb - k) % nb, core)
            arrived(slot)
            send(slot, other)
    for j in range(na):
        pa = (a + na - j) % na
        for k in range(nb):
            arrived(at(pa, (b + nb - k) % nb, 1 - core))
        widen(pa)

    lane = lax.broadcasted_iota(jnp.int32, (rows, LANES), 1)
    sub = lax.broadcasted_iota(jnp.int32, (rows, LANES), 0)
    side = lane // KY
    freq_y = lane % KY - KY // 2
    side_f, freq_yf = side.astype(jnp.float32), freq_y.astype(jnp.float32)
    meta = image[:, full:]

    def column(j):
        return jnp.broadcast_to(meta[:, j:j + 1], (rows, LANES))

    turn_c, turn_s = turn_cos_sin(TILE_KX * meta)
    middle = TILE_KX * (tiles // 2)
    for s in range(shifts):
        at_rows = slice(s * rows, (s + 1) * rows)
        off_x, off_y = column(2 * s), column(2 * s + 1)
        c0, s0 = turn_cos_sin((middle + side_f) * off_x + freq_yf * off_y)
        cd = jnp.broadcast_to(turn_c[:, 2 * s:2 * s + 1], (rows, LANES))
        sd = jnp.broadcast_to(turn_s[:, 2 * s:2 * s + 1], (rows, LANES))
        ec_p[at_rows, :], es_p[at_rows, :] = c0, s0
        ec_m[at_rows, :], es_m[at_rows, :] = c0 * cd + s0 * sd, s0 * cd - c0 * sd
        dc[at_rows, :], ds[at_rows, :] = cd, sd
    group_of = column(2 * shifts)[:, :3 * groups].astype(jnp.int32)
    lane_group = lax.broadcasted_iota(jnp.int32, (rows, 3 * groups), 1) % groups
    one_hot = (group_of == lane_group).astype(jnp.float32).astype(jnp.bfloat16)
    limit = column(2 * shifts + 1)
    limit_sq = limit * limit

    ctf_rows[...] = jnp.dot(one_hot, tabs[...], preferred_element_type=jnp.float32)
    chunk = 4 * LANES
    lane_chunk = lax.broadcasted_iota(jnp.int32, (rows, chunk), 1)
    chunk_x = lane_chunk // KY
    chunk_y = (lane_chunk % KY - KY // 2).astype(jnp.float32)
    limit_chunk = jnp.concatenate([limit_sq] * (chunk // LANES), axis=1)

    def weight_step(step, norm):
        re_cols = pl.ds(pl.multiple_of(step * chunk, chunk), chunk)
        im_cols = pl.ds(pl.multiple_of(half_width + step * chunk, chunk), chunk)
        x_re, x_im = image[:, re_cols], image[:, im_cols]
        c, w = ctf_rows[:, re_cols], ctf_rows[:, im_cols]
        freq_x = (chunk // KY * step + chunk_x).astype(jnp.float32)
        w = jnp.where(freq_x * freq_x + chunk_y * chunk_y < limit_chunk, w, 0.0)
        wc = w * c
        for part, value in enumerate(three_parts(wc * c)):
            quad_w[part * rows:(part + 1) * rows, re_cols] = value
        image[:, re_cols], image[:, im_cols] = wc * x_re, wc * x_im
        return norm + w * (x_re * x_re + x_im * x_im)

    norm = lax.fori_loop(0, half_width // chunk, weight_step, jnp.zeros((rows, chunk), jnp.float32))
    norm = jnp.sum(norm, axis=1, keepdims=True)

    depth = 4
    for ec, es, sign in ((ec_p, es_p, 1), (ec_m, es_m, -1)):
        first = tiles // 2 if sign > 0 else tiles // 2 - 1

        @pl.loop(0, tiles // 2 // depth)
        def _(m):
            for r in range(0, rows, 16):
                cols, factors = [], []
                for q in range(depth):
                    tile = first + sign * (m * depth + q)
                    re_cols = pl.ds(pl.multiple_of(tile * LANES, LANES), LANES)
                    im_cols = pl.ds(pl.multiple_of(half_width + tile * LANES, LANES), LANES)
                    cols.append((re_cols, im_cols))
                    factors.append((image[r:r + 16, re_cols], image[r:r + 16, im_cols]))
                for s in range(shifts):
                    at_rows = slice(s * rows + r, s * rows + r + 16)
                    ck, sk, cd, sd = ec[at_rows, :], es[at_rows, :], dc[at_rows, :], ds[at_rows, :]
                    for (re_cols, im_cols), (u_re, u_im) in zip(cols, factors):
                        wbuf[at_rows, re_cols] = (u_re * ck + u_im * sk).astype(jnp.bfloat16)
                        wbuf[at_rows, im_cols] = (u_im * ck - u_re * sk).astype(jnp.bfloat16)
                        if sign > 0:
                            ck, sk = ck * cd - sk * sd, sk * cd + ck * sd
                        else:
                            ck, sk = ck * cd + sk * sd, sk * cd - ck * sd
                    ec[at_rows, :], es[at_rows, :] = ck, sk

    p_rows = jnp.concatenate([proj_ref[k] for k in range(proj_ref.shape[0])], axis=0)
    cross = lax.dot_general(
        wbuf[...], p_rows, (((1,), (1,)), ((), ())), preferred_element_type=jnp.float32)
    quad = jnp.zeros((rows, power.shape[1]), jnp.float32)
    for part in range(3):
        product = lax.dot_general(
            quad_w[:(3 - part) * rows, :], power[part], (((1,), (1,)), ((), ())),
            preferred_element_type=jnp.float32)
        quad = quad + sum(product[k * rows:(k + 1) * rows] for k in reversed(range(3 - part)))
    base = norm + quad
    scale = 0.5 / math.sqrt(half_width)
    scores = [-(base - 2.0 * cross[s * rows:(s + 1) * rows, :]) * scale for s in range(shifts)]
    top = functools.reduce(jnp.maximum, scores)
    top = jnp.max(top, axis=1, keepdims=True)
    total = sum(jnp.exp(score - top) for score in scores)
    total = jnp.sum(total, axis=1, keepdims=True)

    mid = LANES // 2
    row = jnp.where(lane == sub, top, 0.0) + jnp.where(lane == sub + mid, total, 0.0)
    stats[me] = jnp.sum(row, axis=0, keepdims=True)
    stat_copies = []
    for step in range(1, n):
        copy = pltpu.make_async_remote_copy(
            src_ref=stats.at[me], dst_ref=stats.at[me],
            send_sem=stat_send.at[step], recv_sem=stat_recv.at[me],
            device_id={"blk": (me + step) % n},
        )
        copy.start()
        stat_copies.append(copy)
    for step in range(1, n):
        slot = (me + n - step) % n
        pltpu.make_async_remote_copy(
            src_ref=stats.at[slot], dst_ref=stats.at[slot],
            send_sem=stat_send.at[step], recv_sem=stat_recv.at[slot],
            device_id={"blk": (me + step) % n},
        ).wait_recv()
    tops = jnp.concatenate([stats[d] for d in range(n)], axis=0)
    totals = pltpu.roll(tops, mid, 1)
    best = jnp.max(tops, axis=0, keepdims=True)
    all_total = jnp.sum(totals * jnp.exp(tops - best), axis=0, keepdims=True)
    log_row = best + jnp.log(all_total)
    log_total = jnp.sum(jnp.where(lane == sub, log_row, 0.0), axis=1, keepdims=True)
    best_row = jnp.exp(best - log_row)
    lane_one = lax.broadcasted_iota(jnp.int32, (1, LANES), 1)
    for k, values in enumerate((best_row, log_row)):
        picked = jnp.zeros((1, LANES), jnp.float32)
        for p in range(own_rows):
            mine = jnp.where(lane_one == me * own_rows + p, values, 0.0)
            picked = jnp.where(lane_one == p, jnp.sum(mine, axis=1, keepdims=True), picked)
        own_ref[k:k + 1, :] = picked

    posterior = jnp.concatenate([jnp.exp(score - log_total) for score in scores], axis=0)
    posterior = posterior.T.astype(jnp.bfloat16)
    gain = proj_ref.shape[0] * proj_rows / own_rows

    wide = 1024

    for step in range(full // wide):
        cols = slice(step * wide, (step + 1) * wide)
        part = jnp.dot(posterior, wbuf[:, cols], preferred_element_type=jnp.float32) * gain
        for k in range(proj_ref.shape[0]):
            out_ref[k, :, cols] = part[k * proj_rows:(k + 1) * proj_rows]

    for copy in sends + stat_copies:
        copy.wait_send()


def fused(n, projections, images, ctf_group, shift_offsets, shell_limit, ctf_table, noise_weight):
    batches, orient, full = projections.shape
    half_width = full // 2
    own_rows, shifts = shift_offsets.shape[:2]
    rows, cand = n * own_rows, batches * orient
    na, nb = grid_sides(n)
    groups = ctf_table.shape[0]
    vmem = pl.BlockSpec(memory_space=pltpu.VMEM)
    f32, bf16 = jnp.float32, jnp.bfloat16
    table = pltpu.VMEM((shifts * rows, LANES), f32)
    slices, own = pl.pallas_call(
        functools.partial(kernel, (n, na, nb, rows, shifts, half_width)),
        out_shape=(
            pltpu.VMEM(projections.shape, f32),
            pltpu.VMEM((2, LANES), f32),
        ),
        in_specs=[pl.BlockSpec(memory_space=pltpu.HBM)] * 7,
        out_specs=(vmem, vmem),
        scratch_shapes=[
            pltpu.VMEM(projections.shape, bf16),
            pltpu.SMEM(ctf_group.shape, jnp.int32),
            pltpu.SMEM((own_rows, 2, shifts), jnp.int32),
            pltpu.SMEM(shell_limit.shape, jnp.int32),
            pltpu.VMEM(ctf_table.shape, f32),
            pltpu.VMEM(noise_weight.shape, f32),
            pltpu.VMEM((n, own_rows, full + LANES), bf16),
            pltpu.VMEM((rows, full + LANES), f32),
            pltpu.VMEM((3, cand, half_width), bf16),
            pltpu.VMEM((3 * rows, half_width), bf16),
            pltpu.VMEM((3 * groups, full), bf16),
            pltpu.VMEM((rows, full), f32),
            table, table, table, table, table, table,
            pltpu.VMEM((shifts * rows, full), bf16),
            pltpu.VMEM((n, 1, LANES), f32),
            pltpu.SemaphoreType.DMA((7,)),
            pltpu.SemaphoreType.DMA((n,)),
            pltpu.SemaphoreType.DMA((n,)),
            pltpu.SemaphoreType.DMA((n,)),
            pltpu.SemaphoreType.DMA((n,)),
        ],
        compiler_params=pltpu.CompilerParams(
            collective_id=0, has_side_effects=True, vmem_limit_bytes=VMEM_LIMIT),
    )(projections, images, ctf_group, shift_offsets.transpose(0, 2, 1), shell_limit, ctf_table, noise_weight)
    return slices, own[0, :own_rows], own[1, :own_rows]


def per_device(n, *args):
    particles = n * args[1].shape[0]
    if particles > LANES // 2:
        return local(*args)
    return fused(n, *args)


def solution(mesh):
    in_specs = (
        P(None, ("groups", "blk"), None),
        P(("groups", "blk"), None),
        P(("groups", "blk")),
        P(("groups", "blk"), None, None),
        P(("groups", "blk")),
        P("groups", None),
        P("groups", None),
    )
    out_specs = (P(None, ("groups", "blk"), None), P(("groups", "blk")), P(("groups", "blk")))
    return jax.shard_map(
        functools.partial(per_device, mesh.shape["blk"]),
        mesh=mesh, in_specs=in_specs, out_specs=out_specs, check_vma=False,
    )
```

```python
import functools
import math

import jax
import jax.numpy as jnp
from jax import lax
from jax.experimental import pallas as pl
from jax.experimental.pallas import tpu as pltpu
from jax.sharding import PartitionSpec as P

KY = 64
IMG = 256


def combined_all(value, axis, join):
    pieces = jax.tree.map(lambda part: lax.all_gather(part, axis), value)
    head = jax.tree.map(lambda part: part[0], pieces)
    tail = jax.tree.map(lambda part: part[1:], pieces)
    so_far, _ = lax.scan(lambda so_far, section: (join(so_far, section), None), head, tail)
    return so_far


def frequencies(half_width):
    positions = jnp.arange(half_width, dtype=jnp.int32)
    return (positions // KY, positions % KY - KY // 2)


def shift_factors(offsets, half_width):
    row_count = offsets.shape[0]
    shift_count = offsets.shape[1]
    row_freq = jnp.arange(half_width // KY, dtype=jnp.int32)
    col_freq = jnp.arange(KY, dtype=jnp.int32) - KY // 2
    turns_x = row_freq[None, None, :] * offsets[:, :, 0:1] % IMG
    turns_y = col_freq[None, None, :] * offsets[:, :, 1:2] % IMG
    angle_x = turns_x.astype(jnp.float32) * (2.0 * math.pi / IMG)
    angle_y = turns_y.astype(jnp.float32) * (2.0 * math.pi / IMG)
    cosine_x = jnp.cos(angle_x)[:, :, :, None]
    sine_x = jnp.sin(angle_x)[:, :, :, None]
    cosine_y = jnp.cos(angle_y)[:, :, None, :]
    sine_y = jnp.sin(angle_y)[:, :, None, :]
    cosine = cosine_x * cosine_y - sine_x * sine_y
    sine_part = sine_x * cosine_y + cosine_x * sine_y
    return (
        cosine.reshape(row_count, shift_count, half_width),
        sine_part.reshape(row_count, shift_count, half_width),
    )


def particle_terms(image_rows, ctf_rows, weight_rows, offsets, limits, freq_x, freq_y):
    half_width = image_rows.shape[1] // 2
    image_real = image_rows[:, :half_width].astype(jnp.float32)
    image_imag = image_rows[:, half_width:].astype(jnp.float32)
    radius_sq = freq_x * freq_x + freq_y * freq_y
    inside = (radius_sq[None, :] < (limits * limits)[:, None]).astype(jnp.float32)
    masked_weight = inside * weight_rows
    ctf_weight = masked_weight * ctf_rows
    norm_term = jnp.sum(masked_weight * (image_real * image_real + image_imag * image_imag), axis=1)
    quad_weight = ctf_weight * ctf_rows
    cosine, sine_part = shift_factors(offsets, half_width)
    shift_real = image_real[:, None, :] * cosine + image_imag[:, None, :] * sine_part
    shift_imag = image_imag[:, None, :] * cosine - image_real[:, None, :] * sine_part
    weighted = jnp.concatenate(
        [ctf_weight[:, None, :] * shift_real, ctf_weight[:, None, :] * shift_imag], axis=2
    ).astype(jnp.bfloat16)
    return (weighted, norm_term, quad_weight)


def combine_lse(first, second):
    score_top = jnp.maximum(first[0], second[0])
    exp_total = first[1] * jnp.exp(first[0] - score_top) + second[1] * jnp.exp(
        second[0] - score_top
    )
    return (score_top, exp_total)


def block_shape(row_count):
    return 64 if row_count % 64 == 0 else row_count


def split_rows(members, block_rows):
    return tuple(
        (
            member.reshape((member.shape[0] // block_rows, block_rows) + member.shape[1:])
            for member in members
        )
    )


def local(projections, images, ctf_group, shift_offsets, shell_limit, ctf_table, noise_weight):
    batch_count, orient_dev, full_width = projections.shape
    half_width = full_width // 2
    candidates = batch_count * orient_dev
    flat_proj = projections.reshape(candidates, full_width)
    proj_real = flat_proj[:, :half_width].astype(jnp.float32)
    proj_imag = flat_proj[:, half_width:].astype(jnp.float32)
    proj_power = proj_real * proj_real + proj_imag * proj_imag
    freq_x, freq_y = frequencies(half_width)
    score_scale = 0.5 / math.sqrt(half_width)
    group_count = ctf_table.shape[0]
    particles_dev = images.shape[0]

    def block_terms(members):
        image_rows, groups, offsets, limits = members
        one_hot = (groups[:, None] == jnp.arange(group_count, dtype=jnp.int32)[None, :]).astype(
            jnp.float32
        )
        ctf_rows = jnp.dot(
            one_hot, ctf_table, precision=lax.Precision.HIGHEST, preferred_element_type=jnp.float32
        )
        weight_rows = jnp.dot(
            one_hot,
            noise_weight,
            precision=lax.Precision.HIGHEST,
            preferred_element_type=jnp.float32,
        )
        return particle_terms(image_rows, ctf_rows, weight_rows, offsets, limits, freq_x, freq_y)

    def score_block(members):
        weighted, norm_term, quad_weight = block_terms(members)
        cross_term = lax.dot_general(
            weighted, flat_proj, (((2,), (1,)), ((), ())), preferred_element_type=jnp.float32
        )
        quad_term = lax.dot_general(
            quad_weight,
            proj_power,
            (((1,), (1,)), ((), ())),
            precision=lax.Precision.HIGHEST,
            preferred_element_type=jnp.float32,
        )
        return -(norm_term[:, None, None] - 2.0 * cross_term + quad_term[:, None, :]) * score_scale

    members = (
        lax.all_gather(images, "blk", axis=0, tiled=True),
        lax.all_gather(ctf_group, "blk", axis=0, tiled=True),
        lax.all_gather(shift_offsets, "blk", axis=0, tiled=True),
        lax.all_gather(shell_limit, "blk", axis=0, tiled=True),
    )
    row_count = members[0].shape[0]
    block_rows = block_shape(row_count)
    blocks = lax.map(score_block, split_rows(members, block_rows))
    scores = blocks.reshape((row_count,) + blocks.shape[2:])
    local_top = jnp.max(scores, axis=(1, 2))
    local_total = jnp.sum(jnp.exp(scores - local_top[:, None, None]), axis=(1, 2))
    score_top, exp_total = combined_all((local_top, local_total), "blk", combine_lse)
    log_total = score_top + jnp.log(exp_total)
    pieces = (
        lax.all_gather(images, "blk", axis=0, tiled=True),
        lax.all_gather(ctf_group, "blk", axis=0, tiled=True),
        lax.all_gather(shift_offsets, "blk", axis=0, tiled=True),
        lax.all_gather(shell_limit, "blk", axis=0, tiled=True),
    )
    row_count = pieces[0].shape[0]
    block_rows = block_shape(row_count)

    def add_block(carry, packed):
        member_block, score_block_values, log_block = packed
        weighted = block_terms(member_block)[0]
        posterior = jnp.exp(score_block_values - log_block[:, None, None]).astype(jnp.bfloat16)
        contrib = lax.dot_general(
            posterior, weighted, (((0, 1), (0, 1)), ((), ())), preferred_element_type=jnp.float32
        )
        return (carry + contrib, None)

    zero_slices = jnp.zeros((candidates, full_width), jnp.float32)
    packed_scores = split_rows((scores, log_total), block_rows)
    summed, unused_out = lax.scan(
        add_block, zero_slices, (split_rows(pieces, block_rows), packed_scores[0], packed_scores[1])
    )
    slices = (summed * (candidates / particles_dev)).reshape(batch_count, orient_dev, full_width)
    own_start = lax.axis_index("blk") * particles_dev
    own_top = lax.dynamic_slice_in_dim(score_top, own_start, particles_dev, 0)
    own_log = lax.dynamic_slice_in_dim(log_total, own_start, particles_dev, 0)
    best_posterior = jnp.exp(own_top - own_log)
    return (slices, best_posterior, own_log)


LANES = 128
TILE_KX = LANES // KY
VMEM_LIMIT = 54 * 1024 * 1024


def turn_cos_sin(turns):
    turns = turns - IMG * jnp.floor(turns * (1.0 / IMG) + 0.5)
    half = turns * (math.pi / IMG)
    sq = half * half
    sin_poly = 1.0 / math.factorial(13)
    for power in (11, 9, 7, 5, 3, 1):
        sin_poly = sin_poly * sq + (-1.0) ** (power // 2) / math.factorial(power)
    cos_poly = 1.0 / math.factorial(14) * -1.0
    for power in (12, 10, 8, 6, 4, 2, 0):
        cos_poly = cos_poly * sq + (-1.0) ** (power // 2) / math.factorial(power)
    sin_half = sin_poly * half
    return 1.0 - 2.0 * sin_half * sin_half, 2.0 * sin_half * cos_poly


def three_parts(values):
    first = values.astype(jnp.bfloat16)
    rest = values - first.astype(jnp.float32)
    second = rest.astype(jnp.bfloat16)
    third = (rest - second.astype(jnp.float32)).astype(jnp.bfloat16)
    return first, second, third


def grid_sides(device_count):
    chips = device_count // 2
    outer = 2 ** ((chips.bit_length()) // 2)
    return outer, chips // outer


def kernel(
    sizes,
    proj_hbm, img_hbm, grp_hbm, off_hbm, lim_hbm, ctf_hbm, noise_hbm,
    out_ref, own_ref,
    proj_ref, grp_ref, off_ref, lim_ref, ctf_ref, noise_ref,
    pkt, image, power, quad_w, tabs, ctf_rows, ec_p, es_p, ec_m, es_m, dc, ds, wbuf, stats,
    load_sem, send_sem, recv_sem, stat_send, stat_recv,
):
    n, na, nb, rows, shifts, half_width = sizes
    own_rows = rows // n
    full = 2 * half_width
    tiles = half_width // LANES
    groups = ctf_ref.shape[0]
    me = lax.axis_index("blk")
    core = me % 2
    chip = me // 2
    a, b = chip // nb, chip % nb

    def at(pa, pb, pc):
        return (pa * nb + pb) * 2 + pc

    loads = [
        pltpu.make_async_copy(source, target, load_sem.at[k])
        for k, (source, target) in enumerate((
            (grp_hbm, grp_ref), (off_hbm, off_ref), (lim_hbm, lim_ref),
            (img_hbm, pkt.at[me, :, pl.ds(0, full)]),
            (ctf_hbm, ctf_ref), (noise_hbm, noise_ref), (proj_hbm, proj_ref),
        ))
    ]
    for load in loads:
        load.start()

    barrier = pltpu.get_barrier_semaphore()
    for step in range(1, n):
        pl.semaphore_signal(barrier, inc=1, device_id={"blk": (me + step) % n})

    sub = lax.broadcasted_iota(jnp.int32, (own_rows, LANES), 0)
    lane = lax.broadcasted_iota(jnp.int32, (own_rows, LANES), 1)
    for load in loads[:3]:
        load.wait()
    meta = jnp.zeros((own_rows, LANES), jnp.float32)
    for p in range(own_rows):
        entries = [off_ref[p, j, s] for s in range(shifts) for j in range(2)]
        entries += [grp_ref[p], lim_ref[p]]
        for column, entry in enumerate(entries):
            meta = jnp.where((sub == p) & (lane == column), entry.astype(jnp.float32), meta)
    pkt[me, :, full:] = meta.astype(jnp.bfloat16)
    loads[3].wait()

    pl.semaphore_wait(barrier, n - 1)

    sends = []

    def send(slot, target):
        copy = pltpu.make_async_remote_copy(
            src_ref=pkt.at[slot], dst_ref=pkt.at[slot],
            send_sem=send_sem.at[len(sends)], recv_sem=recv_sem.at[slot],
            device_id={"blk": target},
        )
        copy.start()
        sends.append(copy)

    def arrived(slot):
        pltpu.make_async_remote_copy(
            src_ref=pkt.at[slot], dst_ref=pkt.at[slot],
            send_sem=send_sem.at[0], recv_sem=recv_sem.at[slot],
            device_id={"blk": (me + 1) % n},
        ).wait_recv()

    other = me + 1 - 2 * core
    for j in range(1, na):
        send(me, at((a + j) % na, b, core))
    for k in range(1, nb):
        send(me, at(a, (b + k) % nb, core))
    send(me, other)

    plane = 2 * nb * own_rows

    def widen(pa):
        at_rows = pl.ds(pl.multiple_of(pa * plane, plane), plane)
        image[at_rows, :] = jnp.concatenate(
            [pkt[pa * nb * 2 + d].astype(jnp.float32) for d in range(2 * nb)], axis=0)

    for which, ref in enumerate((ctf_ref, noise_ref)):
        loads[4 + which].wait()
        for part, value in enumerate(three_parts(ref[...])):
            tabs[part * groups:(part + 1) * groups, which * half_width:(which + 1) * half_width] = value
    loads[6].wait()
    proj_rows = proj_ref.shape[1]
    for batch in range(proj_ref.shape[0]):
        real = proj_ref[batch, :, :half_width].astype(jnp.float32)
        imag = proj_ref[batch, :, half_width:].astype(jnp.float32)
        for part, value in enumerate(three_parts(real * real + imag * imag)):
            power[part, batch * proj_rows:(batch + 1) * proj_rows, :] = value

    for j in range(1, na):
        slot = at((a + na - j) % na, b, core)
        arrived(slot)
        for k in range(1, nb):
            send(slot, at(a, (b + k) % nb, core))
        send(slot, other)
    for k in range(1, nb):
        for j in range(na):
            slot = at((a + na - j) % na, (b + nb - k) % nb, core)
            arrived(slot)
            send(slot, other)
    for j in range(na):
        pa = (a + na - j) % na
        for k in range(nb):
            arrived(at(pa, (b + nb - k) % nb, 1 - core))
        widen(pa)

    lane = lax.broadcasted_iota(jnp.int32, (rows, LANES), 1)
    sub = lax.broadcasted_iota(jnp.int32, (rows, LANES), 0)
    side = lane // KY
    freq_y = lane % KY - KY // 2
    side_f, freq_yf = side.astype(jnp.float32), freq_y.astype(jnp.float32)
    meta = image[:, full:]

    def column(j):
        return jnp.broadcast_to(meta[:, j:j + 1], (rows, LANES))

    middle = TILE_KX * (tiles // 2)
    for s in range(shifts):
        at_rows = slice(s * rows, (s + 1) * rows)
        off_x, off_y = column(2 * s), column(2 * s + 1)
        c0, s0 = turn_cos_sin((middle + side_f) * off_x + freq_yf * off_y)
        cd, sd = turn_cos_sin(TILE_KX * off_x)
        ec_p[at_rows, :], es_p[at_rows, :] = c0, s0
        ec_m[at_rows, :], es_m[at_rows, :] = c0 * cd + s0 * sd, s0 * cd - c0 * sd
        dc[at_rows, :], ds[at_rows, :] = cd, sd
    group_of = column(2 * shifts)[:, :3 * groups].astype(jnp.int32)
    lane_group = lax.broadcasted_iota(jnp.int32, (rows, 3 * groups), 1) % groups
    one_hot = (group_of == lane_group).astype(jnp.float32).astype(jnp.bfloat16)
    limit = column(2 * shifts + 1)
    limit_sq = limit * limit

    ctf_rows[...] = jnp.dot(one_hot, tabs[...], preferred_element_type=jnp.float32)
    chunk = 4 * LANES
    lane_chunk = lax.broadcasted_iota(jnp.int32, (rows, chunk), 1)
    chunk_x = lane_chunk // KY
    chunk_y = (lane_chunk % KY - KY // 2).astype(jnp.float32)
    limit_chunk = jnp.concatenate([limit_sq] * (chunk // LANES), axis=1)

    def weight_step(step, norm):
        re_cols = pl.ds(pl.multiple_of(step * chunk, chunk), chunk)
        im_cols = pl.ds(pl.multiple_of(half_width + step * chunk, chunk), chunk)
        x_re, x_im = image[:, re_cols], image[:, im_cols]
        c, w = ctf_rows[:, re_cols], ctf_rows[:, im_cols]
        freq_x = (chunk // KY * step + chunk_x).astype(jnp.float32)
        w = jnp.where(freq_x * freq_x + chunk_y * chunk_y < limit_chunk, w, 0.0)
        wc = w * c
        for part, value in enumerate(three_parts(wc * c)):
            quad_w[part * rows:(part + 1) * rows, re_cols] = value
        image[:, re_cols], image[:, im_cols] = wc * x_re, wc * x_im
        return norm + w * (x_re * x_re + x_im * x_im)

    norm = lax.fori_loop(0, half_width // chunk, weight_step, jnp.zeros((rows, chunk), jnp.float32))
    norm = jnp.sum(norm, axis=1, keepdims=True)

    depth = 8
    for ec, es, sign in ((ec_p, es_p, 1), (ec_m, es_m, -1)):
        first = tiles // 2 if sign > 0 else tiles // 2 - 1

        @pl.loop(0, tiles // 2 // depth)
        def _(m):
            for r in range(0, rows, 16):
                cols, factors = [], []
                for q in range(depth):
                    tile = first + sign * (m * depth + q)
                    re_cols = pl.ds(pl.multiple_of(tile * LANES, LANES), LANES)
                    im_cols = pl.ds(pl.multiple_of(half_width + tile * LANES, LANES), LANES)
                    cols.append((re_cols, im_cols))
                    factors.append((image[r:r + 16, re_cols], image[r:r + 16, im_cols]))
                for s in range(shifts):
                    at_rows = slice(s * rows + r, s * rows + r + 16)
                    ck, sk, cd, sd = ec[at_rows, :], es[at_rows, :], dc[at_rows, :], ds[at_rows, :]
                    for (re_cols, im_cols), (u_re, u_im) in zip(cols, factors):
                        wbuf[at_rows, re_cols] = (u_re * ck + u_im * sk).astype(jnp.bfloat16)
                        wbuf[at_rows, im_cols] = (u_im * ck - u_re * sk).astype(jnp.bfloat16)
                        if sign > 0:
                            ck, sk = ck * cd - sk * sd, sk * cd + ck * sd
                        else:
                            ck, sk = ck * cd + sk * sd, sk * cd - ck * sd
                    ec[at_rows, :], es[at_rows, :] = ck, sk

    p_rows = jnp.concatenate([proj_ref[k] for k in range(proj_ref.shape[0])], axis=0)
    cross = lax.dot_general(
        wbuf[...], p_rows, (((1,), (1,)), ((), ())), preferred_element_type=jnp.float32)
    quad = jnp.zeros((rows, power.shape[1]), jnp.float32)
    for part in range(3):
        product = lax.dot_general(
            quad_w[:(3 - part) * rows, :], power[part], (((1,), (1,)), ((), ())),
            preferred_element_type=jnp.float32)
        quad = quad + sum(product[k * rows:(k + 1) * rows] for k in reversed(range(3 - part)))
    base = norm + quad
    scale = 0.5 / math.sqrt(half_width)
    scores = [-(base - 2.0 * cross[s * rows:(s + 1) * rows, :]) * scale for s in range(shifts)]
    top = functools.reduce(jnp.maximum, scores)
    top = jnp.max(top, axis=1, keepdims=True)
    total = sum(jnp.exp(score - top) for score in scores)
    total = jnp.sum(total, axis=1, keepdims=True)

    mid = LANES // 2
    row = jnp.where(lane == sub, top, 0.0) + jnp.where(lane == sub + mid, total, 0.0)
    stats[me] = jnp.sum(row, axis=0, keepdims=True)
    stat_copies = []
    for step in range(1, n):
        copy = pltpu.make_async_remote_copy(
            src_ref=stats.at[me], dst_ref=stats.at[me],
            send_sem=stat_send.at[step], recv_sem=stat_recv.at[me],
            device_id={"blk": (me + step) % n},
        )
        copy.start()
        stat_copies.append(copy)
    for step in range(1, n):
        slot = (me + n - step) % n
        pltpu.make_async_remote_copy(
            src_ref=stats.at[slot], dst_ref=stats.at[slot],
            send_sem=stat_send.at[step], recv_sem=stat_recv.at[slot],
            device_id={"blk": (me + step) % n},
        ).wait_recv()
    tops = jnp.concatenate([stats[d] for d in range(n)], axis=0)
    totals = pltpu.roll(tops, mid, 1)
    best = jnp.max(tops, axis=0, keepdims=True)
    all_total = jnp.sum(totals * jnp.exp(tops - best), axis=0, keepdims=True)
    log_row = best + jnp.log(all_total)
    log_total = jnp.sum(jnp.where(lane == sub, log_row, 0.0), axis=1, keepdims=True)
    best_row = jnp.exp(best - log_row)
    lane_one = lax.broadcasted_iota(jnp.int32, (1, LANES), 1)
    for k, values in enumerate((best_row, log_row)):
        picked = jnp.zeros((1, LANES), jnp.float32)
        for p in range(own_rows):
            mine = jnp.where(lane_one == me * own_rows + p, values, 0.0)
            picked = jnp.where(lane_one == p, jnp.sum(mine, axis=1, keepdims=True), picked)
        own_ref[k:k + 1, :] = picked

    posterior = jnp.concatenate([jnp.exp(score - log_total) for score in scores], axis=0)
    posterior = posterior.T.astype(jnp.bfloat16)
    gain = proj_ref.shape[0] * proj_rows / own_rows

    wide = 1024

    @pl.loop(0, full // wide)
    def _(step):
        cols = pl.ds(pl.multiple_of(step * wide, wide), wide)
        part = jnp.dot(posterior, wbuf[:, cols], preferred_element_type=jnp.float32) * gain
        for k in range(proj_ref.shape[0]):
            out_ref[k, :, cols] = part[k * proj_rows:(k + 1) * proj_rows]

    for copy in sends + stat_copies:
        copy.wait_send()


def fused(n, projections, images, ctf_group, shift_offsets, shell_limit, ctf_table, noise_weight):
    batches, orient, full = projections.shape
    half_width = full // 2
    own_rows, shifts = shift_offsets.shape[:2]
    rows, cand = n * own_rows, batches * orient
    na, nb = grid_sides(n)
    groups = ctf_table.shape[0]
    vmem = pl.BlockSpec(memory_space=pltpu.VMEM)
    f32, bf16 = jnp.float32, jnp.bfloat16
    table = pltpu.VMEM((shifts * rows, LANES), f32)
    slices, own = pl.pallas_call(
        functools.partial(kernel, (n, na, nb, rows, shifts, half_width)),
        out_shape=(
            pltpu.VMEM(projections.shape, f32),
            pltpu.VMEM((2, LANES), f32),
        ),
        in_specs=[pl.BlockSpec(memory_space=pltpu.HBM)] * 7,
        out_specs=(vmem, vmem),
        scratch_shapes=[
            pltpu.VMEM(projections.shape, bf16),
            pltpu.SMEM(ctf_group.shape, jnp.int32),
            pltpu.SMEM((own_rows, 2, shifts), jnp.int32),
            pltpu.SMEM(shell_limit.shape, jnp.int32),
            pltpu.VMEM(ctf_table.shape, f32),
            pltpu.VMEM(noise_weight.shape, f32),
            pltpu.VMEM((n, own_rows, full + LANES), bf16),
            pltpu.VMEM((rows, full + LANES), f32),
            pltpu.VMEM((3, cand, half_width), bf16),
            pltpu.VMEM((3 * rows, half_width), bf16),
            pltpu.VMEM((3 * groups, full), bf16),
            pltpu.VMEM((rows, full), f32),
            table, table, table, table, table, table,
            pltpu.VMEM((shifts * rows, full), bf16),
            pltpu.VMEM((n, 1, LANES), f32),
            pltpu.SemaphoreType.DMA((7,)),
            pltpu.SemaphoreType.DMA((n,)),
            pltpu.SemaphoreType.DMA((n,)),
            pltpu.SemaphoreType.DMA((n,)),
            pltpu.SemaphoreType.DMA((n,)),
        ],
        compiler_params=pltpu.CompilerParams(
            collective_id=0, has_side_effects=True, vmem_limit_bytes=VMEM_LIMIT),
    )(projections, images, ctf_group, shift_offsets.transpose(0, 2, 1), shell_limit, ctf_table, noise_weight)
    return slices, own[0, :own_rows], own[1, :own_rows]


def per_device(n, *args):
    particles = n * args[1].shape[0]
    if particles > LANES // 2:
        return local(*args)
    return fused(n, *args)


def solution(mesh):
    in_specs = (
        P(None, ("groups", "blk"), None),
        P(("groups", "blk"), None),
        P(("groups", "blk")),
        P(("groups", "blk"), None, None),
        P(("groups", "blk")),
        P("groups", None),
        P("groups", None),
    )
    out_specs = (P(None, ("groups", "blk"), None), P(("groups", "blk")), P(("groups", "blk")))
    return jax.shard_map(
        functools.partial(per_device, mesh.shape["blk"]),
        mesh=mesh, in_specs=in_specs, out_specs=out_specs, check_vma=False,
    )
```
